32 devices in a mesh: shard: 2 (over x), ctx: 4 (over z), tp: 4 (over y, core).
Axes of the slice: x: 2, y: 2, z: 4, core: 2. Of those that a mesh axis runs over, the one named last changes fastest.
Arguments:
- tokens: bfloat16 [16, 1024, 960], P(('shard', 'tp'), 'ctx'), may hold values from -6 to 6
- cotangent: bfloat16 [16, 1024, 960], P(('shard', 'tp'), 'ctx'), may hold values from -6 to 6
- piece_starts: int32 [16, 2], P(('shard', 'tp')), may hold values from 0 to 768, as said below
- doc_lengths: int32 [16, 3], P(('shard', 'tp')), may hold values from 1 to 512, 1024 in all within a row
- attn_gain: bfloat16 [960], P('shard'), may hold values from 0.099609375 to 1.8984375
- w_query: bfloat16 [960, 960], P('shard'), may hold values from -0.1875 to 0.1875
- w_key: bfloat16 [960, 320], P('shard'), may hold values from -0.1875 to 0.1875
- w_value: bfloat16 [960, 320], P('shard'), may hold values from -0.1875 to 0.1875
- w_out: bfloat16 [960, 960], P('shard'), may hold values from -1.5 to 1.5
- ff_gain: bfloat16 [960], P('shard'), may hold values from 0.099609375 to 1.8984375
- w_gate: bfloat16 [960, 2560], P('shard', 'tp'), may hold values from -0.1875 to 0.1875
- w_up: bfloat16 [960, 2560], P('shard', 'tp'), may hold values from -0.1875 to 0.1875
- w_down: bfloat16 [960, 2560], P('shard', 'tp'), may hold values from -0.125 to 0.125
Outputs:
- layer_output: bfloat16 [16, 1024, 960], P(('shard', 'tp'), 'ctx')
- input_grad: float32 [16, 1024, 960], P(('shard', 'tp'), 'ctx')
- attn_gain_grad: float32 [960], P('shard')
- w_query_grad: float32 [960, 960], P('shard')
- w_key_grad: float32 [960, 320], P('shard')
- w_value_grad: float32 [960, 320], P('shard')
- w_out_grad: float32 [960, 960], P('shard')
- ff_gain_grad: float32 [960], P('shard')
- w_gate_grad: float32 [960, 2560], P('shard', 'tp')
- w_up_grad: float32 [960, 2560], P('shard', 'tp')
- w_down_grad: float32 [960, 2560], P('shard', 'tp')
The draws below stay inside these ranges and needn't reach their ends.
Inputs may be any that keep to these rules, and one draw needn't show every extreme that they name: `piece_starts`: each row holds the first positions of two pieces of 256 tokens of its sequence, multiples of 128, the first below the second, the pieces not intersecting. `doc_lengths`: each row lists the lengths of its sequence's consecutive documents, summing to 1024.
All inputs are finite; a program needn't handle non-finite values.
Results may differ from the reference program's by a relative error of at most 0.013.
Values may be sent and summed in bfloat16 or wider, within the bound.
No kernel may reach another device: no remote copies, remote signals or barrier semaphores. Data moves between devices by JAX's collectives and lax.ppermute only.
A program may use at most 448 MiB of HBM per device.

```python
import math
from functools import partial
import jax
import jax.numpy as jnp
import numpy as np
from jax import lax

D = 960
H = 15
KVH = 5
HD = 64
FF = 2560
LEN = 1024
PIECE = 256
GRAIN = 128
DOCS = 3
SEQS = 16


def draw_piece_starts(key, part):
    slots = LEN // GRAIN
    span = PIECE // GRAIN
    key_first, key_second = jax.random.split(key)
    first = jax.random.randint(key_first, (SEQS,), 0, slots - 2 * span + 1)
    second = jax.random.randint(key_second, (SEQS,), first + span, slots - span + 1)
    starts = jnp.stack([first, second], axis=1) * GRAIN
    starts = starts.at[0].set(jnp.array([0, (slots - span) * GRAIN], jnp.int32))
    return starts.astype(jnp.int32)


def shard_levels(key, extent, cuts, smallest, high):
    level, own = 1.0, jax.random.fold_in(key, 6)
    for dim, blocks in cuts:
        draws = jnp.exp(jax.random.uniform(jax.random.fold_in(own, dim), (blocks,), jnp.float32, smallest / len(cuts), high / len(cuts)))
        level = level * jnp.repeat(draws, extent[dim] // blocks).reshape([-1 if axis == dim else 1 for axis in range(len(extent))])
    return level


def profile(number_of, total, reach, skew):
    loads = [(1 << 20) // math.isqrt(grade ** skew) + 1 for grade in range(2, number_of + 1)]
    surplus, given = total - reach - (number_of - 1), [1] * (number_of - 1)
    while surplus > 0:
        movable = [i for i in range(number_of - 1) if given[i] < reach]
        whole, budget = sum([loads[i] for i in movable]), surplus
        for i in movable:
            addition = min(reach - given[i], max(1, budget * loads[i] // whole), surplus)
            given[i] = given[i] + addition
            surplus = surplus - addition
    return np.array([reach] + given)


def uneven(stream_key, count, total, most, lean):
    if count == 2:
        one = jax.random.randint(stream_key, (), max(1, total - most), min(most, total - 1) + 1)
        return jnp.stack([one, total - one])
    sizes = jnp.asarray(profile(count, total, most, lean), jnp.int32)
    couples = (count - 1) // 2
    giver, receiver = sizes[1:1 + 2 * couples:2], sizes[2:2 + 2 * couples:2]
    slack = jnp.minimum(giver - 1, most - receiver)
    moved = jax.random.randint(jax.random.fold_in(stream_key, 1), (couples,), 0, 1 << 20) % (slack + 1)
    sizes = sizes.at[1:1 + 2 * couples:2].set(giver - moved).at[2:2 + 2 * couples:2].set(receiver + moved)
    return sizes[jax.random.permutation(jax.random.fold_in(stream_key, 2), count)]


def scatter_about(rng, dims, deviation, reach, cuts=(), held_as=jnp.bfloat16):
    drawn = jax.random.normal(rng, dims, jnp.float32) * deviation
    if len(cuts) > 0:
        drawn = shard_levels(rng, dims, cuts, -0.22, 0.18) * drawn
    return jnp.clip(drawn, min=-reach, max=reach).astype(held_as)


def setup_inputs(seed: int = 0) -> dict:
    key_list = jax.random.split(jax.random.key(seed), 14)
    return {
        "tokens": scatter_about(key_list[0], (SEQS, LEN, D), 1.0, 6.0, ((0, 8), (1, 4))),
        "cotangent": scatter_about(key_list[1], (SEQS, LEN, D), 1.0, 6.0, ((0, 8), (1, 4))),
        "piece_starts": draw_piece_starts(jax.random.fold_in(key_list[13], 71), 0),
        "doc_lengths": jax.vmap(lambda own: uneven(own, DOCS, LEN, LEN // 2, 0))(jax.random.split(key_list[3], SEQS)).reshape((SEQS, DOCS)).astype(jnp.int32),
        "attn_gain": jnp.clip(1.0 + 0.18 * jax.random.normal(key_list[4], (D,), jnp.float32), 0.099609375, 1.8984375).astype(jnp.bfloat16),
        "w_query": scatter_about(key_list[5], (D, H * HD), D ** -0.5, 0.1875, ((0, 2),)),
        "w_key": scatter_about(key_list[6], (D, KVH * HD), D ** -0.5, 0.1875, ((0, 2),)),
        "w_value": scatter_about(key_list[7], (D, KVH * HD), D ** -0.5, 0.1875, ((0, 2),)),
        "w_out": scatter_about(key_list[8], (H * HD, D), (max(D // 64, 1)) ** -0.5, 1.5, ((0, 2),)),
        "ff_gain": jnp.clip(1.0 + 0.18 * jax.random.normal(key_list[9], (D,), jnp.float32), 0.099609375, 1.8984375).astype(jnp.bfloat16),
        "w_gate": scatter_about(key_list[10], (D, FF), D ** -0.5, 0.1875, ((0, 2), (1, 4))),
        "w_up": scatter_about(key_list[11], (D, FF), D ** -0.5, 0.1875, ((0, 2), (1, 4))),
        "w_down": scatter_about(key_list[12], (D, FF), FF ** -0.5, 0.125, ((0, 2), (1, 4))),
    }


EPS = 1e-05
NEG = -1e+30
HIGH = lax.Precision.HIGHEST

@jax.custom_vjp
def low(v):
    return lax.optimization_barrier(v.astype(jnp.bfloat16)).astype(jnp.float32)

@jax.custom_vjp
def low_back(v):
    return v

def low_keep(v):
    return (low(v), None)

def low_pass(kept, grad):
    return (grad,)

def back_keep(v):
    return (v, None)

def back_low(kept, grad):
    return (low(grad),)
low.defvjp(low_keep, low_pass)
low_back.defvjp(back_keep, back_low)

def rotary_tables():
    half = HD // 2
    place = jnp.arange(LEN).astype(jnp.float32)
    freq = jnp.exp(jnp.arange(half).astype(jnp.float32) * (-2.0 * math.log(10000.0) / HD))
    angle = place[:, None] * freq[None, :]
    return (jnp.cos(angle), jnp.sin(angle))

def rotate(value, cosine, sine):
    half = HD // 2
    first = value[..., :half]
    second = value[..., half:]
    cosine = cosine[:, None, :]
    sine = sine[:, None, :]
    return jnp.concatenate([first * cosine - second * sine, second * cosine + first * sine], axis=-1)

def normed(value, gain):
    return value * lax.rsqrt(lax.optimization_barrier(jnp.mean(value * value, axis=-1, keepdims=True)) + EPS) * gain

def labels(starts, lengths):
    where = jnp.arange(LEN).astype(jnp.int32)
    ends = jnp.cumsum(lengths, axis=1).astype(jnp.int32)
    segment = lax.optimization_barrier(jnp.sum((where[None, :, None] >= ends[:, None, :-1]).astype(jnp.int32), axis=2))
    inside = (where[None, :, None] >= starts[:, None, :]) & (where[None, :, None] < starts[:, None, :] + PIECE)
    number = lax.optimization_barrier(jnp.sum(inside.astype(jnp.int32) * jnp.arange(1, 3).astype(jnp.int32)[None, None, :], axis=2))
    return (segment, number)

def allowed(query_pos, key_pos, query_seg, key_seg, query_num, key_num):
    same_doc = query_seg[:, None] == key_seg[None, :]
    causal = key_pos[None, :] <= query_pos[:, None]
    picture = (query_num[:, None] == key_num[None, :]) & (query_num[:, None] > 0)
    return same_doc & (causal | picture)

def attend_block(query, keys, values, segment, number, start):
    width = query.shape[0]
    query_pos = start + jnp.arange(width).astype(jnp.int32)
    key_pos = jnp.arange(LEN).astype(jnp.int32)
    permit = allowed(query_pos, key_pos, segment[start:start + width], segment, number[start:start + width], number)
    scores = jnp.einsum('qhgd,khd->hgqk', query, keys, precision=HIGH)
    scores = low_back(scores) * HD ** (-0.5)
    scores = jnp.where(permit[None, None], scores, NEG)
    probs = jax.nn.softmax(scores, axis=-1)
    return jnp.einsum('hgqk,khd->qhgd', low(probs), values, precision=HIGH)

def layer(tokens, attn_gain, w_query, w_key, w_value, w_out, ff_gain, w_gate, w_up, w_down, segment, number):
    groups = tokens.shape[0]
    group = H // KVH
    cosine, sine = rotary_tables()
    normed_one = low(normed(tokens, attn_gain))
    query = low_back(jnp.einsum('btd,de->bte', normed_one, w_query, precision=HIGH))
    keys = low_back(jnp.einsum('btd,de->bte', normed_one, w_key, precision=HIGH))
    values = low(low_back(jnp.einsum('btd,de->bte', normed_one, w_value, precision=HIGH)))
    query = low(rotate(query.reshape(groups, LEN, H, HD), cosine, sine)).reshape(groups, LEN, KVH, group, HD)
    keys = low(rotate(keys.reshape(groups, LEN, KVH, HD), cosine, sine))
    values = values.reshape(groups, LEN, KVH, HD)
    block = min(512, LEN)

    def one_sequence(inputs):
        query_seq, keys_seq, values_seq, segment_seq, number_seq = inputs
        parts = []
        for start in range(0, LEN, block):
            block_fn = jax.checkpoint(partial(attend_block, start=start))
            parts.append(block_fn(query_seq[start:start + block], keys_seq, values_seq, segment_seq, number_seq))
        return jnp.concatenate(parts, axis=0)
    mixed = lax.map(one_sequence, (query, keys, values, segment, number))
    mixed = low(low_back(mixed.reshape(groups, LEN, H * HD)))
    branch = low_back(jnp.einsum('bte,ed->btd', mixed, w_out, precision=HIGH))
    hidden_state = tokens + branch
    normed_two = low(normed(hidden_state, ff_gain))
    gate = low_back(jnp.einsum('btd,df->btf', normed_two, w_gate, precision=HIGH))
    up = low_back(jnp.einsum('btd,df->btf', normed_two, w_up, precision=HIGH))
    inner = low(jax.nn.silu(gate) * up)
    return hidden_state + jnp.einsum('btf,df->btd', inner, w_down, precision=HIGH)

def reference(tokens, cotangent, piece_starts, doc_lengths, attn_gain, w_query, w_key, w_value, w_out, ff_gain, w_gate, w_up, w_down):
    weights = tuple((weight.astype(jnp.float32) for weight in (attn_gain, w_query, w_key, w_value, w_out, ff_gain, w_gate, w_up, w_down)))
    size = 4
    count = SEQS // size
    groups_in = (tokens.reshape(count, size, LEN, D), cotangent.reshape(count, size, LEN, D), piece_starts.reshape(count, size, 2), doc_lengths.reshape(count, size, DOCS))

    def step(totals, group_in):
        tokens_group, cotangent_group, starts_group, lengths_group = group_in
        segment, number = labels(starts_group, lengths_group)

        def forward(inputs, *params):
            return layer(inputs, *params, segment, number)
        output, pull = jax.vjp(forward, tokens_group.astype(jnp.float32), *weights)
        grads = pull(cotangent_group.astype(jnp.float32))
        totals = tuple((total + grad for total, grad in zip(totals, grads[1:])))
        return (totals, (output.astype(jnp.bfloat16), grads[0]))
    init = tuple((jnp.zeros(weight.shape, jnp.float32) for weight in weights))
    totals, (outputs, input_grads) = lax.scan(step, init, groups_in)
    return (outputs.reshape(SEQS, LEN, D), input_grads.reshape(SEQS, LEN, D), totals[0], totals[1], totals[2], totals[3], totals[4], totals[5], totals[6], totals[7], totals[8])
```

```python
import functools
import math

import jax
import jax.numpy as jnp
from jax import lax
from jax.experimental import pallas as pl
from jax.experimental.pallas import tpu as pltpu
from jax.sharding import PartitionSpec as P

H = 15
KVH = 5
HD = 64
LEN = 1024
PIECE = 256
GRAIN = 128
MAXDOC = 512
GROUP = H // KVH
KW = KVH * HD
QW = H * HD
SPAN = MAXDOC + 2 * GRAIN

EPS = 1e-05
NEG = -1e30
F32 = jnp.float32
BF16 = jnp.bfloat16
VMEM_LIMIT = 56 * 1024 * 1024


def dot(left, right, dims):
    return lax.dot_general(left, right, (dims, ((), ())), preferred_element_type=F32)


def nn(left, right):
    return dot(left, right, ((1,), (0,)))


def nt(left, right):
    return dot(left, right, ((1,), (1,)))


def tn(left, right):
    return dot(left, right, ((0,), (0,)))


def call(kernel, outs, args, *, grid, in_specs, out_specs, scratch=(), flops=0, transcendentals=0):
    moved = sum(math.prod(a.shape) * a.dtype.itemsize for a in (*args, *outs))
    return pl.pallas_call(
        kernel,
        out_shape=outs,
        grid=grid,
        in_specs=in_specs,
        out_specs=out_specs,
        scratch_shapes=list(scratch),
        compiler_params=pltpu.CompilerParams(vmem_limit_bytes=VMEM_LIMIT),
        cost_estimate=pl.CostEstimate(
            flops=int(flops), bytes_accessed=int(moved), transcendentals=int(transcendentals)
        ),
    )(*args)


def seq_block(*shape):
    return pl.BlockSpec((1, *shape), lambda s, *_: (s,) + (0,) * len(shape))


def whole(*shape):
    return pl.BlockSpec(shape, lambda *_: (0,) * len(shape))


def smem():
    return pl.BlockSpec(memory_space=pltpu.SMEM)


def struct(shape, dtype):
    return jax.ShapeDtypeStruct(shape, dtype)


def rotary_tables(offset, length):
    half = HD // 2
    place = (offset + jnp.arange(length, dtype=jnp.int32)).astype(F32)
    freq = jnp.exp(jnp.arange(half).astype(F32) * (-2.0 * math.log(10000.0) / HD))
    angle = place[:, None] * freq[None, :]
    cosine, sine = jnp.cos(angle), jnp.sin(angle)
    return (
        jnp.concatenate([cosine] * 4, axis=1),
        jnp.concatenate([-sine, sine, -sine, sine], axis=1),
    )


def rotate(tile, cosine, sine):
    lane = lax.broadcasted_iota(jnp.int32, tile.shape, 1)
    partner = jnp.where(lane % HD < HD // 2, pltpu.roll(tile, 96, 1), pltpu.roll(tile, 32, 1))
    return tile * cosine + partner * sine


def rotate_into(out_ref, value_ref, width, cosine, sine, factor):
    for start in range(0, width, 128):
        stop = min(start + 128, width)
        turned = rotate(value_ref[:, start : start + 128], cosine, sine) * factor
        out_ref[0, :, start:stop] = turned[:, : stop - start].astype(out_ref.dtype)


def inverse_mean(value):
    return lax.rsqrt(jnp.mean(value * value, axis=-1, keepdims=True) + EPS)


def project_kernel(
    tok_ref, gain_ref, wq_ref, wkv_ref, cos_ref, sin_ref, normed_ref, q_ref, kv_ref, qs, ks
):
    source = tok_ref[0].astype(F32)
    normed = (source * inverse_mean(source) * gain_ref[...]).astype(BF16)
    normed_ref[0] = normed
    cosine, sine = cos_ref[...], sin_ref[...]
    raw = nn(normed, wkv_ref[...])
    ks[:, :KW] = raw[:, :KW]
    kv_ref[0, :, KW:] = raw[:, KW:].astype(BF16)
    rotate_into(kv_ref, ks, KW, cosine, sine, 1.0)
    qs[:, :QW] = nn(normed, wq_ref[...])
    rotate_into(q_ref, qs, QW, cosine, sine, HD**-0.5)


def project(tokens, gain, wq, wkv, cosine, sine):
    n, rows, width = tokens.shape
    up = lambda w: -(-w // 128) * 128
    return call(
        project_kernel,
        [
            struct((n, rows, width), BF16),
            struct((n, rows, QW), BF16),
            struct((n, rows, 2 * KW), BF16),
        ],
        (tokens, gain, wq, wkv, cosine, sine),
        grid=(n,),
        in_specs=[
            seq_block(rows, width),
            whole(1, width),
            whole(width, QW),
            whole(width, 2 * KW),
            whole(rows, 128),
            whole(rows, 128),
        ],
        out_specs=[seq_block(rows, width), seq_block(rows, QW), seq_block(rows, 2 * KW)],
        scratch=[pltpu.VMEM((rows, up(QW)), F32), pltpu.VMEM((rows, up(KW)), F32)],
        flops=2 * n * rows * width * (QW + 2 * KW),
    )


def marks(scal_ref, seq, pos, valid):
    segment = jnp.zeros(pos.shape, jnp.int32)
    for d in range(2):
        segment += (pos >= scal_ref[seq, d]).astype(jnp.int32)
    number = jnp.zeros(pos.shape, jnp.int32)
    for j in range(2):
        start = scal_ref[seq, 2 + j]
        number += jnp.where((pos >= start) & (pos < start + PIECE), j + 1, 0)
    return jnp.where(valid, segment, -1), number


def bias_of(scal_ref, seq, start, across):
    q_shape, k_shape, q_dim, k_dim = (
        ((GRAIN, 1), (1, SPAN), 0, 1) if across else ((1, GRAIN), (SPAN, 1), 1, 0)
    )
    q_pos = start + lax.broadcasted_iota(jnp.int32, q_shape, q_dim)
    k_pos = start - MAXDOC + lax.broadcasted_iota(jnp.int32, k_shape, k_dim)
    q_seg, q_num = marks(scal_ref, seq, q_pos, q_pos >= 0)
    k_seg, k_num = marks(scal_ref, seq, k_pos, (k_pos >= 0) & (k_pos < LEN))
    q_num = jnp.where(q_num > 0, q_num, -1)
    permit = (q_seg == k_seg) & ((k_pos <= q_pos) | (q_num == k_num))
    return jnp.where(permit, 0.0, NEG).astype(F32)


def load_window(window, parts):
    row = 0
    for part in parts:
        window[row : row + part.shape[1], :] = part[0]
        row += part.shape[1]


def attend_kernel(scal_ref, q_ref, far_ref, near_ref, own_ref, next_ref, mixed_ref, lse_ref, window):
    seq, sub = pl.program_id(0), pl.program_id(1)

    @pl.when(sub == 0)
    def _():
        load_window(window, (far_ref, near_ref, own_ref, next_ref))

    bias = bias_of(scal_ref, seq, scal_ref[seq, 4] + sub * GRAIN, True)
    rows = pl.ds(pl.multiple_of(sub * GRAIN, GRAIN), SPAN)
    lse = jnp.zeros((GRAIN, 128), F32)
    lane = lax.broadcasted_iota(jnp.int32, (GRAIN, 128), 1)
    for j in range(KVH):
        key = window[rows, j * HD : (j + 1) * HD]
        value = window[rows, KW + j * HD : KW + (j + 1) * HD]
        for g in range(GROUP):
            h = j * GROUP + g
            scores = nt(q_ref[0, :, h * HD : (h + 1) * HD], key) + bias
            top = jnp.max(scores, axis=-1, keepdims=True)
            raised = jnp.exp(scores - top)
            total = jnp.sum(raised, axis=-1, keepdims=True)
            out = nn(raised.astype(BF16), value) / total
            mixed_ref[0, :, h * HD : (h + 1) * HD] = out.astype(BF16)
            lse = jnp.where(lane == h, top + jnp.log(total), lse)
    lse_ref[0] = lse


def window_specs(local):
    return [
        seq_block(local, 2 * KW),
        seq_block(local, 2 * KW),
        seq_block(local, 2 * KW),
        seq_block(GRAIN, 2 * KW),
    ]


def sub_block(width):
    return pl.BlockSpec((1, GRAIN, width), lambda s, i: (s, i, 0))


def attend(scal, q, parts):
    n, local, _ = q.shape
    return call(
        attend_kernel,
        [struct((n, local, QW), BF16), struct((n, local, 128), F32)],
        (scal, q, *parts),
        grid=(n, local // GRAIN),
        in_specs=[smem(), sub_block(QW), *window_specs(local)],
        out_specs=[sub_block(QW), sub_block(128)],
        scratch=[pltpu.VMEM((MAXDOC + local + GRAIN, 2 * KW), BF16)],
        flops=16 * n * local * SPAN * QW,
        transcendentals=n * local * SPAN * H,
    )


def attend_back_kernel(
    scal_ref,
    q_ref,
    far_ref,
    near_ref,
    own_ref,
    next_ref,
    mixed_ref,
    lse_ref,
    grad_ref,
    dq_ref,
    dfar_ref,
    dnear_ref,
    down_ref,
    dnext_ref,
    window,
    sums,
):
    seq, sub = pl.program_id(0), pl.program_id(1)

    @pl.when(sub == 0)
    def _():
        load_window(window, (far_ref, near_ref, own_ref, next_ref))
        sums[...] = jnp.zeros_like(sums)

    bias = bias_of(scal_ref, seq, scal_ref[seq, 4] + sub * GRAIN, False)
    bias = jnp.concatenate([bias] * GROUP, axis=1)
    rows = pl.ds(pl.multiple_of(sub * GRAIN, GRAIN), SPAN)
    lane = lax.broadcasted_iota(jnp.int32, (GRAIN, 128), 1)
    product = mixed_ref[0].astype(F32) * grad_ref[0].astype(F32)
    delta = jnp.zeros((GRAIN, 128), F32)
    for h in range(H):
        part = jnp.sum(product[:, h * HD : (h + 1) * HD], axis=-1, keepdims=True)
        delta = jnp.where(lane == h, part, delta)
    delta = delta.T
    lse = lse_ref[0].T

    def heads(array, j):
        return [array[h : h + 1, :] for h in range(j * GROUP, (j + 1) * GROUP)]

    for j in range(KVH):
        k_cols = slice(j * HD, (j + 1) * HD)
        v_cols = slice(KW + j * HD, KW + (j + 1) * HD)
        key, value = window[rows, k_cols], window[rows, v_cols]
        cols = [slice(h * HD, (h + 1) * HD) for h in range(j * GROUP, (j + 1) * GROUP)]
        query = jnp.concatenate([q_ref[0, :, c] for c in cols], axis=0)
        grad = jnp.concatenate([grad_ref[0, :, c] for c in cols], axis=0)
        lse_row = jnp.concatenate(heads(lse, j), axis=1)
        delta_row = jnp.concatenate(heads(delta, j), axis=1)
        probs = jnp.exp(nt(key, query) + bias - lse_row)
        grad_scores = (probs * (nt(value, grad) - delta_row)).astype(BF16)
        sums[rows, v_cols] += nn(probs.astype(BF16), grad)
        sums[rows, k_cols] += nn(grad_scores, query)
        dq = tn(grad_scores, key)
        for g, c in enumerate(cols):
            dq_ref[0, :, c] = dq[g * GRAIN : (g + 1) * GRAIN, :]

    @pl.when(sub == pl.num_programs(1) - 1)
    def _():
        row = 0
        for part in (dfar_ref, dnear_ref, down_ref, dnext_ref):
            part[0] = sums[row : row + part.shape[1], :].astype(part.dtype)
            row += part.shape[1]


def attend_back(scal, q, parts, mixed, lse, grad):
    n, local, _ = q.shape
    window = MAXDOC + local + GRAIN
    return call(
        attend_back_kernel,
        [
            struct((n, local, QW), F32),
            struct((n, local, 2 * KW), BF16),
            struct((n, local, 2 * KW), BF16),
            struct((n, local, 2 * KW), F32),
            struct((n, GRAIN, 2 * KW), BF16),
        ],
        (scal, q, *parts, mixed, lse, grad),
        grid=(n, local // GRAIN),
        in_specs=[
            smem(),
            sub_block(QW),
            *window_specs(local),
            sub_block(QW),
            sub_block(128),
            sub_block(QW),
        ],
        out_specs=[sub_block(QW), *window_specs(local)],
        scratch=[pltpu.VMEM((window, 2 * KW), BF16), pltpu.VMEM((window, 2 * KW), F32)],
        flops=40 * n * local * SPAN * QW,
        transcendentals=n * local * SPAN * H,
    )


def residual_kernel(tok_ref, mixed_ref, wo_ref, gain_ref, hidden_ref, normed_ref):
    hidden = tok_ref[0].astype(F32) + nn(mixed_ref[0], wo_ref[...])
    hidden_ref[0] = hidden
    normed_ref[0] = (hidden * inverse_mean(hidden) * gain_ref[...]).astype(BF16)


def residual(tokens, mixed, wo, gain):
    n, rows, width = tokens.shape
    return call(
        residual_kernel,
        [struct((n, rows, width), F32), struct((n, rows, width), BF16)],
        (tokens, mixed, wo, gain),
        grid=(n,),
        in_specs=[seq_block(rows, width), seq_block(rows, QW), whole(QW, width), whole(1, width)],
        out_specs=[seq_block(rows, width), seq_block(rows, width)],
        flops=2 * n * rows * width * QW,
    )


def ff_kernel(
    nrm_a, nrm_b, cot_a, cot_b, wg_ref, wu_ref, wd_ref, inner_ref, gg_ref, gu_ref, ff_ref, gn_ref
):
    rows = nrm_a.shape[0]
    step = min(rows, 256)
    for half, (nrm_ref, cot_ref) in enumerate(((nrm_a, cot_a), (nrm_b, cot_b))):
        for start in range(0, rows, step):
            at = slice(half * rows + start, half * rows + start + step)
            normed = nrm_ref[start : start + step, :]
            gate = nn(normed, wg_ref[...])
            up = nn(normed, wu_ref[...])
            grad = nn(cot_ref[start : start + step, :], wd_ref[...])
            sigma = jax.nn.sigmoid(gate)
            raised = gate * sigma
            inner = (raised * up).astype(BF16)
            grad_gate = (grad * up * (sigma + raised * (1.0 - sigma))).astype(BF16)
            grad_up = (grad * raised).astype(BF16)
            inner_ref[at, :] = inner
            gg_ref[at, :] = grad_gate
            gu_ref[at, :] = grad_up
            gn_ref[at, :] = (nt(grad_gate, wg_ref[...]) + nt(grad_up, wu_ref[...])).astype(BF16)
            ff_ref[at, :] = nt(inner, wd_ref[...]).astype(BF16)


def ff(normed_pair, cot_pair, wg, wu, wd):
    rows, width = normed_pair[0].shape
    units = wg.shape[1]
    args = (*normed_pair, *cot_pair, wg, wu, wd)
    outs = [struct((2 * rows, units), BF16)] * 3 + [struct((2 * rows, width), BF16)] * 2
    return call(
        ff_kernel,
        outs,
        args,
        grid=(1,),
        in_specs=[whole(*a.shape) for a in args],
        out_specs=[whole(*o.shape) for o in outs],
        flops=24 * rows * width * units,
        transcendentals=2 * rows * units,
    )


def ff_back_kernel(hidden_ref, cot_ref, a_ref, b_ref, gain_ref, wo_ref, gh_ref, gb_ref, gm_ref, gg_ref):
    hidden, gain = hidden_ref[0], gain_ref[...]
    factor = inverse_mean(hidden)
    grad = a_ref[0].astype(F32) + b_ref[0].astype(F32)
    weighted = grad * gain
    back = factor * weighted - hidden * factor**3 * jnp.mean(
        hidden * weighted, axis=-1, keepdims=True
    )
    grad_hidden = cot_ref[0].astype(F32) + back
    branch = grad_hidden.astype(BF16)
    gh_ref[0] = grad_hidden
    gb_ref[0] = branch
    gm_ref[0] = nt(branch, wo_ref[...]).astype(BF16)
    gg_ref[0] = jnp.sum(grad * hidden * factor, axis=0, keepdims=True)


def ff_back(hidden, cotangent, part_a, part_b, gain, wo):
    n, rows, width = hidden.shape
    block = seq_block(rows, width)
    return call(
        ff_back_kernel,
        [
            struct((n, rows, width), F32),
            struct((n, rows, width), BF16),
            struct((n, rows, QW), BF16),
            struct((n, 1, width), F32),
        ],
        (hidden, cotangent, part_a, part_b, gain, wo),
        grid=(n,),
        in_specs=[block, block, block, block, whole(1, width), whole(QW, width)],
        out_specs=[block, block, seq_block(rows, QW), seq_block(1, width)],
        flops=2 * n * rows * width * QW,
    )


def query_back_kernel(dq_ref, cos_ref, sin_ref, out_ref, qs):
    qs[:, :QW] = dq_ref[0]
    rotate_into(out_ref, qs, QW, cos_ref[...], -sin_ref[...], HD**-0.5)


def query_back(dq, cosine, sine):
    n, rows, _ = dq.shape
    return call(
        query_back_kernel,
        [struct((n, rows, QW), BF16)],
        (dq, cosine, sine),
        grid=(n,),
        in_specs=[seq_block(rows, QW), whole(rows, 128), whole(rows, 128)],
        out_specs=[seq_block(rows, QW)],
        scratch=[pltpu.VMEM((rows, -(-QW // 128) * 128), F32)],
    )[0]


def input_kernel(
    tok_ref,
    gh_ref,
    gq_ref,
    own_ref,
    left_ref,
    right_ref,
    gain_ref,
    wq_ref,
    wkv_ref,
    cos_ref,
    sin_ref,
    ig_ref,
    gkv_ref,
    gg_ref,
    ks,
):
    total = own_ref[0] + right_ref[0].astype(F32)
    ks[...] = total
    ks[:GRAIN, :] += left_ref[0].astype(F32)
    gkv_ref[0, :, KW:] = ks[:, KW:].astype(BF16)
    rotate_into(gkv_ref, ks, KW, cos_ref[...], -sin_ref[...], 1.0)
    grad = nt(gq_ref[0], wq_ref[...]) + nt(gkv_ref[0], wkv_ref[...])
    source, gain = tok_ref[0].astype(F32), gain_ref[...]
    factor = inverse_mean(source)
    weighted = grad * gain
    back = factor * weighted - source * factor**3 * jnp.mean(
        source * weighted, axis=-1, keepdims=True
    )
    ig_ref[0] = gh_ref[0] + back
    gg_ref[0] = jnp.sum(grad * source * factor, axis=0, keepdims=True)


def input_back(tokens, grad_hidden, gq, own, left, right, gain, wq, wkv, cosine, sine):
    n, rows, width = tokens.shape
    block, kv_block = seq_block(rows, width), seq_block(rows, 2 * KW)
    return call(
        input_kernel,
        [
            struct((n, rows, width), F32),
            struct((n, rows, 2 * KW), BF16),
            struct((n, 1, width), F32),
        ],
        (tokens, grad_hidden, gq, own, left, right, gain, wq, wkv, cosine, sine),
        grid=(n,),
        in_specs=[
            block,
            block,
            seq_block(rows, QW),
            kv_block,
            seq_block(GRAIN, 2 * KW),
            kv_block,
            whole(1, width),
            whole(width, QW),
            whole(width, 2 * KW),
            whole(rows, 128),
            whole(rows, 128),
        ],
        out_specs=[block, kv_block, seq_block(1, width)],
        scratch=[pltpu.VMEM((rows, 2 * KW), F32)],
        flops=2 * n * rows * width * (QW + 2 * KW),
    )


def program(mesh):
    shards, ctxs, tps = (mesh.shape[axis] for axis in ("shard", "ctx", "tp"))

    def swap(value, axis, bit):
        count = mesh.shape[axis]
        return lax.ppermute(value, axis, [(i, i ^ bit) for i in range(count)])

    def shift(value, by):
        pairs = [(i, i + by) for i in range(ctxs) if 0 <= i + by < ctxs]
        return lax.ppermute(value, "ctx", pairs)

    def in_order(index, own, other):
        first = jnp.concatenate([own, other], axis=0)
        return jnp.where(index == 0, first, jnp.concatenate([other, own], axis=0))

    def pick(value, index):
        return lax.dynamic_index_in_dim(value, index, 0, keepdims=False)

    def gather_rows(value, split):
        if shards != 2:
            return lax.all_gather(value, "shard", axis=0, tiled=True)
        mine = lax.axis_index("shard")
        if not split:
            return in_order(mine, value, swap(value, "shard", 1))
        core = lax.axis_index("tp") % 2
        half = value.shape[0] // 2
        part = swap(lax.dynamic_slice_in_dim(value, core * half, half), "shard", 1)
        return in_order(mine, value, in_order(core, part, swap(part, "tp", 1)))

    def over_shard(grad):
        if shards != 2:
            return lax.psum_scatter(grad, "shard", scatter_dimension=0, tiled=True)
        mine = lax.axis_index("shard")
        halves = grad.reshape(2, grad.shape[0] // 2, *grad.shape[1:])
        got = swap(pick(halves, 1 - mine).astype(BF16), "shard", 1)
        return pick(halves, mine) + got.astype(F32)

    def all_over_ctx(value):
        bit = 1
        while bit < ctxs:
            low = value.astype(BF16)
            value = low.astype(F32) + swap(low, "ctx", bit).astype(F32)
            bit *= 2
        return value

    def reduce_attention(grad):
        if shards != 2:
            return lax.psum(over_shard(grad), ("ctx", "tp"))
        mine, tp = lax.axis_index("shard"), lax.axis_index("tp")
        core, row = tp % 2, tp // 2
        quarter = grad.shape[0] // 4
        parts = grad.reshape(2, 2, quarter, -1)
        take = lambda c: lax.dynamic_index_in_dim(parts, c, 1, keepdims=False)
        held = take(core) + swap(take(1 - core).astype(BF16), "tp", 1).astype(F32)
        held = pick(held, mine) + swap(pick(held, 1 - mine).astype(BF16), "shard", 1).astype(F32)
        held = held.reshape(2, quarter // 2, -1)
        held = pick(held, row) + swap(pick(held, 1 - row).astype(BF16), "tp", 2).astype(F32)
        held = all_over_ctx(held).astype(BF16)
        held = in_order(row, held, swap(held, "tp", 2))
        return in_order(core, held, swap(held, "tp", 1)).astype(F32)

    def per_device(
        tokens,
        cotangent,
        piece_starts,
        doc_lengths,
        attn_gain,
        w_query,
        w_key,
        w_value,
        w_out,
        ff_gain,
        w_gate,
        w_up,
        w_down,
    ):
        seqs, local, width = tokens.shape
        offset = lax.axis_index("ctx") * local
        wq = gather_rows(w_query, True)
        wkv = gather_rows(jnp.concatenate([w_key, w_value], axis=1), True)
        gains = gather_rows(jnp.stack([attn_gain, ff_gain], axis=1), False).astype(F32).T
        gain_one, gain_two = gains[:1], gains[1:]
        wo = gather_rows(w_out, True)
        wg, wu, wd = (gather_rows(w, False) for w in (w_gate, w_up, w_down))
        cosine, sine = rotary_tables(offset, local)
        ends = jnp.cumsum(doc_lengths, axis=1)[:, :-1]
        scal = jnp.concatenate(
            [ends, piece_starts, jnp.broadcast_to(offset, (seqs, 1)).astype(jnp.int32)], axis=1
        )

        chunks = [slice(s, s + 1) for s in range(seqs)]
        rows = local
        state = []
        for c in chunks:
            tok, cot = tokens[c], cotangent[c]
            cot_own = cot.reshape(rows, width)
            cot_y = swap(cot_own, "tp", 2)
            cot_core = swap(cot_own, "tp", 1)
            cot_diag = swap(cot_y, "tp", 1)
            normed_one, q, kv = project(tok, gain_one, wq, wkv, cosine, sine)
            near = shift(kv, 1)
            far = shift(near, 1)
            ahead = shift(kv[:, :GRAIN], -1)
            parts = (far, near, kv, ahead)
            state.append((c, tok, cot, (cot_own, cot_core, cot_y, cot_diag), normed_one, q, parts))
        after = []
        for c, tok, cot, cots, normed_one, q, parts in state:
            mixed, lse = attend(scal[c], q, parts)
            hidden, normed_two = residual(tok, mixed, wo, gain_two)
            own = normed_two.reshape(rows, width)
            n_y = swap(own, "tp", 2)
            n_core = swap(own, "tp", 1)
            n_diag = swap(n_y, "tp", 1)
            after.append((mixed, lse, hidden, (own, n_core, n_y, n_diag)))
        middle = []
        outputs = []
        for (c, tok, cot, cots, *_), (mixed, lse, hidden, nrm) in zip(state, after):
            near_ff = ff(nrm[:2], cots[:2], wg, wu, wd)
            far_ff = ff(nrm[2:], cots[2:], wg, wu, wd)

            def scatter(a, b):
                own, core = a[:rows], a[rows:]
                facing, diag = b[:rows], b[rows:]
                from_core = swap(jnp.concatenate([core, diag], axis=0), "tp", 1)
                mine = own.astype(F32) + from_core[:rows].astype(F32)
                theirs = (facing.astype(F32) + from_core[rows:].astype(F32)).astype(BF16)
                return mine[None], swap(theirs, "tp", 2)[None]

            grads = scatter(near_ff[4], far_ff[4])
            outs = scatter(near_ff[3], far_ff[3])
            output = (hidden + outs[0] + outs[1].astype(F32)).astype(BF16)
            outputs.append(output)
            grad_hidden, branch, grad_mixed, gain_grad = ff_back(hidden, cot, *grads, gain_two, wo)
            middle.append((near_ff, far_ff, grad_hidden, branch, grad_mixed, gain_grad))

        def joined(pick_array):
            return jnp.concatenate([pick_array(i) for i in range(len(chunks))], axis=0)

        ff_rows = joined(lambda i: jnp.concatenate(after[i][3], axis=0))
        cot_rows = joined(lambda i: jnp.concatenate(state[i][3], axis=0))
        ff_units = [
            joined(lambda i: jnp.concatenate([middle[i][0][k], middle[i][1][k]], axis=0))
            for k in range(3)
        ]
        sums = [over_shard(tn(cot_rows, ff_units[0]))]
        sums += [over_shard(tn(ff_rows, ff_units[k])) for k in (1, 2)]
        sum_down, sum_gate, sum_up = [
            lax.psum(total.astype(BF16), "ctx").astype(F32) for total in sums
        ]
        mixed_rows = joined(lambda i: after[i][0].reshape(rows, QW))
        branch_rows = joined(lambda i: middle[i][3].reshape(rows, width))
        sum_out = reduce_attention(tn(mixed_rows, branch_rows))

        last = []
        for i, (c, tok, cot, cots, normed_one, q, parts) in enumerate(state):
            mixed, lse, hidden, _ = after[i]
            dq, dfar, dnear, down, dnext = attend_back(scal[c], q, parts, mixed, lse, middle[i][4])
            passed = shift(dfar, -1)
            right = shift((dnear.astype(F32) + passed.astype(F32)).astype(BF16), -1)
            left = shift(dnext, 1)
            gq = query_back(dq, cosine, sine)
            input_grad, gkv, gain_grad = input_back(
                tok, middle[i][2], gq, down, left, right, gain_one, wq, wkv, cosine, sine
            )
            last.append((input_grad, gq, gkv, gain_grad, normed_one))
        normed_rows = joined(lambda i: last[i][4].reshape(rows, width))
        gq_rows = joined(lambda i: last[i][1].reshape(rows, QW))
        gkv_rows = joined(lambda i: last[i][2].reshape(rows, 2 * KW))
        sum_query = reduce_attention(tn(normed_rows, gq_rows))
        sum_kv = reduce_attention(tn(normed_rows, gkv_rows))
        gain_grads = jnp.stack(
            [sum(m[3][0, 0] for m in last), sum(m[5][0, 0] for m in middle)], axis=1
        )
        sum_gain = reduce_attention(gain_grads)
        return (
            jnp.concatenate(outputs, axis=0),
            jnp.concatenate([m[0] for m in last], axis=0),
            sum_gain[:, 0],
            sum_query,
            sum_kv[:, :KW],
            sum_kv[:, KW:],
            sum_out,
            sum_gain[:, 1],
            sum_gate,
            sum_up,
            sum_down,
        )

    return per_device


def solution(mesh):
    rows = P(("shard", "tp"), "ctx", None)
    seq = P(("shard", "tp"), None)
    gain, weight, ff_weight = P("shard"), P("shard", None), P("shard", "tp")
    weights = (gain, weight, weight, weight, weight, gain, ff_weight, ff_weight, ff_weight)
    return jax.shard_map(
        program(mesh),
        mesh=mesh,
        in_specs=(rows, rows, seq, seq, *weights),
        out_specs=(rows, rows, *weights),
        check_vma=False,
    )
```

```python
import functools
import math

import jax
import jax.numpy as jnp
from jax import lax
from jax.experimental import pallas as pl
from jax.experimental.pallas import tpu as pltpu
from jax.sharding import PartitionSpec as P

H = 15
KVH = 5
HD = 64
LEN = 1024
PIECE = 256
GRAIN = 128
MAXDOC = 512
GROUP = H // KVH
KW = KVH * HD
QW = H * HD
SPAN = MAXDOC + 2 * GRAIN

EPS = 1e-05
NEG = -1e30
F32 = jnp.float32
BF16 = jnp.bfloat16
VMEM_LIMIT = 56 * 1024 * 1024
COST = 0.1


def dot(left, right, dims):
    return lax.dot_general(left, right, (dims, ((), ())), preferred_element_type=F32)


def nn(left, right):
    return dot(left, right, ((1,), (0,)))


def nt(left, right):
    return dot(left, right, ((1,), (1,)))


def tn(left, right):
    return dot(left, right, ((0,), (0,)))


def call(kernel, outs, args, in_specs, out_specs, *, grid=(1,), scratch=(), flops=0, aliases=None):
    return pl.pallas_call(
        kernel,
        out_shape=outs,
        grid=grid,
        in_specs=in_specs,
        out_specs=out_specs,
        scratch_shapes=list(scratch),
        input_output_aliases=aliases or {},
        compiler_params=pltpu.CompilerParams(vmem_limit_bytes=VMEM_LIMIT),
        cost_estimate=pl.CostEstimate(
            flops=int(flops * COST), bytes_accessed=int(flops * COST / 300), transcendentals=0
        ),
    )(*args)


def part(array, seq):
    index = seq if array.shape[0] > 1 else 0
    return pl.BlockSpec((1, *array.shape[1:]), lambda *_: (index,) + (0,) * (len(array.shape) - 1))


def sub_part(array):
    return pl.BlockSpec((1, GRAIN, array.shape[2]), lambda i: (0, i, 0))


def whole(array):
    return pl.BlockSpec(array.shape, lambda *_: (0,) * len(array.shape))


def untouched():
    return pl.BlockSpec(memory_space=pl.ANY)


def smem():
    return pl.BlockSpec(memory_space=pltpu.SMEM)


def struct(shape, dtype):
    return jax.ShapeDtypeStruct(shape, dtype)


def after(value, *deps):
    return lax.optimization_barrier((value, deps))[0]


def rotary_tables(offset, length):
    half = HD // 2
    place = (offset + jnp.arange(length, dtype=jnp.int32)).astype(F32)
    freq = jnp.exp(jnp.arange(half).astype(F32) * (-2.0 * math.log(10000.0) / HD))
    angle = place[:, None] * freq[None, :]
    cosine, sine = jnp.cos(angle), jnp.sin(angle)
    return (
        jnp.concatenate([cosine] * 4, axis=1),
        jnp.concatenate([-sine, sine, -sine, sine], axis=1),
    )


def rotate(tile, cosine, sine):
    lane = lax.broadcasted_iota(jnp.int32, tile.shape, 1)
    partner = jnp.where(lane % HD < HD // 2, pltpu.roll(tile, 96, 1), pltpu.roll(tile, 32, 1))
    return tile * cosine + partner * sine


def rotate_into(out_ref, value_ref, width, cosine, sine, factor):
    for start in range(0, width, 128):
        stop = min(start + 128, width)
        turned = rotate(value_ref[:, start : start + 128], cosine, sine) * factor
        out_ref[0, :, start:stop] = turned[:, : stop - start].astype(out_ref.dtype)


def inverse_mean(value):
    return lax.rsqrt(jnp.mean(value * value, axis=-1, keepdims=True) + EPS)


def wide(width):
    return -(-width // 128) * 128


def project_rows(tok_ref, gain_ref, wq_ref, wkv_ref, cos_ref, sin_ref, normed_ref, q_ref, kv_ref, qs, ks):
    source = tok_ref[0].astype(F32)
    normed = (source * inverse_mean(source) * gain_ref[...]).astype(BF16)
    normed_ref[0] = normed
    cosine, sine = cos_ref[...], sin_ref[...]
    raw = nn(normed, wkv_ref[...])
    ks[:, :KW] = raw[:, :KW]
    kv_ref[0, :, KW:] = raw[:, KW:].astype(BF16)
    rotate_into(kv_ref, ks, KW, cosine, sine, 1.0)
    qs[:, :QW] = nn(normed, wq_ref[...])
    rotate_into(q_ref, qs, QW, cosine, sine, HD**-0.5)


def project_first_kernel(pieces, place_ref, tok_ref, gain_ref, cos_ref, sin_ref, *refs):
    q_pieces, kv_pieces = refs[:pieces], refs[pieces : 2 * pieces]
    normed_ref, q_ref, kv_ref, wq_ref, wkv_ref, qs, ks = refs[2 * pieces :]
    for out_ref, parts in ((wq_ref, q_pieces), (wkv_ref, kv_pieces)):
        for i, piece in enumerate(parts):
            count = piece.shape[0]
            out_ref[pl.ds(pl.multiple_of(place_ref[i], 16), count), :] = piece[...]
    project_rows(
        tok_ref, gain_ref, wq_ref, wkv_ref, cos_ref, sin_ref, normed_ref, q_ref, kv_ref, qs, ks
    )


def project_outs(tokens):
    rows, width = tokens.shape[1:]
    return (
        [
            struct((1, rows, width), BF16),
            struct((1, rows, QW), BF16),
            struct((1, rows, 2 * KW), BF16),
        ],
        [pltpu.VMEM((rows, wide(QW)), F32), pltpu.VMEM((rows, wide(KW)), F32)],
        2 * rows * width * (QW + 2 * KW),
    )


def project_first(tokens, seq, gain, q_pieces, kv_pieces, places, cosine, sine):
    width = tokens.shape[2]
    outs, scratch, flops = project_outs(tokens)
    outs = outs + [struct((width, QW), BF16), struct((width, 2 * KW), BF16)]
    rest = (gain, cosine, sine, *q_pieces, *kv_pieces)
    return call(
        functools.partial(project_first_kernel, len(q_pieces)),
        outs,
        (places, tokens, *rest),
        [smem(), part(tokens, seq), *map(whole, rest)],
        [whole(o) for o in outs],
        scratch=scratch,
        flops=flops,
    )


def project(tokens, seq, gain, wq, wkv, cosine, sine):
    outs, scratch, flops = project_outs(tokens)
    rest = (gain, wq, wkv, cosine, sine)
    return call(
        project_rows,
        outs,
        (tokens, *rest),
        [part(tokens, seq), *map(whole, rest)],
        [whole(o) for o in outs],
        scratch=scratch,
        flops=flops,
    )


def marks(scal_ref, pos, valid):
    segment = jnp.zeros(pos.shape, jnp.int32)
    for d in range(2):
        segment += (pos >= scal_ref[0, d]).astype(jnp.int32)
    number = jnp.zeros(pos.shape, jnp.int32)
    for j in range(2):
        start = scal_ref[0, 2 + j]
        number += jnp.where((pos >= start) & (pos < start + PIECE), j + 1, 0)
    return jnp.where(valid, segment, -1), number


def bias_of(scal_ref, start, across):
    q_shape, k_shape, q_dim, k_dim = (
        ((GRAIN, 1), (1, SPAN), 0, 1) if across else ((1, GRAIN), (SPAN, 1), 1, 0)
    )
    q_pos = start + lax.broadcasted_iota(jnp.int32, q_shape, q_dim)
    k_pos = start - MAXDOC + lax.broadcasted_iota(jnp.int32, k_shape, k_dim)
    q_seg, q_num = marks(scal_ref, q_pos, q_pos >= 0)
    k_seg, k_num = marks(scal_ref, k_pos, (k_pos >= 0) & (k_pos < LEN))
    q_num = jnp.where(q_num > 0, q_num, -1)
    permit = (q_seg == k_seg) & ((k_pos <= q_pos) | (q_num == k_num))
    return jnp.where(permit, 0.0, NEG).astype(F32)


def load_window(window, parts):
    row = 0
    for part in parts:
        window[row : row + part.shape[1], :] = part[0]
        row += part.shape[1]


def attend_kernel(scal_ref, q_ref, far_ref, near_ref, own_ref, next_ref, mixed_ref, lse_ref, window):
    sub = pl.program_id(0)

    @pl.when(sub == 0)
    def _():
        load_window(window, (far_ref, near_ref, own_ref, next_ref))

    bias = bias_of(scal_ref, scal_ref[0, 4] + sub * GRAIN, True)
    rows = pl.ds(pl.multiple_of(sub * GRAIN, GRAIN), SPAN)
    lse = jnp.zeros((GRAIN, 128), F32)
    lane = lax.broadcasted_iota(jnp.int32, (GRAIN, 128), 1)
    for j in range(KVH):
        key = window[rows, j * HD : (j + 1) * HD]
        value = window[rows, KW + j * HD : KW + (j + 1) * HD]
        for g in range(GROUP):
            h = j * GROUP + g
            scores = nt(q_ref[0, :, h * HD : (h + 1) * HD], key) + bias
            top = jnp.max(scores, axis=-1, keepdims=True)
            raised = jnp.exp(scores - top)
            total = jnp.sum(raised, axis=-1, keepdims=True)
            out = nn(raised.astype(BF16), value) / total
            mixed_ref[0, :, h * HD : (h + 1) * HD] = out.astype(BF16)
            lse = jnp.where(lane == h, top + jnp.log(total), lse)
    lse_ref[0] = lse


def attend(scal, q, parts):
    local = q.shape[1]
    outs = [struct((1, local, QW), BF16), struct((1, local, 128), F32)]
    return call(
        attend_kernel,
        outs,
        (scal, q, *parts),
        [smem(), sub_part(q), *map(whole, parts)],
        [sub_part(o) for o in outs],
        grid=(local // GRAIN,),
        scratch=[pltpu.VMEM((MAXDOC + local + GRAIN, 2 * KW), BF16)],
        flops=16 * local * SPAN * QW,
    )


def attend_back_kernel(
    scal_ref,
    q_ref,
    far_ref,
    near_ref,
    own_ref,
    next_ref,
    mixed_ref,
    lse_ref,
    grad_ref,
    dq_ref,
    dfar_ref,
    dnear_ref,
    down_ref,
    dnext_ref,
    window,
    sums,
):
    sub = pl.program_id(0)

    @pl.when(sub == 0)
    def _():
        load_window(window, (far_ref, near_ref, own_ref, next_ref))
        sums[...] = jnp.zeros_like(sums)

    bias = bias_of(scal_ref, scal_ref[0, 4] + sub * GRAIN, False)
    bias = jnp.concatenate([bias] * GROUP, axis=1)
    rows = pl.ds(pl.multiple_of(sub * GRAIN, GRAIN), SPAN)
    lane = lax.broadcasted_iota(jnp.int32, (GRAIN, 128), 1)
    product = mixed_ref[0].astype(F32) * grad_ref[0].astype(F32)
    delta = jnp.zeros((GRAIN, 128), F32)
    for h in range(H):
        part = jnp.sum(product[:, h * HD : (h + 1) * HD], axis=-1, keepdims=True)
        delta = jnp.where(lane == h, part, delta)
    delta = delta.T
    lse = lse_ref[0].T

    def heads(array, j):
        return [array[h : h + 1, :] for h in range(j * GROUP, (j + 1) * GROUP)]

    for j in range(KVH):
        k_cols = slice(j * HD, (j + 1) * HD)
        v_cols = slice(KW + j * HD, KW + (j + 1) * HD)
        key, value = window[rows, k_cols], window[rows, v_cols]
        cols = [slice(h * HD, (h + 1) * HD) for h in range(j * GROUP, (j + 1) * GROUP)]
        query = jnp.concatenate([q_ref[0, :, c] for c in cols], axis=0)
        grad = jnp.concatenate([grad_ref[0, :, c] for c in cols], axis=0)
        lse_row = jnp.concatenate(heads(lse, j), axis=1)
        delta_row = jnp.concatenate(heads(delta, j), axis=1)
        probs = jnp.exp(nt(key, query) + bias - lse_row)
        grad_scores = (probs * (nt(value, grad) - delta_row)).astype(BF16)
        sums[rows, v_cols] += nn(probs.astype(BF16), grad)
        sums[rows, k_cols] += nn(grad_scores, query)
        dq = tn(grad_scores, key)
        for g, c in enumerate(cols):
            dq_ref[0, :, c] = dq[g * GRAIN : (g + 1) * GRAIN, :]

    @pl.when(sub == pl.num_programs(0) - 1)
    def _():
        row = 0
        for part in (dfar_ref, dnear_ref, down_ref, dnext_ref):
            part[0] = sums[row : row + part.shape[1], :].astype(part.dtype)
            row += part.shape[1]


def attend_back(scal, q, parts, mixed, lse, grad):
    local = q.shape[1]
    window = MAXDOC + local + GRAIN
    outs = [
        struct((1, local, QW), F32),
        struct((1, local, 2 * KW), BF16),
        struct((1, local, 2 * KW), BF16),
        struct((1, local, 2 * KW), F32),
        struct((1, GRAIN, 2 * KW), BF16),
    ]
    return call(
        attend_back_kernel,
        outs,
        (scal, q, *parts, mixed, lse, grad),
        [smem(), sub_part(q), *map(whole, parts), sub_part(mixed), sub_part(lse), sub_part(grad)],
        [sub_part(outs[0]), *map(whole, outs[1:])],
        grid=(local // GRAIN,),
        scratch=[pltpu.VMEM((window, 2 * KW), BF16), pltpu.VMEM((window, 2 * KW), F32)],
        flops=40 * local * SPAN * QW,
    )


def residual_kernel(tok_ref, mixed_ref, wo_ref, gain_ref, hidden_ref, normed_ref):
    hidden = tok_ref[0].astype(F32) + nn(mixed_ref[0], wo_ref[...])
    hidden_ref[0] = hidden
    normed_ref[0] = (hidden * inverse_mean(hidden) * gain_ref[...]).astype(BF16)


def residual(tokens, seq, mixed, wo, gain):
    rows, width = tokens.shape[1:]
    outs = [struct((1, rows, width), F32), struct((1, rows, width), BF16)]
    return call(
        residual_kernel,
        outs,
        (tokens, mixed, wo, gain),
        [part(tokens, seq), whole(mixed), whole(wo), whole(gain)],
        [whole(o) for o in outs],
        flops=2 * rows * width * QW,
    )


def ff_kernel(
    nrm_a,
    nrm_b,
    cot_a,
    cot_b,
    wg_ref,
    wu_ref,
    wd_ref,
    *refs,
):
    inner_ref, gg_ref, gu_ref, rows_ref, ff_a, ff_b, gn_a, gn_b = refs[-8:]
    first = pl.program_id(0) == 0
    normed = jnp.where(first, nrm_a[0], nrm_b[0])
    rows_ref[...] = normed
    gate = nn(normed, wg_ref[...])
    up = nn(normed, wu_ref[...])
    grad = nn(jnp.where(first, cot_a[0], cot_b[0]), wd_ref[...])
    sigma = jax.nn.sigmoid(gate)
    raised = gate * sigma
    inner = (raised * up).astype(BF16)
    grad_gate = (grad * up * (sigma + raised * (1.0 - sigma))).astype(BF16)
    grad_up = (grad * raised).astype(BF16)
    inner_ref[...] = inner
    gg_ref[...] = grad_gate
    gu_ref[...] = grad_up
    grad_normed = (nt(grad_gate, wg_ref[...]) + nt(grad_up, wu_ref[...])).astype(BF16)
    out = nt(inner, wd_ref[...]).astype(BF16)

    @pl.when(first)
    def _():
        ff_a[0] = out
        gn_a[0] = grad_normed

    @pl.when(jnp.logical_not(first))
    def _():
        ff_b[0] = out
        gn_b[0] = grad_normed


def ff(normed_pair, cot_pair, weights, seq, base, seqs, kept):
    _, rows, width = normed_pair[0].shape
    units = weights[0].shape[1]

    def block(columns):
        return pl.BlockSpec((rows, columns), lambda i: (base + i * seqs + seq, 0))

    args = (*normed_pair, *cot_pair, *weights, *kept)
    count = 4 * seqs * rows
    outs = [struct((count, units), BF16)] * 3 + [struct((count, width), BF16)]
    outs += [struct((1, rows, width), BF16)] * 4
    result = call(
        ff_kernel,
        outs,
        args,
        [
            *map(whole, normed_pair),
            *(part(c, seq) for c in cot_pair),
            *map(whole, weights),
            *(untouched() for _ in kept),
        ],
        [block(units)] * 3 + [block(width)] + [whole(o) for o in outs[4:]],
        grid=(2,),
        aliases={7 + i: i for i in range(len(kept))},
        flops=24 * rows * width * units,
    )
    return result[:4], result[4:6], result[6:]


def ff_back_kernel(
    hidden_ref, cot_ref, a_ref, b_ref, c_ref, gain_ref, wo_ref, gh_ref, gb_ref, gm_ref, gg_ref
):
    hidden, gain = hidden_ref[0], gain_ref[...]
    factor = inverse_mean(hidden)
    grad = a_ref[0].astype(F32) + b_ref[0].astype(F32) + c_ref[0].astype(F32)
    weighted = grad * gain
    back = factor * weighted - hidden * factor**3 * jnp.mean(
        hidden * weighted, axis=-1, keepdims=True
    )
    grad_hidden = cot_ref[0].astype(F32) + back
    branch = grad_hidden.astype(BF16)
    gh_ref[0] = grad_hidden
    gb_ref[0] = branch
    gm_ref[0] = nt(branch, wo_ref[...]).astype(BF16)
    gg_ref[0] = jnp.sum(grad * hidden * factor, axis=0, keepdims=True)


def ff_back(hidden, cotangent, seq, terms, gain, wo):
    _, rows, width = hidden.shape
    outs = [
        struct((1, rows, width), F32),
        struct((1, rows, width), BF16),
        struct((1, rows, QW), BF16),
        struct((1, 1, width), F32),
    ]
    return call(
        ff_back_kernel,
        outs,
        (hidden, cotangent, *terms, gain, wo),
        [whole(hidden), part(cotangent, seq), *map(whole, terms), whole(gain), whole(wo)],
        [whole(o) for o in outs],
        flops=2 * rows * width * QW,
    )


def query_back_kernel(dq_ref, cos_ref, sin_ref, out_ref, qs):
    qs[:, :QW] = dq_ref[0]
    rotate_into(out_ref, qs, QW, cos_ref[...], -sin_ref[...], HD**-0.5)


def query_back(dq, cosine, sine):
    rows = dq.shape[1]
    return call(
        query_back_kernel,
        [struct((1, rows, QW), BF16)],
        (dq, cosine, sine),
        [whole(dq), whole(cosine), whole(sine)],
        [whole(dq)],
        scratch=[pltpu.VMEM((rows, wide(QW)), F32)],
        flops=rows * QW * 100,
    )[0]


def input_kernel(
    tok_ref,
    gh_ref,
    gq_ref,
    own_ref,
    left_ref,
    right_ref,
    gain_ref,
    wq_ref,
    wkv_ref,
    cos_ref,
    sin_ref,
    *refs,
):
    ig_ref, gkv_ref, gg_ref, ks = refs[-4:]
    ks[...] = own_ref[0] + right_ref[0].astype(F32)
    ks[:GRAIN, :] += left_ref[0].astype(F32)
    gkv_ref[0, :, KW:] = ks[:, KW:].astype(BF16)
    rotate_into(gkv_ref, ks, KW, cos_ref[...], -sin_ref[...], 1.0)
    grad = nt(gq_ref[0], wq_ref[...]) + nt(gkv_ref[0], wkv_ref[...])
    source, gain = tok_ref[0].astype(F32), gain_ref[...]
    factor = inverse_mean(source)
    weighted = grad * gain
    back = factor * weighted - source * factor**3 * jnp.mean(
        source * weighted, axis=-1, keepdims=True
    )
    ig_ref[0] = gh_ref[0] + back
    gg_ref[0] = jnp.sum(grad * source * factor, axis=0, keepdims=True)


def input_back(tokens, seq, args, kept):
    _, rows, width = tokens.shape
    outs = [
        struct(tokens.shape, F32),
        struct((1, rows, 2 * KW), BF16),
        struct((1, 1, width), F32),
    ]
    return call(
        input_kernel,
        outs,
        (tokens, *args, *kept),
        [part(tokens, seq), *map(whole, args), *(untouched() for _ in kept)],
        [part(outs[0], seq), whole(outs[1]), whole(outs[2])],
        aliases={1 + len(args): 0} if kept else None,
        scratch=[pltpu.VMEM((rows, 2 * KW), F32)],
        flops=2 * rows * width * (QW + 2 * KW),
    )


def program(mesh):
    shards, ctxs = mesh.shape["shard"], mesh.shape["ctx"]

    def swap(value, axis, bit):
        count = mesh.shape[axis]
        return lax.ppermute(value, axis, [(i, i ^ bit) for i in range(count)])

    def shift(value, by):
        pairs = [(i, i + by) for i in range(ctxs) if 0 <= i + by < ctxs]
        return lax.ppermute(value, "ctx", pairs)

    def in_order(index, own, other):
        first = jnp.concatenate([own, other], axis=0)
        return jnp.where(index == 0, first, jnp.concatenate([other, own], axis=0))

    def pick(value, index):
        return lax.dynamic_index_in_dim(value, index, 0, keepdims=False)

    def fetch(value):
        half = value.shape[0] // 2
        core = lax.axis_index("tp") % 2
        return swap(lax.dynamic_slice_in_dim(value, core * half, half), "shard", 1)

    def over_shard(grad):
        if shards != 2:
            return lax.psum_scatter(grad, "shard", scatter_dimension=0, tiled=True)
        mine = lax.axis_index("shard")
        halves = grad.reshape(2, grad.shape[0] // 2, *grad.shape[1:])
        got = swap(pick(halves, 1 - mine).astype(BF16), "shard", 1)
        return pick(halves, mine) + got.astype(F32)

    def all_over_ctx(value):
        bit = 1
        while bit < ctxs:
            low = value.astype(BF16)
            value = low.astype(F32) + swap(low, "ctx", bit).astype(F32)
            bit *= 2
        return value

    def reduce_attention(grad):
        if shards != 2:
            return lax.psum(over_shard(grad), ("ctx", "tp"))
        mine, tp = lax.axis_index("shard"), lax.axis_index("tp")
        core, row = tp % 2, tp // 2
        quarter = grad.shape[0] // 4
        parts = grad.reshape(2, 2, quarter, -1)
        take = lambda c: lax.dynamic_index_in_dim(parts, c, 1, keepdims=False)
        held = take(core) + swap(take(1 - core).astype(BF16), "tp", 1).astype(F32)
        held = pick(held, mine) + swap(pick(held, 1 - mine).astype(BF16), "shard", 1).astype(F32)
        held = held.reshape(2, quarter // 2, -1)
        held = pick(held, row) + swap(pick(held, 1 - row).astype(BF16), "tp", 2).astype(F32)
        held = all_over_ctx(held).astype(BF16)
        held = in_order(row, held, swap(held, "tp", 2))
        return in_order(core, held, swap(held, "tp", 1)).astype(F32)

    def reduce_gains(grad):
        if shards != 2:
            return lax.psum(over_shard(grad), ("ctx", "tp"))
        for axis in ("tp", "shard", "ctx"):
            bit = 1
            while bit < mesh.shape[axis]:
                grad = grad + swap(grad, axis, bit)
                bit *= 2
        half = grad.shape[1] // 2
        return lax.dynamic_slice_in_dim(grad, lax.axis_index("shard") * half, half, axis=1)

    def per_device(
        tokens,
        cotangent,
        piece_starts,
        doc_lengths,
        attn_gain,
        w_query,
        w_key,
        w_value,
        w_out,
        ff_gain,
        w_gate,
        w_up,
        w_down,
    ):
        seqs, rows, width = tokens.shape
        offset = (lax.axis_index("ctx") * rows).astype(jnp.int32)
        mine, core = lax.axis_index("shard"), lax.axis_index("tp") % 2
        every = range(seqs)

        w_kv = jnp.concatenate([w_key, w_value], axis=1)
        gains = jnp.stack([attn_gain, ff_gain])
        ff_weights = (w_gate, w_up, w_down)
        if shards == 2:
            half = w_query.shape[0] // 2
            q_part, kv_part = fetch(w_query), fetch(w_kv)
            q_pieces = (w_query, q_part, swap(q_part, "tp", 1))
            kv_pieces = (w_kv, kv_part, swap(kv_part, "tp", 1))
            other = (1 - mine) * 2 * half
            places = jnp.stack([mine * 2 * half, other + core * half, other + (1 - core) * half])
            got = swap(gains, "shard", 1)
            gains = jnp.where(
                mine == 0,
                jnp.concatenate([gains, got], axis=1),
                jnp.concatenate([got, gains], axis=1),
            )
            out_part = fetch(after(w_out, q_part, kv_part))
            wo = in_order(mine, w_out, in_order(core, out_part, swap(out_part, "tp", 1)))
            ff_weights = [
                in_order(mine, w, swap(after(w, out_part), "shard", 1)) for w in ff_weights
            ]
        else:
            gather = lambda w, axis: lax.all_gather(w, "shard", axis=axis, tiled=True)
            q_pieces, kv_pieces = (gather(w_query, 0),), (gather(w_kv, 0),)
            places = jnp.zeros((1,), jnp.int32)
            gains, wo = gather(gains, 1), gather(w_out, 0)
            ff_weights = [gather(w, 0) for w in ff_weights]
        gain_one, gain_two = gains[:1].astype(F32), gains[1:].astype(F32)

        cot_y = swap(cotangent, "tp", 2)
        cots = (cotangent, swap(cotangent, "tp", 1), cot_y, swap(cot_y, "tp", 1))
        cosine, sine = rotary_tables(offset, rows)
        ends = jnp.cumsum(doc_lengths, axis=1)[:, :-1]
        scal = jnp.concatenate(
            [ends, piece_starts, jnp.broadcast_to(offset, (seqs, 1))], axis=1
        ).astype(jnp.int32)
        scals = [scal[s : s + 1] for s in every]

        normed_one, query, windows = [], [], []
        previous = ()
        for s in every:
            if s == 0:
                *made, wq, wkv = project_first(
                    tokens, s, gain_one, q_pieces, kv_pieces, places.astype(jnp.int32), cosine, sine
                )
            else:
                made = project(tokens, s, gain_one, wq, wkv, cosine, sine)
            normed_one.append(made[0])
            query.append(made[1])
            kv = made[2]
            near = shift(after(kv, *previous), 1)
            ahead = shift(after(kv[:, :GRAIN], *previous), -1)
            previous = (near, ahead)
            windows.append((shift(near, 1), near, kv, ahead))

        mixed, lse, hidden, normed_rows = [], [], [], []
        for s in every:
            m, l = attend(scals[s], query[s] if s == 0 else after(query[s], hidden[-1]), windows[s])
            h, own = residual(tokens, s, m, wo, gain_two)
            facing = swap(own, "tp", 2)
            normed_rows.append((own, swap(own, "tp", 1), facing, swap(facing, "tp", 1)))
            mixed.append(m)
            lse.append(l)
            hidden.append(h)

        kept = ()
        last = hidden[-1]
        grad_terms, out_pairs = [], []
        for s in every:
            own, beside, facing, diagonal = normed_rows[s]
            kept, near_out, near_grad = ff(
                (after(own, last), beside), cots[:2], ff_weights, s, 0, seqs, kept
            )
            kept, far_out, far_grad = ff(
                (after(facing, near_out[0]), diagonal), cots[2:], ff_weights, s, 2 * seqs, seqs, kept
            )
            last = far_out[0]

            def scatter(near, far):
                here, there = swap(near[1], "tp", 1), swap(far[1], "tp", 1)
                facing = (far[0].astype(F32) + there.astype(F32)).astype(BF16)
                return near[0], here, swap(facing, "tp", 2)

            grad_terms.append(scatter(near_grad, far_grad))
            out_pairs.append((near_out, far_out))
        inner_all, gate_all, up_all, rows_all = kept
        cot_all = jnp.concatenate([c.reshape(seqs * rows, width) for c in cots], axis=0)

        down_w = over_shard(tn(cot_all, after(inner_all, last)))
        gate_w = over_shard(tn(rows_all, after(gate_all, last)))
        up_w = over_shard(tn(rows_all, after(up_all, last)))
        sum_down = lax.psum(down_w.astype(BF16), "ctx")
        sum_gate = lax.psum(after(gate_w.astype(BF16), sum_down), "ctx")
        sum_up = lax.psum(after(up_w.astype(BF16), sum_gate), "ctx")

        branch, gain_two_grad, grad_hidden = [], 0.0, []
        backs = []
        order = up_w
        for s in every:
            gh, gb, gm, gg = ff_back(
                after(hidden[s], order), cotangent, s, grad_terms[s], gain_two, wo
            )
            grad_hidden.append(gh)
            branch.append(gb[0])
            gain_two_grad = gain_two_grad + gg[0]
            dq, dfar, dnear, down, dnext = attend_back(
                scals[s], query[s], windows[s], mixed[s], lse[s], gm
            )
            order = dq
            passed = shift(dfar, -1)
            left = shift(dnext, 1)
            right = shift((dnear.astype(F32) + passed.astype(F32)).astype(BF16), -1)
            backs.append((dq, down, left, right))
        stack = lambda blocks: jnp.concatenate(blocks, axis=0)
        out_grad = tn(stack([m[0] for m in mixed]), after(stack(branch), order))
        sum_out = reduce_attention(out_grad)
        gq = [query_back(after(backs[s][0], out_grad), cosine, sine) for s in every]
        one_all = stack([n[0] for n in normed_one])
        query_grad = tn(one_all, stack([g[0] for g in gq]))
        sum_query = reduce_attention(query_grad)

        outputs = []
        for s in every:
            near_out, far_out = out_pairs[s]
            terms = scatter(near_out, (far_out[0], after(far_out[1], *(t[2] for t in grad_terms))))
            outputs.append((hidden[s] + sum(t.astype(F32) for t in terms)).astype(BF16))

        kept, gain_one_grad, gkv = (), 0.0, []
        order = query_grad
        for s in every:
            _, down, left, right = backs[s]
            args = (grad_hidden[s], gq[s], down, left, right)
            args += (gain_one, wq, wkv, cosine, sine)
            input_grad, g, gg = input_back(tokens, s, (after(args[0], order), *args[1:]), kept)
            kept = (input_grad,)
            order = g
            gkv.append(g[0])
            gain_one_grad = gain_one_grad + gg[0]
        sum_kv = reduce_attention(tn(one_all, stack(gkv)))
        gain_grads = jnp.concatenate([gain_one_grad, gain_two_grad], axis=0)
        sum_gain = reduce_gains(gain_grads if shards == 2 else gain_grads.T)
        if shards != 2:
            sum_gain = sum_gain.T
        return (
            stack(outputs),
            input_grad,
            sum_gain[0],
            sum_query,
            sum_kv[:, :KW],
            sum_kv[:, KW:],
            sum_out,
            sum_gain[1],
            sum_gate.astype(F32),
            sum_up.astype(F32),
            sum_down.astype(F32),
        )

    return per_device


def solution(mesh):
    rows = P(("shard", "tp"), "ctx", None)
    seq = P(("shard", "tp"), None)
    gain, weight, ff_weight = P("shard"), P("shard", None), P("shard", "tp")
    weights = (gain, weight, weight, weight, weight, gain, ff_weight, ff_weight, ff_weight)
    return jax.shard_map(
        program(mesh),
        mesh=mesh,
        in_specs=(rows, rows, seq, seq, *weights),
        out_specs=(rows, rows, *weights),
        check_vma=False,
    )
```

```python
import functools
import math

import jax
import jax.numpy as jnp
from jax import lax
from jax.experimental import pallas as pl
from jax.experimental.pallas import tpu as pltpu
from jax.sharding import PartitionSpec as P

H = 15
KVH = 5
HD = 64
LEN = 1024
PIECE = 256
GRAIN = 128
MAXDOC = 512
GROUP = H // KVH
KW = KVH * HD
QW = H * HD
SPAN = MAXDOC + 2 * GRAIN

EPS = 1e-05
NEG = -1e30
F32 = jnp.float32
BF16 = jnp.bfloat16
VMEM_LIMIT = 20 * 1024 * 1024
COST = 0.1


def dot(left, right, dims):
    return lax.dot_general(left, right, (dims, ((), ())), preferred_element_type=F32)


def nn(left, right):
    return dot(left, right, ((1,), (0,)))


def nt(left, right):
    return dot(left, right, ((1,), (1,)))


def tn(left, right):
    return dot(left, right, ((0,), (0,)))


def call(kernel, outs, args, in_specs, out_specs, *, grid=(1,), scratch=(), flops=0):
    return pl.pallas_call(
        kernel,
        out_shape=outs,
        grid=grid,
        in_specs=in_specs,
        out_specs=out_specs,
        scratch_shapes=list(scratch),
        compiler_params=pltpu.CompilerParams(vmem_limit_bytes=VMEM_LIMIT),
        cost_estimate=pl.CostEstimate(
            flops=int(flops * COST), bytes_accessed=int(flops * COST / 300), transcendentals=0
        ),
    )(*args)


def part(array, seq):
    index = seq if array.shape[0] > 1 else 0
    return pl.BlockSpec((1, *array.shape[1:]), lambda *_: (index,) + (0,) * (len(array.shape) - 1))


def sub_part(array):
    return pl.BlockSpec((1, GRAIN, array.shape[2]), lambda i: (0, i, 0))


def whole(array):
    return pl.BlockSpec(array.shape, lambda *_: (0,) * len(array.shape))


def smem():
    return pl.BlockSpec(memory_space=pltpu.SMEM)


def struct(shape, dtype):
    return jax.ShapeDtypeStruct(shape, dtype)


def after(value, *deps):
    return lax.optimization_barrier((value, deps))[0] if deps else value


class Chain:
    def __init__(self, steps):
        self.steps, self.result = steps, None
        self.step(None)

    def step(self, deps=()):
        if self.result is None:
            try:
                self.got = self.steps.send(deps)
            except StopIteration as stop:
                self.got = self.result = stop.value

    def finish(self):
        while self.result is None:
            self.step()
        return self.result


def rotary_tables(offset, length):
    half = HD // 2
    place = (offset + jnp.arange(length, dtype=jnp.int32)).astype(F32)
    freq = jnp.exp(jnp.arange(half).astype(F32) * (-2.0 * math.log(10000.0) / HD))
    angle = place[:, None] * freq[None, :]
    cosine, sine = jnp.cos(angle), jnp.sin(angle)
    return (
        jnp.concatenate([cosine] * 4, axis=1),
        jnp.concatenate([-sine, sine, -sine, sine], axis=1),
    )


def rotate(tile, cosine, sine):
    lane = lax.broadcasted_iota(jnp.int32, tile.shape, 1)
    partner = jnp.where(lane % HD < HD // 2, pltpu.roll(tile, 96, 1), pltpu.roll(tile, 32, 1))
    return tile * cosine + partner * sine


def rotate_into(out_ref, value_ref, width, cosine, sine, factor):
    for start in range(0, width, 128):
        stop = min(start + 128, width)
        turned = rotate(value_ref[:, start : start + 128], cosine, sine) * factor
        out_ref[0, :, start:stop] = turned[:, : stop - start].astype(out_ref.dtype)


def inverse_mean(value):
    return lax.rsqrt(jnp.mean(value * value, axis=-1, keepdims=True) + EPS)


def wide(width):
    return -(-width // 128) * 128


def prepare_kernel(*refs):
    count = len(refs) // 2
    for source, out in zip(refs[:count], refs[count:]):
        out[0] = source[0].T


def prepare(*arrays):
    seqs, width, rows = arrays[0].shape
    block = lambda *shape: pl.BlockSpec((1, *shape), lambda s: (s, 0, 0))
    return call(
        prepare_kernel,
        [struct((seqs, rows, width), a.dtype) for a in arrays],
        arrays,
        [block(width, rows)] * len(arrays),
        [block(rows, width)] * len(arrays),
        grid=(seqs,),
        flops=seqs * width * rows * 100,
    )


def put_rows(out_ref, place_ref, pieces):
    for i, piece in enumerate(pieces):
        rows = pl.ds(pl.multiple_of(place_ref[i], 16), piece.shape[0])
        out_ref[rows, :] = piece[...]


def kv_kernel(tok_ref, gain_ref, cos_ref, sin_ref, w_ref, normed_ref, kv_ref, ks):
    source = tok_ref[0].astype(F32)
    normed = (source * inverse_mean(source) * gain_ref[...]).astype(BF16)
    normed_ref[0] = normed
    raw = nn(normed, w_ref[...])
    ks[:, :KW] = raw[:, :KW]
    kv_ref[0, :, KW:] = raw[:, KW:].astype(BF16)
    rotate_into(kv_ref, ks, KW, cos_ref[...], sin_ref[...], 1.0)


def q_kernel(normed_ref, cos_ref, sin_ref, w_ref, q_ref, qs):
    qs[:, :QW] = nn(normed_ref[0], w_ref[...])
    rotate_into(q_ref, qs, QW, cos_ref[...], sin_ref[...], HD**-0.5)


def residual_kernel(tok_ref, mixed_ref, gain_ref, w_ref, hidden_ref, normed_ref):
    hidden = tok_ref[0].astype(F32) + nn(mixed_ref[0], w_ref[...])
    hidden_ref[0] = hidden
    normed_ref[0] = (hidden * inverse_mean(hidden) * gain_ref[...]).astype(BF16)


def with_weight(kernel, outs, args, specs, pieces, places, scratch, flops):
    if len(pieces) == 1:
        return (
            *call(
                kernel,
                outs,
                (*args, pieces[0]),
                [*specs, whole(pieces[0])],
                [whole(o) for o in outs],
                scratch=scratch,
                flops=flops,
            ),
            pieces[0],
        )
    count = len(outs)
    outs = [*outs, struct((2 * pieces[0].shape[0], pieces[0].shape[1]), pieces[0].dtype)]
    return call(
        functools.partial(place_first, kernel, len(args), len(pieces), count),
        outs,
        (places, *args, *pieces),
        [smem(), *specs, *map(whole, pieces)],
        [whole(o) for o in outs],
        scratch=scratch,
        flops=flops,
    )


def place_first(kernel, ins, count, outs, place_ref, *refs):
    args, parts, rest = refs[:ins], refs[ins : ins + count], refs[ins + count :]
    w_ref = rest[outs]
    put_rows(w_ref, place_ref, parts)
    kernel(*args, w_ref, *rest[:outs], *rest[outs + 1 :])


def project_kv(tokens, seq, gain, cosine, sine, pieces, places):
    rows, width = tokens.shape[1:]
    args = (tokens, gain, cosine, sine)
    return with_weight(
        kv_kernel,
        [struct((1, rows, width), BF16), struct((1, rows, 2 * KW), BF16)],
        args,
        [part(tokens, seq), *map(whole, args[1:])],
        pieces,
        places,
        [pltpu.VMEM((rows, wide(KW)), F32)],
        4 * rows * width * KW,
    )


def project_q(normed, cosine, sine, pieces, places):
    _, rows, width = normed.shape
    args = (normed, cosine, sine)
    return with_weight(
        q_kernel,
        [struct((1, rows, QW), BF16)],
        args,
        [*map(whole, args)],
        pieces,
        places,
        [pltpu.VMEM((rows, wide(QW)), F32)],
        2 * rows * width * QW,
    )


def residual(tokens, seq, mixed, gain, pieces, places):
    rows, width = tokens.shape[1:]
    args = (tokens, mixed, gain)
    return with_weight(
        residual_kernel,
        [struct((1, rows, width), F32), struct((1, rows, width), BF16)],
        args,
        [part(tokens, seq), whole(mixed), whole(gain)],
        pieces,
        places,
        [],
        2 * rows * width * QW,
    )


def marks(scal_ref, pos, valid):
    segment = jnp.zeros(pos.shape, jnp.int32)
    for d in range(2):
        segment += (pos >= scal_ref[0, d]).astype(jnp.int32)
    number = jnp.zeros(pos.shape, jnp.int32)
    for j in range(2):
        start = scal_ref[0, 2 + j]
        number += jnp.where((pos >= start) & (pos < start + PIECE), j + 1, 0)
    return jnp.where(valid, segment, -1), number


def bias_of(scal_ref, start, across):
    q_shape, k_shape, q_dim, k_dim = (
        ((GRAIN, 1), (1, SPAN), 0, 1) if across else ((1, GRAIN), (SPAN, 1), 1, 0)
    )
    q_pos = start + lax.broadcasted_iota(jnp.int32, q_shape, q_dim)
    k_pos = start - MAXDOC + lax.broadcasted_iota(jnp.int32, k_shape, k_dim)
    q_seg, q_num = marks(scal_ref, q_pos, q_pos >= 0)
    k_seg, k_num = marks(scal_ref, k_pos, (k_pos >= 0) & (k_pos < LEN))
    q_num = jnp.where(q_num > 0, q_num, -1)
    permit = (q_seg == k_seg) & ((k_pos <= q_pos) | (q_num == k_num))
    return jnp.where(permit, 0.0, NEG).astype(F32)


def load_window(window, parts):
    row = 0
    for part in parts:
        window[row : row + part.shape[1], :] = part[0]
        row += part.shape[1]


def attend_kernel(scal_ref, q_ref, far_ref, near_ref, own_ref, next_ref, mixed_ref, lse_ref, window):
    sub = pl.program_id(0)

    @pl.when(sub == 0)
    def _():
        load_window(window, (far_ref, near_ref, own_ref, next_ref))

    bias = bias_of(scal_ref, scal_ref[0, 4] + sub * GRAIN, True)
    bias = jnp.concatenate([bias] * GROUP, axis=0)
    rows = pl.ds(pl.multiple_of(sub * GRAIN, GRAIN), SPAN)
    lse = jnp.zeros((GRAIN, 128), F32)
    lane = lax.broadcasted_iota(jnp.int32, (GRAIN, 128), 1)
    for j in range(KVH):
        key = window[rows, j * HD : (j + 1) * HD]
        value = window[rows, KW + j * HD : KW + (j + 1) * HD]
        cols = [slice(h * HD, (h + 1) * HD) for h in range(j * GROUP, (j + 1) * GROUP)]
        query = jnp.concatenate([q_ref[0, :, c] for c in cols], axis=0)
        scores = nt(query, key) + bias
        top = jnp.max(scores, axis=-1, keepdims=True)
        raised = jnp.exp(scores - top)
        total = jnp.sum(raised, axis=-1, keepdims=True)
        out = nn(raised.astype(BF16), value) / total
        logsum = top + jnp.log(total)
        for g, c in enumerate(cols):
            at = slice(g * GRAIN, (g + 1) * GRAIN)
            mixed_ref[0, :, c] = out[at].astype(BF16)
            lse = jnp.where(lane == j * GROUP + g, logsum[at], lse)
    lse_ref[0] = lse


def attend(scal, q, parts):
    local = q.shape[1]
    outs = [struct((1, local, QW), BF16), struct((1, local, 128), F32)]
    return call(
        attend_kernel,
        outs,
        (scal, q, *parts),
        [smem(), sub_part(q), *map(whole, parts)],
        [sub_part(o) for o in outs],
        grid=(local // GRAIN,),
        scratch=[pltpu.VMEM((MAXDOC + local + GRAIN, 2 * KW), BF16)],
        flops=16 * local * SPAN * QW,
    )


def attend_back_kernel(
    scal_ref,
    q_ref,
    far_ref,
    near_ref,
    own_ref,
    next_ref,
    mixed_ref,
    lse_ref,
    grad_ref,
    dq_ref,
    dfar_ref,
    dnear_ref,
    down_ref,
    dnext_ref,
    window,
    sums,
):
    sub = pl.program_id(0)

    @pl.when(sub == 0)
    def _():
        load_window(window, (far_ref, near_ref, own_ref, next_ref))
        sums[...] = jnp.zeros_like(sums)

    bias = bias_of(scal_ref, scal_ref[0, 4] + sub * GRAIN, False)
    bias = jnp.concatenate([bias] * GROUP, axis=1)
    rows = pl.ds(pl.multiple_of(sub * GRAIN, GRAIN), SPAN)
    lane = lax.broadcasted_iota(jnp.int32, (GRAIN, 128), 1)
    product = mixed_ref[0].astype(F32) * grad_ref[0].astype(F32)
    delta = jnp.zeros((GRAIN, 128), F32)
    for h in range(H):
        part = jnp.sum(product[:, h * HD : (h + 1) * HD], axis=-1, keepdims=True)
        delta = jnp.where(lane == h, part, delta)
    delta = delta.T
    lse = lse_ref[0].T

    def heads(array, j):
        return [array[h : h + 1, :] for h in range(j * GROUP, (j + 1) * GROUP)]

    for j in range(KVH):
        k_cols = slice(j * HD, (j + 1) * HD)
        v_cols = slice(KW + j * HD, KW + (j + 1) * HD)
        key, value = window[rows, k_cols], window[rows, v_cols]
        cols = [slice(h * HD, (h + 1) * HD) for h in range(j * GROUP, (j + 1) * GROUP)]
        query = jnp.concatenate([q_ref[0, :, c] for c in cols], axis=0)
        grad = jnp.concatenate([grad_ref[0, :, c] for c in cols], axis=0)
        lse_row = jnp.concatenate(heads(lse, j), axis=1)
        delta_row = jnp.concatenate(heads(delta, j), axis=1)
        probs = jnp.exp(nt(key, query) + bias - lse_row)
        grad_scores = (probs * (nt(value, grad) - delta_row)).astype(BF16)
        sums[rows, v_cols] += nn(probs.astype(BF16), grad)
        sums[rows, k_cols] += nn(grad_scores, query)
        dq = tn(key, grad_scores).T
        for g, c in enumerate(cols):
            dq_ref[0, :, c] = dq[g * GRAIN : (g + 1) * GRAIN, :]

    @pl.when(sub == pl.num_programs(0) - 1)
    def _():
        row = 0
        for part in (dfar_ref, dnear_ref, down_ref, dnext_ref):
            part[0] = sums[row : row + part.shape[1], :].astype(part.dtype)
            row += part.shape[1]


def attend_back(scal, q, parts, mixed, lse, grad):
    local = q.shape[1]
    window = MAXDOC + local + GRAIN
    outs = [
        struct((1, local, QW), F32),
        struct((1, local, 2 * KW), BF16),
        struct((1, local, 2 * KW), BF16),
        struct((1, local, 2 * KW), F32),
        struct((1, GRAIN, 2 * KW), BF16),
    ]
    return call(
        attend_back_kernel,
        outs,
        (scal, q, *parts, mixed, lse, grad),
        [smem(), sub_part(q), *map(whole, parts), sub_part(mixed), sub_part(lse), sub_part(grad)],
        [sub_part(outs[0]), *map(whole, outs[1:])],
        grid=(local // GRAIN,),
        scratch=[pltpu.VMEM((window, 2 * KW), BF16), pltpu.VMEM((window, 2 * KW), F32)],
        flops=40 * local * SPAN * QW,
    )


def ff_kernel(nrm_a, nrm_b, cot_a, cot_b, w_ref, inner_ref, gg_ref, gu_ref, ff_a, ff_b, gn_a, gn_b):
    first = pl.program_id(0) == 0
    units = inner_ref.shape[1]
    wg, wu, wd = (w_ref[:, k * units : (k + 1) * units] for k in range(3))
    normed = jnp.where(first, nrm_a[0], nrm_b[0])
    gate = nn(normed, wg)
    up = nn(normed, wu)
    grad = nn(jnp.where(first, cot_a[0], cot_b[0]), wd)
    sigma = jax.nn.sigmoid(gate)
    raised = gate * sigma
    inner = (raised * up).astype(BF16)
    grad_gate = (grad * up * (sigma + raised * (1.0 - sigma))).astype(BF16)
    grad_up = (grad * raised).astype(BF16)
    inner_ref[...] = inner
    gg_ref[...] = grad_gate
    gu_ref[...] = grad_up
    grad_normed = (nt(grad_gate, wg) + nt(grad_up, wu)).astype(BF16)
    out = nt(inner, wd).astype(BF16)

    @pl.when(first)
    def _():
        ff_a[0] = out
        gn_a[0] = grad_normed

    @pl.when(jnp.logical_not(first))
    def _():
        ff_b[0] = out
        gn_b[0] = grad_normed


def ff(normed_pair, cot_pair, weights, seq):
    _, rows, width = normed_pair[0].shape
    units = weights.shape[1] // 3
    args = (*normed_pair, *cot_pair, weights)
    outs = [struct((2 * rows, units), BF16)] * 3 + [struct((1, rows, width), BF16)] * 4
    result = call(
        ff_kernel,
        outs,
        args,
        [*map(whole, normed_pair), *(part(c, seq) for c in cot_pair), whole(weights)],
        [pl.BlockSpec((rows, units), lambda i: (i, 0))] * 3 + [whole(o) for o in outs[3:]],
        grid=(2,),
        flops=24 * rows * width * units,
    )
    return result[:3], result[3:5], result[5:]


def outer_kernel(lefts, rights, gains, split, place_ref, *refs):
    outs = refs[lefts + rights + gains : -1]
    acc = refs[-1]
    gain_refs = refs[lefts + rights : lefts + rights + gains]
    rows = lambda ref: ref[...].reshape(-1, ref.shape[-1])
    width = refs[lefts].shape[-1]
    per = lefts // rights
    for i, right in enumerate(refs[lefts : lefts + rights]):
        left = jnp.concatenate([rows(r) for r in refs[i * per : (i + 1) * per]], axis=0)
        product = tn(left, rows(right))
        if i == 0:
            acc[:, :width] = product
        else:
            acc[:, :width] += product
    if gains:
        total = functools.reduce(jnp.add, [g[0] for g in gain_refs])
        across = jnp.broadcast_to(total, (128, total.shape[1])).T
        acc[:, width:] = across[:, : acc.shape[1] - width]
    if split is None:
        outs[0][...] = acc[...]
        return
    keep_ref, send_ref = outs
    half = keep_ref.shape[-2]
    for s in range(acc.shape[0] // (2 * half)):
        kept = acc[pl.ds(pl.multiple_of(2 * s * half + place_ref[0], 16), half), :]
        sent = acc[pl.ds(pl.multiple_of((2 * s + 1) * half - place_ref[0], 16), half), :]
        if split == "shard":
            keep_ref[...], send_ref[...] = kept, sent.astype(BF16)
        else:
            keep_ref[s], send_ref[s] = kept, sent.astype(BF16)


def outer(lefts, rights, place, split, gains=()):
    width = lefts[0][0].shape[-1]
    columns = rights[0].shape[-1]
    full = wide(columns) if gains else columns
    if split is None:
        outs = [struct((width, full), F32)]
    else:
        shape = (width // 2, full) if split == "shard" else (2, width // 4, full)
        outs = [struct(shape, F32), struct(shape, BF16)]
    count = sum(math.prod(r.shape[:-1]) for r in rights)
    return call(
        functools.partial(outer_kernel, len(lefts), len(rights), len(gains), split),
        outs,
        (place, *(a for a, _ in lefts), *rights, *gains),
        [smem(), *(part(a, s) for a, s in lefts), *map(whole, rights), *map(whole, gains)],
        [whole(o) for o in outs],
        scratch=[pltpu.VMEM((width, full), F32)],
        flops=2 * count * width * columns,
    )


def output_kernel(hidden_ref, *refs):
    total = hidden_ref[0]
    for term in refs[:-1]:
        total += term[0].astype(F32)
    refs[-1][0] = total.T.astype(BF16)


def output_of(hidden, terms):
    _, rows, width = hidden.shape
    out = struct((1, width, rows), BF16)
    return call(
        output_kernel,
        [out],
        (hidden, *terms),
        [whole(hidden), *map(whole, terms)],
        [whole(out)],
        flops=rows * width * 100,
    )[0]


def ff_back_kernel(
    hidden_ref, cot_ref, a_ref, b_ref, c_ref, gain_ref, wo_ref, gh_ref, gb_ref, gm_ref, gg_ref
):
    hidden, gain = hidden_ref[0], gain_ref[...]
    factor = inverse_mean(hidden)
    grad = a_ref[0].astype(F32) + b_ref[0].astype(F32) + c_ref[0].astype(F32)
    weighted = grad * gain
    back = factor * weighted - hidden * factor**3 * jnp.mean(
        hidden * weighted, axis=-1, keepdims=True
    )
    grad_hidden = cot_ref[0].astype(F32) + back
    branch = grad_hidden.astype(BF16)
    gh_ref[0] = grad_hidden
    gb_ref[0] = branch
    gm_ref[0] = nt(branch, wo_ref[...]).astype(BF16)
    gg_ref[0] = jnp.sum(grad * hidden * factor, axis=0, keepdims=True)


def ff_back(hidden, cotangent, seq, terms, gain, wo):
    _, rows, width = hidden.shape
    outs = [
        struct((1, rows, width), F32),
        struct((1, rows, width), BF16),
        struct((1, rows, QW), BF16),
        struct((1, 1, width), F32),
    ]
    return call(
        ff_back_kernel,
        outs,
        (hidden, cotangent, *terms, gain, wo),
        [whole(hidden), part(cotangent, seq), *map(whole, terms), whole(gain), whole(wo)],
        [whole(o) for o in outs],
        flops=2 * rows * width * QW,
    )


def query_back_kernel(dq_ref, cos_ref, sin_ref, out_ref, qs):
    qs[:, :QW] = dq_ref[0]
    rotate_into(out_ref, qs, QW, cos_ref[...], -sin_ref[...], HD**-0.5)


def query_back(dq, cosine, sine):
    rows = dq.shape[1]
    return call(
        query_back_kernel,
        [struct((1, rows, QW), BF16)],
        (dq, cosine, sine),
        [whole(dq), whole(cosine), whole(sine)],
        [whole(dq)],
        scratch=[pltpu.VMEM((rows, wide(QW)), F32)],
        flops=rows * QW * 100,
    )[0]


def input_kernel(
    tok_ref,
    gh_ref,
    gq_ref,
    own_ref,
    left_ref,
    right_ref,
    gain_ref,
    wq_ref,
    wkv_ref,
    cos_ref,
    sin_ref,
    ig_ref,
    gkv_ref,
    ks,
):
    ks[...] = own_ref[0] + right_ref[0].astype(F32)
    ks[:GRAIN, :] += left_ref[0].astype(F32)
    gkv_ref[0, :, KW:] = ks[:, KW:].astype(BF16)
    rotate_into(gkv_ref, ks, KW, cos_ref[...], -sin_ref[...], 1.0)
    grad = nt(gq_ref[0], wq_ref[...]) + nt(gkv_ref[0], wkv_ref[...])
    source, gain = tok_ref[0].astype(F32), gain_ref[...]
    factor = inverse_mean(source)
    weighted = grad * gain
    back = factor * weighted - source * factor**3 * jnp.mean(
        source * weighted, axis=-1, keepdims=True
    )
    ig_ref[0] = (gh_ref[0] + back).T


def input_back(tokens, seq, args):
    _, rows, width = tokens.shape
    outs = [struct((1, width, rows), F32), struct((1, rows, 2 * KW), BF16)]
    return call(
        input_kernel,
        outs,
        (tokens, *args),
        [part(tokens, seq), *map(whole, args)],
        [whole(o) for o in outs],
        scratch=[pltpu.VMEM((rows, 2 * KW), F32)],
        flops=2 * rows * width * (QW + 2 * KW),
    )


def program(mesh):
    shards, ctxs = mesh.shape["shard"], mesh.shape["ctx"]

    def swap(value, axis, bit):
        count = mesh.shape[axis]
        return lax.ppermute(value, axis, [(i, i ^ bit) for i in range(count)])

    def shift(value, by):
        pairs = [(i, i + by) for i in range(ctxs) if 0 <= i + by < ctxs]
        return lax.ppermute(value, "ctx", pairs)

    def in_order(index, own, other):
        first = jnp.concatenate([own, other], axis=0)
        return jnp.where(index == 0, first, jnp.concatenate([other, own], axis=0))

    def pick(value, index):
        return lax.dynamic_index_in_dim(value, index, 0, keepdims=False)

    def add(terms):
        return functools.reduce(jnp.add, [t.astype(F32) for t in terms])

    def over_shard(terms):
        if shards != 2:
            return (lax.psum_scatter(terms[0], "shard", scatter_dimension=0, tiled=True),)
        return terms[0], swap(terms[1], "shard", 1)

    def reduce_attention(terms):
        if shards != 2:
            return lax.psum(add(over_shard(terms)), ("ctx", "tp"))
        mine, tp = lax.axis_index("shard"), lax.axis_index("tp")
        core, row = tp % 2, tp // 2
        keep, send = terms
        got = swap(send, "tp", 1)
        deps = yield got
        held = keep + after(got, *deps).astype(F32)
        got = swap(pick(held, 1 - mine).astype(BF16), "shard", 1)
        deps = yield got
        held = pick(held, mine) + after(got, *deps).astype(F32)
        held = held.reshape(2, held.shape[0] // 2, -1)
        got = swap(pick(held, 1 - row).astype(BF16), "tp", 2)
        deps = yield got
        held = pick(held, row) + after(got, *deps).astype(F32)
        bit = 1
        while bit < ctxs:
            low = held.astype(BF16)
            got = swap(low, "ctx", bit)
            deps = yield got
            held = low.astype(F32) + after(got, *deps).astype(F32)
            bit *= 2
        held = held.astype(BF16)
        got = swap(held, "tp", 2)
        deps = yield got
        held = in_order(row, held, after(got, *deps))
        got = swap(held, "tp", 1)
        deps = yield got
        return in_order(core, held, after(got, *deps)).astype(F32)

    def per_device(
        tokens,
        cotangent,
        piece_starts,
        doc_lengths,
        attn_gain,
        w_query,
        w_key,
        w_value,
        w_out,
        ff_gain,
        w_gate,
        w_up,
        w_down,
    ):
        seqs, rows, width = tokens.shape
        offset = (lax.axis_index("ctx") * rows).astype(jnp.int32)
        mine, tp = lax.axis_index("shard"), lax.axis_index("tp")
        core, row = tp % 2, tp // 2
        every = range(seqs)
        last = seqs - 1

        w_kv = jnp.concatenate([w_key, w_value], axis=1)
        gains = jnp.stack([attn_gain, ff_gain])
        w_ff = jnp.concatenate([w_gate, w_up, w_down], axis=1)
        if shards == 2:
            full = w_query.shape[0]
            half = full // 2
            span = -(-half // 32) * 16
            other = (1 - mine) * full
            here, there = other + core * half, other + (1 - core) * half
            step, back = row * (half - span), (1 - row) * (half - span)
            kv_places = jnp.stack([mine * full, here, there])
            places = jnp.stack([mine * full, here + step, here + back, there + step, there + back])
            kv_places, places = kv_places.astype(jnp.int32), places.astype(jnp.int32)

            got = swap(gains, "shard", 1)
            gains = jnp.where(
                mine == 0,
                jnp.concatenate([gains, got], axis=1),
                jnp.concatenate([got, gains], axis=1),
            )
            kv_part = swap(lax.dynamic_slice_in_dim(w_kv, core * half, half), "shard", 1)
            kv_pieces = (w_kv, kv_part, swap(kv_part, "tp", 1))
            quarter = lambda w: lax.dynamic_slice_in_dim(w, core * half + step, span)
            q_part = swap(after(quarter(w_query), kv_part), "shard", 1)
            q_facing = swap(q_part, "tp", 2)
            q_pieces = (w_query, q_part, q_facing, swap(q_part, "tp", 1), swap(q_facing, "tp", 1))
            out_part = swap(after(quarter(w_out), q_part), "shard", 1)
            out_facing = swap(after(out_part, q_facing), "tp", 2)
            out_pieces = (w_out, out_part, out_facing)
            out_pieces += (swap(out_part, "tp", 1), swap(out_facing, "tp", 1))
            w_ff = after(w_ff, out_part)
        else:
            gather = lambda w: lax.all_gather(w, "shard", axis=0, tiled=True)
            kv_places = places = jnp.zeros((1,), jnp.int32)
            gains = lax.all_gather(gains, "shard", axis=1, tiled=True)
            kv_pieces, q_pieces, out_pieces = (gather(w_kv),), (gather(w_query),), (gather(w_out),)
            q_facing = q_pieces[-1]
        ff_weights = lax.all_gather(w_ff, "shard", axis=0, tiled=True)
        gain_one, gain_two = gains[:1].astype(F32), gains[1:].astype(F32)

        tokens, cotangent = prepare(tokens.transpose(0, 2, 1), cotangent.transpose(0, 2, 1))
        cosine, sine = rotary_tables(offset, rows)
        ends = jnp.cumsum(doc_lengths, axis=1)[:, :-1]
        scal = jnp.concatenate(
            [ends, piece_starts, jnp.broadcast_to(offset, (seqs, 1))], axis=1
        ).astype(jnp.int32)
        scals = [scal[s : s + 1] for s in every]

        normed_one, query, windows = [], [], []
        previous, order = (), ()
        for s in every:
            normed, kv, wkv = project_kv(
                after(tokens, *order), s, gain_one, cosine, sine, kv_pieces, kv_places
            )
            kv_pieces = (wkv,)
            normed_one.append(normed)
            order = (kv,)
            near = shift(after(kv, *previous), 1)
            ahead = shift(after(kv[:, :GRAIN], *previous), -1)
            previous = (near, ahead)
            windows.append((shift(near, 1), near, kv, ahead))
        cot_y = swap(after(cotangent, q_facing), "tp", 2)
        cot_core = swap(cotangent, "tp", 1)
        for s in every:
            normed = after(normed_one[s], *order)
            q, wq = project_q(normed, cosine, sine, q_pieces, places)
            q_pieces = (wq,)
            query.append(q)
            order = (q,)

        mixed, lse, hidden, normed_rows = [], [], [], []
        order = (query[last], *out_pieces)
        for s in every:
            m, l = attend(scals[s], after(query[s], *order), windows[s])
            deps = (*windows[min(s + 1, last)], cot_y) if s == 0 else (normed_rows[-1][2],)
            h, own, wo = residual(tokens, s, after(m, *deps), gain_two, out_pieces, places)
            out_pieces = (wo,)
            normed_rows.append((own, swap(own, "tp", 1), swap(own, "tp", 2)))
            mixed.append(m)
            lse.append(l)
            hidden.append(h)
            order = (h,)
        cots = (cotangent, cot_core, cot_y, swap(after(cot_y, hidden[0]), "tp", 1))

        def to_facing(near, far):
            here, there = swap(near[1], "tp", 1), swap(far[1], "tp", 1)
            return (near[0], here), (far[0].astype(F32) + there.astype(F32)).astype(BF16)

        row_blocks, units, out_pairs = [], [], []
        grad_terms, crossed = [], []
        order = (hidden[last],)
        for s in every:
            own, beside, facing = normed_rows[s]
            unit, near_out, near_grad = ff((after(own, *order), beside), cots[:2], ff_weights, s)
            units.append(unit)
            diagonal = swap(after(facing, hidden[last], *(u[0] for u in units[: 2 * s])), "tp", 1)
            order = (unit[0], *(t[1] for t in crossed), *(n[2] for n in normed_rows[s + 1 :]))
            unit, far_out, far_grad = ff(
                (after(facing, *order), diagonal), cots[2:], ff_weights, s
            )
            units.append(unit)
            order = (unit[0],)
            terms, partial = to_facing(near_grad, far_grad)
            crossed.append((terms, partial, swap(partial, "tp", 2)))
            grad_terms.append((*terms, crossed[-1][2]))
            out_pairs.append((near_out, far_out))
            row_blocks += [own, beside, facing, diagonal]

        by_shard, by_core = ("shard", "core") if shards == 2 else (None, None)
        shard_place = (mine * (width // 2)).astype(jnp.int32)[None]
        core_place = (core * (width // 4)).astype(jnp.int32)[None]

        def unit_outer(lefts, k, *deps):
            rights = [u[k] for u in units]
            return outer(lefts, [after(rights[0], *deps), *rights[1:]], shard_place, by_shard)

        cot_lefts = [(c, s) for s in every for c in cots]
        row_lefts = [(b, 0) for b in row_blocks]
        down_grad = unit_outer(cot_lefts, 0, *order, *(t[2] for t in crossed[:-1]))
        down_terms = over_shard(down_grad)
        gate_grad = unit_outer(row_lefts, 1, down_grad[0], crossed[-1][1])
        gate_terms = over_shard(gate_grad)
        branch, gain_two_grad, grad_hidden = [], [], []
        backs = []
        order = gate_grad[0]
        for s in every:
            deps = ()
            if s == last:
                facing_outs = []
                for near_out, far_out in out_pairs:
                    held = after((near_out, far_out), down_grad[0])
                    facing_outs.append(to_facing(*held))
                deps = tuple(f[1] for f in facing_outs)
            gh, gb, gm, gg = ff_back(
                after(hidden[s], order, *deps), cotangent, s, grad_terms[s], gain_two, wo
            )
            grad_hidden.append(gh)
            branch.append(gb)
            gain_two_grad.append(gg)
            deps = ()
            if s == last:
                out_grad = outer([(m, 0) for m in mixed], branch, core_place, by_core, gain_two_grad)
                out_chain = Chain(reduce_attention(out_grad))
                deps = (out_grad[0], *(b[2] for b in backs))
            dq, dfar, dnear, down, dnext = attend_back(
                scals[s], query[s], windows[s], mixed[s], lse[s], after(gm, *deps)
            )
            order = dq
            passed = shift(dfar, -1)
            left = shift(dnext, 1)
            if s == 0:
                up_grad = unit_outer(row_lefts, 2, dq)
                up_terms = over_shard(up_grad)
                order = up_grad[0]
                sum_down = lax.psum(add(after(down_terms, dq)).astype(BF16), "ctx")
            nearer = (dnear.astype(F32) + passed.astype(F32)).astype(BF16)
            backs.append((dq, down, nearer, left, shift(nearer, -1)))
        out_chain.step((order,))
        outs_got = [swap(after(f[1], *(t[2] for t in crossed)), "tp", 2) for f in facing_outs]
        arrived = [a for b in backs[:-1] for a in b[3:]]
        gq = [query_back(after(b[0], order, *arrived), cosine, sine) for b in backs]
        ones = [(n, 0) for n in normed_one]
        query_grad = outer(ones, gq, core_place, by_core)
        query_chain = Chain(reduce_attention(query_grad))
        order = (query_grad[0], outs_got[0], backs[last][2], out_chain.got, query_chain.got)
        out_chain.step((query_grad[0],))
        query_chain.step()

        input_grads, gkv = [], []
        for s in every:
            _, down, _, left, right = backs[s]
            args = (grad_hidden[s], gq[s], down, left, right)
            args += (gain_one, wq, wkv, cosine, sine)
            input_grad, g = input_back(tokens, s, (after(args[0], *order), *args[1:]))
            input_grads.append(input_grad)
            gkv.append(g)
            order = (g, outs_got[last], out_chain.got, query_chain.got)
        out_chain.step((g,))
        query_chain.step((g,))
        kv_grad = outer(ones, gkv, core_place, by_core)
        kv_chain = Chain(reduce_attention(kv_grad))
        sums = [add(t).astype(BF16) for t in after((gate_terms, up_terms), query_grad[0])]
        sum_gate, sum_up = lax.psum(after(sums, sum_down, kv_grad[0]), "ctx")
        outputs = [
            output_of(after(hidden[s], kv_grad[0]), (*facing_outs[s][0], outs_got[s]))
            for s in every
        ]
        sum_out, sum_query, sum_kv = (c.finish() for c in (out_chain, query_chain, kv_chain))
        sum_key, sum_value = sum_kv[:, :KW], sum_kv[:, KW:]
        sum_gain = functools.reduce(
            jnp.add,
            [
                jnp.sum(w.astype(F32) * g, axis=1)
                for w, g in ((w_query, sum_query), (w_key, sum_key), (w_value, sum_value))
            ],
        ) / attn_gain.astype(F32)
        join = lambda blocks: jnp.concatenate(blocks, axis=0).transpose(0, 2, 1)
        return (
            join(outputs),
            join(input_grads),
            sum_gain,
            sum_query,
            sum_key,
            sum_value,
            sum_out[:, :width],
            sum_out[:, width],
            sum_gate.astype(F32),
            sum_up.astype(F32),
            sum_down.astype(F32),
        )

    return per_device


def solution(mesh):
    rows = P(("shard", "tp"), "ctx", None)
    seq = P(("shard", "tp"), None)
    gain, weight, ff_weight = P("shard"), P("shard", None), P("shard", "tp")
    weights = (gain, weight, weight, weight, weight, gain, ff_weight, ff_weight, ff_weight)
    return jax.shard_map(
        program(mesh),
        mesh=mesh,
        in_specs=(rows, rows, seq, seq, *weights),
        out_specs=(rows, rows, *weights),
        check_vma=False,
    )
```

```python
import functools
import math

import jax
import jax.numpy as jnp
from jax import lax
from jax.experimental import pallas as pl
from jax.experimental.pallas import tpu as pltpu
from jax.sharding import PartitionSpec as P

H = 15
KVH = 5
HD = 64
LEN = 1024
PIECE = 256
GRAIN = 128
MAXDOC = 512
GROUP = H // KVH
KW = KVH * HD
QW = H * HD
SPAN = MAXDOC + 2 * GRAIN

EPS = 1e-05
NEG = -1e30
F32 = jnp.float32
BF16 = jnp.bfloat16
VMEM_LIMIT = 20 * 1024 * 1024
SCALE = 10.0
FLOPS_PER_US = 1.15e9


def dot(left, right, dims):
    return lax.dot_general(left, right, (dims, ((), ())), preferred_element_type=F32)


def nn(left, right):
    return dot(left, right, ((1,), (0,)))


def nt(left, right):
    return dot(left, right, ((1,), (1,)))


def tn(left, right):
    return dot(left, right, ((0,), (0,)))


def wide(width):
    return -(-width // 128) * 128


class Order:
    last = None
    awaited = ()


def arrive(*values):
    Order.awaited += values


def after(value, *deps):
    return lax.optimization_barrier((value, deps))[0] if deps else value


def in_turn(value):
    return value if Order.last is None else after(value, *Order.last)


def struct(shape, dtype):
    return jax.ShapeDtypeStruct(shape, dtype)


def rows_at(array, index, count):
    return array, pl.BlockSpec((count, array.shape[1]), lambda *_: (index, 0))


def rows_each(array, count):
    return array, pl.BlockSpec((count, array.shape[1]), lambda i: (i, 0))


def call(kernel, outs, args, *, us, grid=(1,), scratch=(), limit=VMEM_LIMIT):
    def split(operands):
        arrays, specs = [], []
        for operand in operands:
            if isinstance(operand, tuple):
                array, spec = operand
            elif operand.dtype == jnp.int32:
                array, spec = operand, pl.BlockSpec(memory_space=pltpu.SMEM)
            else:
                array = operand
                spec = pl.BlockSpec(array.shape, lambda *_, n=len(array.shape): (0,) * n)
            arrays.append(array)
            specs.append(spec)
        return arrays, specs

    arrays, in_specs = split(args)
    shapes, out_specs = split(outs)
    first = next(i for i, a in enumerate(arrays) if a.dtype != jnp.int32)
    arrays[first] = after(arrays[first], *(Order.last or ()), *Order.awaited)
    Order.awaited = ()
    result = pl.pallas_call(
        kernel,
        out_shape=shapes,
        grid=grid,
        in_specs=in_specs,
        out_specs=out_specs,
        scratch_shapes=list(scratch),
        compiler_params=pltpu.CompilerParams(vmem_limit_bytes=limit),
        cost_estimate=pl.CostEstimate(
            flops=int(us * SCALE * FLOPS_PER_US), bytes_accessed=0, transcendentals=0
        ),
    )(*arrays)
    Order.last = (result[0],)
    return result


class Chain:
    def __init__(self, steps):
        self.steps, self.result = steps, None
        self.step()

    def step(self):
        if self.result is None:
            try:
                self.got = next(self.steps)
            except StopIteration as stop:
                self.result = stop.value

    def finish(self):
        while self.result is None:
            self.step()
        return self.result


def rotary_tables(offset, length):
    half = HD // 2
    place = (offset + jnp.arange(length, dtype=jnp.int32)).astype(F32)
    freq = jnp.exp(jnp.arange(half).astype(F32) * (-2.0 * math.log(10000.0) / HD))
    angle = place[:, None] * freq[None, :]
    cosine, sine = jnp.cos(angle), jnp.sin(angle)
    return (
        jnp.concatenate([cosine] * 4, axis=1),
        jnp.concatenate([-sine, sine, -sine, sine], axis=1),
    )


def rotate(tile, cosine, sine):
    lane = lax.broadcasted_iota(jnp.int32, tile.shape, 1)
    partner = jnp.where(lane % HD < HD // 2, pltpu.roll(tile, 96, 1), pltpu.roll(tile, 32, 1))
    return tile * cosine + partner * sine


def rotate_into(out_ref, value_ref, width, cosine, sine, factor):
    for start in range(0, width, 128):
        stop = min(start + 128, width)
        turned = rotate(value_ref[:, start : start + 128], cosine, sine) * factor
        out_ref[:, start:stop] = turned[:, : stop - start].astype(out_ref.dtype)


def inverse_mean(value):
    return lax.rsqrt(jnp.mean(value * value, axis=-1, keepdims=True) + EPS)


def prepare_kernel(*refs):
    count = len(refs) // 2
    for source, out in zip(refs[:count], refs[count:]):
        seqs, _, rows = source.shape
        for s in range(seqs):
            out[s * rows : (s + 1) * rows, : source.shape[1]] = source[s].T


def prepare(*arrays):
    outs = [struct((a.shape[0] * a.shape[2], wide(a.shape[1])), a.dtype) for a in arrays]
    return call(prepare_kernel, outs, arrays, us=0.8)


def weight_kernel(kernel, ins, outs, pieces, place_ref, *refs):
    args, parts, rest = refs[:ins], refs[ins : ins + len(pieces)], refs[ins + len(pieces) :]
    if len(pieces) == 1:
        kernel(*args, parts[0], *rest)
        return
    w_ref = rest[outs]

    @pl.when(pl.program_id(0) == 0)
    def _():
        for i, ((start, count), part) in enumerate(zip(pieces, parts)):
            rows = pl.ds(pl.multiple_of(place_ref[i], 16), count)
            w_ref[rows, :] = part[start : start + count, :]

    kernel(*args, w_ref, *rest[:outs], *rest[outs + 1 :])


def with_weight(kernel, outs, args, pieces, places, **kw):
    counts = [(start, count) for _, start, count in pieces]
    arrays = [a for a, _, _ in pieces]
    made = list(outs)
    if len(pieces) > 1:
        made.append(struct((2 * pieces[0][2], arrays[0].shape[1]), arrays[0].dtype))
    body = functools.partial(weight_kernel, kernel, len(args), len(outs), counts)
    result = call(body, made, (places, *args, *arrays), **kw)
    weight = result[-1] if len(pieces) > 1 else arrays[0]
    return result[: len(outs)], [(weight, 0, weight.shape[0])]


def kv_kernel(tok_ref, gain_ref, cos_ref, sin_ref, w_ref, normed_ref, kv_ref, first_ref, ks):
    source = tok_ref[:, : normed_ref.shape[1]].astype(F32)
    normed = (source * inverse_mean(source) * gain_ref[...]).astype(BF16)
    normed_ref[...] = normed
    raw = nn(normed, w_ref[...])
    ks[:, :KW] = raw[:, :KW]
    kv_ref[:, KW:] = raw[:, KW:].astype(BF16)
    rotate_into(kv_ref, ks, KW, cos_ref[...], sin_ref[...], 1.0)
    first_ref[...] = kv_ref[:GRAIN, :]


def project_kv(tokens, seqs, gain, cosine, sine, pieces, places):
    total, width = tokens.shape[0], gain.shape[1]
    rows = total // seqs
    outs = [
        rows_each(struct((total, width), BF16), rows),
        rows_each(struct((total, 2 * KW), BF16), rows),
        rows_each(struct((seqs * GRAIN, 2 * KW), BF16), GRAIN),
    ]
    return with_weight(
        kv_kernel,
        outs,
        (rows_each(tokens, rows), gain, cosine, sine),
        pieces,
        places,
        grid=(seqs,),
        scratch=[pltpu.VMEM((rows, wide(KW)), F32)],
        us=2.2,
    )


def q_kernel(normed_ref, cos_ref, sin_ref, w_ref, q_ref, qs):
    qs[:, :QW] = nn(normed_ref[...], w_ref[...])
    rotate_into(q_ref, qs, QW, cos_ref[...], sin_ref[...], HD**-0.5)


def project_q(normed, seqs, cosine, sine, pieces, places):
    total = normed.shape[0]
    rows = total // seqs
    return with_weight(
        q_kernel,
        [rows_each(struct((total, QW), BF16), rows)],
        (rows_each(normed, rows), cosine, sine),
        pieces,
        places,
        grid=(seqs,),
        scratch=[pltpu.VMEM((rows, wide(QW)), F32)],
        us=2.2,
    )


def residual_kernel(tok_ref, mixed_ref, gain_ref, w_ref, hidden_ref, normed_ref):
    hidden = tok_ref[:, : hidden_ref.shape[1]].astype(F32) + nn(mixed_ref[...], w_ref[...])
    hidden_ref[...] = hidden
    normed_ref[...] = (hidden * inverse_mean(hidden) * gain_ref[...]).astype(BF16)


def residual(tokens, seq, mixed, gain, pieces, places):
    rows, width = mixed.shape[0], gain.shape[1]
    return with_weight(
        residual_kernel,
        [struct((rows, width), F32), struct((rows, width), BF16)],
        (rows_at(tokens, seq, rows), mixed, gain),
        pieces,
        places,
        us=1.8,
    )


def marks(scal_ref, pos, valid):
    segment = jnp.zeros(pos.shape, jnp.int32)
    for d in range(2):
        segment += (pos >= scal_ref[0, d]).astype(jnp.int32)
    number = jnp.zeros(pos.shape, jnp.int32)
    for j in range(2):
        start = scal_ref[0, 2 + j]
        number += jnp.where((pos >= start) & (pos < start + PIECE), j + 1, 0)
    return jnp.where(valid, segment, -1), number


def bias_of(scal_ref, start, across):
    q_shape, k_shape, q_dim, k_dim = (
        ((GRAIN, 1), (1, SPAN), 0, 1) if across else ((1, GRAIN), (SPAN, 1), 1, 0)
    )
    q_pos = start + lax.broadcasted_iota(jnp.int32, q_shape, q_dim)
    k_pos = start - MAXDOC + lax.broadcasted_iota(jnp.int32, k_shape, k_dim)
    q_seg, q_num = marks(scal_ref, q_pos, q_pos >= 0)
    k_seg, k_num = marks(scal_ref, k_pos, (k_pos >= 0) & (k_pos < LEN))
    q_num = jnp.where(q_num > 0, q_num, -1)
    permit = (q_seg == k_seg) & ((k_pos <= q_pos) | (q_num == k_num))
    return jnp.where(permit, 0.0, NEG).astype(F32)


def load_window(window, parts):
    row = 0
    for part in parts:
        window[row : row + part.shape[0], :] = part[...]
        row += part.shape[0]


def head_columns(j):
    return [slice(h * HD, (h + 1) * HD) for h in range(j * GROUP, (j + 1) * GROUP)]


def attend_kernel(scal_ref, q_ref, far_ref, near_ref, own_ref, next_ref, mixed_ref, lse_ref, window):
    sub = pl.program_id(0)

    @pl.when(sub == 0)
    def _():
        load_window(window, (far_ref, near_ref, own_ref, next_ref))

    bias = bias_of(scal_ref, scal_ref[0, 4] + sub * GRAIN, True)
    bias = jnp.concatenate([bias] * GROUP, axis=0)
    rows = pl.ds(pl.multiple_of(sub * GRAIN, GRAIN), SPAN)
    lse = jnp.zeros((GRAIN, 128), F32)
    lane = lax.broadcasted_iota(jnp.int32, (GRAIN, 128), 1)
    for j in range(KVH):
        key = window[rows, j * HD : (j + 1) * HD]
        value = window[rows, KW + j * HD : KW + (j + 1) * HD]
        query = jnp.concatenate([q_ref[:, c] for c in head_columns(j)], axis=0)
        scores = nt(query, key) + bias
        top = jnp.max(scores, axis=-1, keepdims=True)
        raised = jnp.exp(scores - top)
        total = jnp.sum(raised, axis=-1, keepdims=True)
        out = nn(raised.astype(BF16), value) / total
        logsum = top + jnp.log(total)
        for g, c in enumerate(head_columns(j)):
            at = slice(g * GRAIN, (g + 1) * GRAIN)
            mixed_ref[:, c] = out[at].astype(BF16)
            lse = jnp.where(lane == j * GROUP + g, logsum[at], lse)
    lse_ref[...] = lse


def window_parts(windows, seq, rows):
    far, near, own, ahead = windows
    parts = [rows_at(a, seq, rows) for a in (far, near, own)]
    return (*parts, rows_at(ahead, seq, GRAIN))


def sub_rows(array, seq, rows):
    first = seq * (rows // GRAIN)
    return array, pl.BlockSpec((GRAIN, array.shape[1]), lambda i: (first + i, 0))


def attend(scal, q, seq, rows, windows):
    return call(
        attend_kernel,
        [rows_each(struct((rows, w), t), GRAIN) for w, t in ((QW, BF16), (128, F32))],
        (scal, sub_rows(q, seq, rows), *window_parts(windows, seq, rows)),
        grid=(rows // GRAIN,),
        scratch=[pltpu.VMEM((MAXDOC + rows + GRAIN, 2 * KW), BF16)],
        us=6.8,
    )


def attend_back_kernel(
    earlier,
    scal_ref,
    q_ref,
    far_ref,
    near_ref,
    own_ref,
    next_ref,
    mixed_ref,
    lse_ref,
    grad_ref,
    cos_ref,
    sin_ref,
    *refs,
):
    dq_ref, dfar_ref, dnear_ref, down_ref, dnext_ref, window, sums, qs = refs[earlier:]
    sub = pl.program_id(0)

    @pl.when(sub == 0)
    def _():
        load_window(window, (far_ref, near_ref, own_ref, next_ref))
        sums[...] = jnp.zeros_like(sums)

    bias = bias_of(scal_ref, scal_ref[0, 4] + sub * GRAIN, False)
    bias = jnp.concatenate([bias] * GROUP, axis=1)
    rows = pl.ds(pl.multiple_of(sub * GRAIN, GRAIN), SPAN)
    lane = lax.broadcasted_iota(jnp.int32, (GRAIN, 128), 1)
    product = mixed_ref[...].astype(F32) * grad_ref[...].astype(F32)
    delta = jnp.zeros((GRAIN, 128), F32)
    for h in range(H):
        share = jnp.sum(product[:, h * HD : (h + 1) * HD], axis=-1, keepdims=True)
        delta = jnp.where(lane == h, share, delta)
    delta = delta.T
    lse = lse_ref[...].T

    def heads(array, j):
        return jnp.concatenate([array[h : h + 1] for h in range(j * GROUP, (j + 1) * GROUP)], axis=1)

    for j in range(KVH):
        k_cols = slice(j * HD, (j + 1) * HD)
        v_cols = slice(KW + j * HD, KW + (j + 1) * HD)
        key, value = window[rows, k_cols], window[rows, v_cols]
        query = jnp.concatenate([q_ref[:, c] for c in head_columns(j)], axis=0)
        grad = jnp.concatenate([grad_ref[:, c] for c in head_columns(j)], axis=0)
        probs = jnp.exp(nt(key, query) + bias - heads(lse, j))
        grad_scores = (probs * (nt(value, grad) - heads(delta, j))).astype(BF16)
        sums[rows, v_cols] += nn(probs.astype(BF16), grad)
        sums[rows, k_cols] += nn(grad_scores, query)
        dq = tn(key, grad_scores).T
        for g, c in enumerate(head_columns(j)):
            qs[:, c] = dq[g * GRAIN : (g + 1) * GRAIN, :]
    rotate_into(dq_ref, qs, QW, cos_ref[...], -sin_ref[...], HD**-0.5)

    @pl.when(sub == pl.num_programs(0) - 1)
    def _():
        row = 0
        for part in (dfar_ref, dnear_ref, down_ref):
            part[...] = sums[row : row + part.shape[0], :].astype(part.dtype)
            row += part.shape[0]
        done = dnext_ref.shape[0] - GRAIN
        if earlier:
            dnext_ref[:done, :] = refs[0][...]
        dnext_ref[done:, :] = sums[row:, :].astype(BF16)


def attend_back(scal, q, seq, rows, windows, mixed, lse, grad, cosine, sine, earlier):
    window = MAXDOC + rows + GRAIN
    each = lambda a: rows_each(a, GRAIN)
    shapes = ((rows, BF16), (rows, BF16), (rows, F32), ((seq + 1) * GRAIN, BF16))
    return call(
        functools.partial(attend_back_kernel, len(earlier)),
        [each(struct((rows, QW), BF16)), *(struct((r, 2 * KW), t) for r, t in shapes)],
        (
            scal,
            sub_rows(q, seq, rows),
            *window_parts(windows, seq, rows),
            *map(each, (mixed, lse, grad, cosine, sine)),
            *earlier,
        ),
        grid=(rows // GRAIN,),
        scratch=[
            pltpu.VMEM((window, 2 * KW), BF16),
            pltpu.VMEM((window, 2 * KW), F32),
            pltpu.VMEM((GRAIN, wide(QW)), F32),
        ],
        us=11.7,
    )


def ff_kernel(nrm_a, nrm_b, cot_a, cot_b, w_ref, inner_ref, gg_ref, gu_ref, sum_a, sum_b):
    first = pl.program_id(0) == 0
    (rows, units), width = inner_ref.shape, w_ref.shape[0]
    wg, wu, wd = (w_ref[:, k * units : (k + 1) * units] for k in range(3))
    normed = jnp.where(first, nrm_a[...], nrm_b[...])
    gate = nn(normed, wg)
    up = nn(normed, wu)
    grad = nn(jnp.where(first, cot_a[:, :width], cot_b[:, :width]), wd)
    sigma = jax.nn.sigmoid(gate)
    raised = gate * sigma
    inner = (raised * up).astype(BF16)
    grad_gate = (grad * up * (sigma + raised * (1.0 - sigma))).astype(BF16)
    grad_up = (grad * raised).astype(BF16)
    inner_ref[...] = inner
    gg_ref[...] = grad_gate
    gu_ref[...] = grad_up
    grad_normed = (nt(grad_gate, wg) + nt(grad_up, wu)).astype(BF16)
    out = nt(inner, wd).astype(BF16)

    @pl.when(first)
    def _():
        sum_a[:rows, :width] = grad_normed
        sum_a[rows:, :width] = out

    @pl.when(jnp.logical_not(first))
    def _():
        sum_b[:rows, :width] = grad_normed
        sum_b[rows:, :width] = out


def ff(normed_pair, cot_pair, weights, seq):
    rows, width = normed_pair[0].shape
    units = weights.shape[1] // 3
    unit = lambda: rows_each(struct((2 * rows, units), BF16), rows)
    result = call(
        ff_kernel,
        [unit(), unit(), unit()] + [struct((2 * rows, wide(width)), BF16)] * 2,
        (*normed_pair, *(rows_at(c, seq, rows) for c in cot_pair), weights),
        grid=(2,),
        us=7.2,
    )
    return result[:3], result[3:]


def outer_kernel(counts, split, place_ref, *refs):
    acc = refs[-1]
    column = 0
    for lefts, rights, gains in counts:
        left_refs, refs = refs[:lefts], refs[lefts:]
        right_refs, refs = refs[:rights], refs[rights:]
        gain_refs, refs = refs[:gains], refs[gains:]
        width = right_refs[0].shape[-1]
        at = slice(column, column + width)
        join = lambda some, w: jnp.concatenate([r[:, :w] for r in some], axis=0)
        if lefts % rights:
            groups = [(left_refs, right_refs)]
        else:
            per = lefts // rights
            groups = [(left_refs[i * per : (i + 1) * per], [r]) for i, r in enumerate(right_refs)]
        for i, (some_left, some_right) in enumerate(groups):
            product = tn(join(some_left, acc.shape[0]), join(some_right, width))
            if i == 0:
                acc[:, at] = product
            else:
                acc[:, at] += product
        column += width
        if gains:
            total = functools.reduce(jnp.add, [g[...] for g in gain_refs])
            across = jnp.broadcast_to(total, (128, total.shape[1])).T
            stop = wide(column)
            acc[:, column:stop] = across[:, : stop - column]
            column = stop
    outs = refs[:-1]
    if split is None:
        outs[0][...] = acc[...]
        return
    keep_ref, send_ref = outs
    half = keep_ref.shape[0] if split == "shard" else keep_ref.shape[0] // 2
    for s in range(acc.shape[0] // (2 * half)):
        rows = slice(s * half, (s + 1) * half)
        keep_ref[rows, :] = acc[pl.ds(pl.multiple_of(2 * s * half + place_ref[0], 16), half), :]
        other = pl.ds(pl.multiple_of((2 * s + 1) * half - place_ref[0], 16), half)
        send_ref[rows, :] = acc[other, :].astype(BF16)


def outer(products, width, place, split, us, limit=VMEM_LIMIT):
    array = lambda operand: operand[0] if isinstance(operand, tuple) else operand
    full = 0
    for _, rights, gains in products:
        full += array(rights[0]).shape[1]
        full = wide(full) if gains else full
    if split is None:
        outs = [struct((width, full), F32)]
    else:
        outs = [struct((width // 2, full), F32), struct((width // 2, full), BF16)]
    args = [a for product in products for group in product for a in group]
    return call(
        functools.partial(outer_kernel, [tuple(map(len, p)) for p in products], split),
        outs,
        (place, *args),
        scratch=[pltpu.VMEM((width, full), F32)],
        us=us,
        limit=limit,
    )


def output_kernel(hidden_ref, *refs):
    total = hidden_ref[...]
    for term in refs[:-1]:
        total += term[:, : total.shape[1]].astype(F32)
    refs[-1][...] = total.T.astype(BF16)


def output_of(hidden, terms):
    rows, width = hidden.shape
    return call(output_kernel, [struct((width, rows), BF16)], (hidden, *terms), us=1.4)[0]


def ff_back_kernel(
    hidden_ref, cot_ref, a_ref, b_ref, c_ref, gain_ref, wo_ref, gh_ref, gb_ref, gm_ref, gg_ref
):
    hidden, gain = hidden_ref[...], gain_ref[...]
    factor = inverse_mean(hidden)
    width = hidden.shape[1]
    grad = sum(ref[:, :width].astype(F32) for ref in (a_ref, b_ref, c_ref))
    weighted = grad * gain
    back = factor * weighted - hidden * factor**3 * jnp.mean(
        hidden * weighted, axis=-1, keepdims=True
    )
    grad_hidden = cot_ref[:, :width].astype(F32) + back
    branch = grad_hidden.astype(BF16)
    gh_ref[...] = grad_hidden
    gb_ref[...] = branch
    gm_ref[...] = nt(branch, wo_ref[...]).astype(BF16)
    gg_ref[...] = jnp.sum(grad * hidden * factor, axis=0, keepdims=True)


def ff_back(hidden, cotangent, seq, terms, gain, wo):
    rows, width = hidden.shape
    outs = [
        struct((rows, width), F32),
        struct((rows, width), BF16),
        struct((rows, QW), BF16),
        struct((1, width), F32),
    ]
    return call(
        ff_back_kernel,
        outs,
        (hidden, rows_at(cotangent, seq, rows), *terms, gain, wo),
        us=1.8,
    )


def input_kernel(
    tok_ref,
    gh_ref,
    gq_ref,
    own_ref,
    left_ref,
    right_ref,
    gain_ref,
    wq_ref,
    wkv_ref,
    cos_ref,
    sin_ref,
    ig_ref,
    gkv_ref,
    ks,
):
    ks[...] = own_ref[...] + right_ref[...].astype(F32)
    ks[:GRAIN, :] += left_ref[...].astype(F32)
    gkv_ref[:, KW:] = ks[:, KW:].astype(BF16)
    rotate_into(gkv_ref, ks, KW, cos_ref[...], -sin_ref[...], 1.0)
    grad = nt(gq_ref[...], wq_ref[...]) + nt(gkv_ref[...], wkv_ref[...])
    source, gain = tok_ref[:, : gh_ref.shape[1]].astype(F32), gain_ref[...]
    factor = inverse_mean(source)
    weighted = grad * gain
    back = factor * weighted - source * factor**3 * jnp.mean(
        source * weighted, axis=-1, keepdims=True
    )
    ig_ref[...] = (gh_ref[...] + back).T


def input_back(tokens, seq, args):
    rows, width = args[0].shape
    return call(
        input_kernel,
        [struct((width, rows), F32), struct((rows, 2 * KW), BF16)],
        (rows_at(tokens, seq, rows), *args),
        scratch=[pltpu.VMEM((rows, 2 * KW), F32)],
        us=1.8,
    )


def add_kernel(*refs):
    total = refs[0][...].astype(F32)
    for ref in refs[1:-1]:
        total += ref[...].astype(F32)
    refs[-1][...] = total.astype(refs[-1].dtype)


def add_up(terms, shape, dtype):
    return call(add_kernel, [struct(shape, dtype)], terms, us=0.7)[0]


def side_kernel(*refs):
    width = refs[0].shape[1]
    for i, ref in enumerate(refs[:-1]):
        refs[-1][:, i * width : (i + 1) * width] = ref[...]


def side_by_side(*arrays):
    rows, width = arrays[0].shape
    return call(side_kernel, [struct((rows, len(arrays) * width), BF16)], arrays, us=0.8)[0]


def widen_kernel(all_ref, *outs):
    units = outs[0].shape[1]
    for i, out in enumerate(outs):
        out[...] = all_ref[:, i * units : (i + 1) * units].astype(F32)


def widen(value):
    rows, columns = value.shape
    return call(widen_kernel, [struct((rows, columns // 3), F32)] * 3, (value,), us=2.0)


def beside_kernel(left_ref, keep_ref, got_ref, out_ref):
    columns = left_ref.shape[1]
    out_ref[:, :columns] = left_ref[...]
    out_ref[:, columns:] = (keep_ref[...] + got_ref[...].astype(F32)).astype(BF16)


def set_beside(left, keep, got):
    shape = (left.shape[0], left.shape[1] + keep.shape[1])
    return call(beside_kernel, [struct(shape, BF16)], (left, keep, got), us=1.5)[0]


def pair_kernel(*refs):
    out = refs[-1]
    rows = refs[0].shape[0]
    for s in range(len(refs) // 2):
        total = refs[2 * s][...].astype(F32) + refs[2 * s + 1][...].astype(F32)
        out[s * rows : (s + 1) * rows, :] = total.astype(BF16)


def split_kernel(at_ref, keep_ref, got_ref, kept_ref, sent_ref, total):
    total[...] = keep_ref[...].astype(F32) + got_ref[...].astype(F32)
    half = kept_ref.shape[0]
    kept_ref[...] = total[pl.ds(pl.multiple_of(at_ref[0] * half, 8), half), :]
    sent_ref[...] = total[pl.ds(pl.multiple_of((1 - at_ref[0]) * half, 8), half), :].astype(BF16)


def split_sum(at, keep, got):
    shape = (keep.shape[0] // 2, keep.shape[1])
    return call(
        split_kernel,
        [struct(shape, F32), struct(shape, BF16)],
        (at, keep, got),
        scratch=[pltpu.VMEM(keep.shape, F32)],
        us=0.9,
    )


def put_halves(both, at_ref, own_ref, got_ref):
    half = own_ref.shape[0]
    if half == both.shape[0]:
        both[...] = own_ref[...].astype(F32)
        return
    for place, ref in ((at_ref[0], own_ref), (1 - at_ref[0], got_ref)):
        both[pl.ds(pl.multiple_of(place * half, 8), half), :] = ref[...].astype(F32)


def join_kernel(at_ref, own_ref, got_ref, out_ref, both):
    put_halves(both, at_ref, own_ref, got_ref)
    out_ref[...] = both[...].astype(out_ref.dtype)


def join_rows(at, own, got):
    shape = (2 * own.shape[0], own.shape[1])
    return call(
        join_kernel,
        [struct(shape, BF16)],
        (at, own, got),
        scratch=[pltpu.VMEM(shape, F32)],
        us=0.9,
    )[0]


def as_row(column):
    return jnp.broadcast_to(column, (column.shape[0], 128)).T[:1]


def finish_pair_kernel(at_ref, own_ref, got_ref, w_ref, out_ref, gain_ref, query_ref, sum_ref, both):
    put_halves(both, at_ref, own_ref, got_ref)
    width = out_ref.shape[1]
    out_ref[...] = both[:, :width]
    gain_ref[...] = as_row(both[:, width : width + 1])
    query = both[:, both.shape[1] - QW :]
    query_ref[...] = query
    sum_ref[...] = as_row(jnp.sum(query * w_ref[...].astype(F32), axis=-1, keepdims=True))


def finish_pair(at, own, got, weight, width):
    rows = weight.shape[0]
    return call(
        finish_pair_kernel,
        [struct(s, F32) for s in ((rows, width), (1, rows), (rows, QW), (1, rows))],
        (at, own, got, weight),
        scratch=[pltpu.VMEM((rows, own.shape[1]), F32)],
        us=1.5,
    )


def finish_kv_kernel(at_ref, own_ref, got_ref, w_ref, sum_ref, gain_ref, k_ref, v_ref, grad_ref, both):
    put_halves(both, at_ref, own_ref, got_ref)
    k_ref[...] = both[:, :KW].T
    v_ref[...] = both[:, KW:].T
    rest = as_row(jnp.sum(both[...] * w_ref[...].astype(F32), axis=-1, keepdims=True))
    grad_ref[...] = (sum_ref[...] + rest) / gain_ref[...]


def finish_kv(at, own, got, weight, sums, gain):
    rows = weight.shape[0]
    return call(
        finish_kv_kernel,
        [struct(s, F32) for s in ((KW, rows), (KW, rows), (1, rows))],
        (at, own, got, weight, sums, gain),
        scratch=[pltpu.VMEM((rows, own.shape[1]), F32)],
        us=1.5,
    )


def program(mesh):
    shards, ctxs = mesh.shape["shard"], mesh.shape["ctx"]

    def swap(value, axis, bit):
        count = mesh.shape[axis]
        return lax.ppermute(value, axis, [(i, i ^ bit) for i in range(count)])

    def shift(value, by):
        pairs = [(i, i + by) for i in range(ctxs) if 0 <= i + by < ctxs]
        return lax.ppermute(value, "ctx", pairs)

    def place_of(index):
        return index.astype(jnp.int32)[None]

    def over_shard(terms):
        return lax.psum_scatter(terms[0], "shard", scatter_dimension=0, tiled=True)

    def reduce_units(terms, finish):
        if shards != 2:
            return finish(over_shard(terms), None)
        keep, send = terms
        got = swap(send, "shard", 1)
        yield got
        return finish(keep, got)

    def all_over_ctx(value):
        part = lax.psum_scatter(value, "ctx", scatter_dimension=0, tiled=True)
        return lax.all_gather(part, "ctx", axis=0, tiled=True)

    def reduce_attention(terms, finish):
        zero = jnp.zeros((1,), jnp.int32)
        if shards != 2:
            total = lax.psum(over_shard(terms), ("ctx", "tp"))
            return finish(zero, total, total)
        tp = lax.axis_index("tp")
        mine, core, row = map(place_of, (lax.axis_index("shard"), tp % 2, tp // 2))
        held, low = terms
        got = swap(low, "tp", 1)
        yield got
        held, low = split_sum(mine, held, got)
        got = swap(low, "shard", 1)
        yield got
        held, low = split_sum(row, held, got)
        got = swap(low, "tp", 2)
        yield got
        low = add_up((held, got), held.shape, BF16)
        bit = 1
        while bit < ctxs:
            got = swap(low, "ctx", bit)
            yield got
            low = add_up((low, got), low.shape, BF16)
            bit *= 2
        got = swap(low, "tp", 2)
        yield got
        low = join_rows(row, low, got)
        got = swap(low, "tp", 1)
        yield got
        return finish(core, low, got)

    def per_device(
        tokens,
        cotangent,
        piece_starts,
        doc_lengths,
        attn_gain,
        w_query,
        w_key,
        w_value,
        w_out,
        ff_gain,
        w_gate,
        w_up,
        w_down,
    ):
        Order.last, Order.awaited = None, ()
        seqs, rows, width = tokens.shape
        offset = (lax.axis_index("ctx") * rows).astype(jnp.int32)
        mine, tp = lax.axis_index("shard"), lax.axis_index("tp")
        core, row = tp % 2, tp // 2
        every = range(seqs)
        last = seqs - 1

        (tokens,) = prepare(tokens.transpose(0, 2, 1))
        cosine, sine = rotary_tables(offset, rows)
        ends = jnp.cumsum(doc_lengths, axis=1)[:, :-1]
        scal = jnp.concatenate(
            [ends, piece_starts, jnp.broadcast_to(offset, (seqs, 1))], axis=1
        ).astype(jnp.int32)
        scals = [scal[s : s + 1] for s in every]

        w_kv = jnp.concatenate([w_key, w_value], axis=1)
        gains = jnp.stack([attn_gain, ff_gain])
        if shards == 2:
            full = w_query.shape[0]
            half = full // 2
            span = -(-half // 32) * 16
            other = (1 - mine) * full
            near_rows, far_rows = other + core * half, other + (1 - core) * half
            step, back = row * (half - span), (1 - row) * (half - span)
            kv_places = jnp.stack([mine * full, near_rows, far_rows]).astype(jnp.int32)
            places = [near_rows + step, near_rows + back, far_rows + step, far_rows + back]
            places = jnp.stack([mine * full, *places]).astype(jnp.int32)
            quarter = lambda w: lax.dynamic_slice_in_dim(w, core * half + step, span)

            got = swap(gains, "shard", 1)
            all_gains = jnp.where(
                mine == 0,
                jnp.concatenate([gains, got], axis=1),
                jnp.concatenate([got, gains], axis=1),
            )
            kv_part = swap(lax.dynamic_slice_in_dim(w_kv, core * half, half), "shard", 1)
            kv_beside = swap(in_turn(kv_part), "tp", 1)
            kv_pieces = [(w_kv, 0, full), (kv_part, 0, half), (kv_beside, 0, half)]
            two = jnp.concatenate([quarter(w_query), quarter(w_out)], axis=0)
            two_x = swap(after(two, kv_part), "shard", 1)
        else:
            gather = lambda w: lax.all_gather(w, "shard", axis=0, tiled=True)
            kv_places = places = jnp.zeros((1,), jnp.int32)
            all_gains = lax.all_gather(gains, "shard", axis=1, tiled=True)
            kv_pieces = [(gather(w_kv), 0, width)]
        gain_one, gain_two = all_gains[:1].astype(F32), all_gains[1:].astype(F32)

        (normed_one, kv, first), kv_pieces = project_kv(
            tokens, seqs, gain_one, cosine, sine, kv_pieces, kv_places
        )
        wkv = kv_pieces[0][0]
        near, ahead = shift(kv, 1), shift(first, -1)
        (cotangent,) = prepare(cotangent.transpose(0, 2, 1))
        if shards == 2:
            two_x = in_turn(two_x)
            two_y, two_beside = swap(two_x, "tp", 2), swap(two_x, "tp", 1)
        ff_weights = lax.all_gather(side_by_side(w_gate, w_up, w_down), "shard", axis=0, tiled=True)
        if shards == 2:
            two_y = in_turn(two_y)
            parts = (two_x, two_y, two_beside, swap(two_y, "tp", 1))
            q_pieces = [(w_query, 0, full), *((p, 0, span) for p in parts)]
            out_pieces = [(w_out, 0, full), *((p, span, span) for p in parts)]
        else:
            q_pieces, out_pieces = ([(gather(w), 0, width)] for w in (w_query, w_out))
            two_y = w_query
        windows = (shift(in_turn(near), 1), near, kv, ahead)
        cot_y = swap(after(cotangent, two_y, near), "tp", 2)
        arrive(ahead)
        (query,), q_pieces = project_q(normed_one, seqs, cosine, sine, q_pieces, places)
        wq = q_pieces[0][0]
        cot_core = swap(in_turn(cotangent), "tp", 1)

        mixed, lse, hidden, normed_rows = [], [], [], []
        for s in every:
            if s == 1:
                cot_y = in_turn(cot_y)
                cot_diagonal = swap(cot_y, "tp", 1)
            m, l = attend(scals[s], query, s, rows, windows)
            if s == 0:
                arrive(cot_core)
            else:
                arrive(normed_rows[-1][1])
            if s == 1:
                arrive(cot_diagonal)
            (h, own), out_pieces = residual(tokens, s, m, gain_two, out_pieces, places)
            normed_rows.append((own, swap(own, "tp", 1), swap(own, "tp", 2)))
            mixed.append(m)
            lse.append(l)
            hidden.append(h)
        wo = out_pieces[0][0]
        if seqs == 1:
            cot_diagonal = swap(cot_y, "tp", 1)
        cots = (cotangent, cot_core, cot_y, cot_diagonal)

        row_blocks, units, near_sums, far_sums = [], [], [], []
        grad_at = lambda a: rows_at(a, 0, rows)
        out_at = lambda a: rows_at(a, 1, rows)

        def cross_grad(s):
            partial = add_up([grad_at(a) for a in far_sums[s]], (rows, wide(width)), BF16)
            return (*map(grad_at, near_sums[s]), swap(partial, "tp", 2))

        grad_terms = []
        for s in every:
            own, beside, facing = normed_rows[s]
            diagonal = swap(in_turn(facing), "tp", 1)
            if s > 0:
                arrive(near_sums[s - 1][1])
            unit, (a, b) = ff((own, beside), cots[:2], ff_weights, s)
            near_sums.append((a, swap(b, "tp", 1)))
            units.append(unit)
            if s > 0:
                grad_terms.append(cross_grad(s - 1))
            arrive(*(n[1] for n in normed_rows[s + 1 : s + 2]))
            unit, (a, b) = ff((facing, diagonal), cots[2:], ff_weights, s)
            far_sums.append((a, swap(b, "tp", 1)))
            units.append(unit)
            row_blocks += [own, beside, facing, diagonal]

        by_shard, by_core = ("shard", "core") if shards == 2 else (None, None)
        shard_place, core_place = place_of(mine * (width // 2)), place_of(core * (width // 4))
        cot_lefts = [rows_at(c, s, rows) for s in every for c in cots]

        def unit_product(lefts, k):
            return lefts, [u[k] for u in units], ()

        arrive(near_sums[last][1])
        def down_sum(keep, got):
            if got is None:
                return keep.astype(BF16)
            return add_up((keep, got), keep.shape, BF16)

        def units_sum(keep, got):
            left = down.finish()
            if got is None:
                return jnp.concatenate([left, keep.astype(BF16)], axis=1)
            return set_beside(left, keep, got)

        down_grad = outer([unit_product(cot_lefts, 0)], width, shard_place, by_shard, 5.0)
        down = Chain(reduce_units(down_grad, down_sum))
        grad_terms.append(cross_grad(last))
        both = [unit_product(row_blocks, 1), unit_product(row_blocks, 2)]
        arrive(*(t[2] for t in grad_terms[:-1]))
        gate_up_grad = outer(both, width, shard_place, by_shard, 10.0, 2 * VMEM_LIMIT)
        gate_up = Chain(reduce_units(gate_up_grad, units_sum))
        out_terms = [out_at(a) for s in every for a in far_sums[s]]
        out_partial = call(
            pair_kernel, [struct((seqs * rows, wide(width)), BF16)], out_terms, us=0.9
        )[0]
        outs_got = swap(after(out_partial, grad_terms[last][2]), "tp", 2)

        branch, gain_two_grad, grad_hidden = [], [], []
        backs, input_grads, gkv = [], [], []
        ahead_grads = ()

        def mixed_back(s, ahead_grads):
            gh, gb, gm, gg = ff_back(hidden[s], cotangent, s, grad_terms[s], gain_two, wo)
            grad_hidden.append(gh)
            branch.append(gb)
            gain_two_grad.append(gg)
            dq, dfar, dnear, own, dnext = attend_back(
                scals[s], query, s, rows, windows, mixed[s], lse[s], gm, cosine, sine, ahead_grads
            )
            backs.append((dq, dnear, own, shift(dfar, -1)))
            return (dnext,)

        def pass_on(s):
            dq, dnear, own, passed = backs[s]
            backs[s] = dq, own, shift(add_up((dnear, passed), dnear.shape, BF16), -1)

        def rows_back(s):
            dq, own, right = backs[s]
            args = (grad_hidden[s], dq, own, rows_at(left, s, GRAIN), right)
            args += (gain_one, wq, wkv, cosine, sine)
            input_grad, g = input_back(tokens, s, args)
            input_grads.append(input_grad)
            gkv.append(g)

        for s in every:
            ahead_grads = mixed_back(s, ahead_grads)
            if s == 0:
                down.step()
                down.finish()
        left = shift(ahead_grads[0], 1)
        for s in every[:-1]:
            pass_on(s)
        arrive(outs_got)
        gate_up.step()
        unit_sums = all_over_ctx(gate_up.finish())
        pass_on(last)
        grads = [b[0] for b in backs]
        pair = Chain(
            reduce_attention(
                outer(
                    [(mixed, branch, gain_two_grad), ([normed_one], grads, ())],
                    width,
                    core_place,
                    by_core,
                    2.7,
                    2 * VMEM_LIMIT,
                ),
                lambda at, own, got: finish_pair(at, own, got, w_query, width),
            )
        )
        outputs = []
        for s in every:
            near_terms = [out_at(a) for a in near_sums[s]]
            outputs.append(output_of(hidden[s], (*near_terms, rows_at(outs_got, s, rows))))
        pair.step()
        for s in every:
            rows_back(s)
        pair.step()
        finish_last = lambda at, own, got: (at, own, got)
        keys = Chain(
            reduce_attention(
                outer([([normed_one], gkv, ())], width, core_place, by_core, 1.1), finish_last
            )
        )
        for chain in (keys, pair, keys, pair, keys):
            chain.step()
        for chain in (pair, keys):
            chain.step()
        sum_down, sum_gate, sum_up = widen(unit_sums)
        for chain in (pair, keys, pair, keys):
            chain.step()
        sum_out, sum_gain_two, sum_query, products = pair.finish()
        keys_done = keys.finish()
        sum_key, sum_value, sum_gain_one = finish_kv(
            *keys_done, w_kv, products, gains[:1].astype(F32)
        )
        join = lambda blocks: jnp.stack(blocks).transpose(0, 2, 1)
        return (
            join(outputs),
            join(input_grads),
            sum_gain_one[0],
            sum_query,
            sum_key.T,
            sum_value.T,
            sum_out,
            sum_gain_two[0],
            sum_gate,
            sum_up,
            sum_down,
        )

    return per_device


def solution(mesh):
    rows = P(("shard", "tp"), "ctx", None)
    seq = P(("shard", "tp"), None)
    gain, weight, ff_weight = P("shard"), P("shard", None), P("shard", "tp")
    weights = (gain, weight, weight, weight, weight, gain, ff_weight, ff_weight, ff_weight)
    return jax.shard_map(
        program(mesh),
        mesh=mesh,
        in_specs=(rows, rows, seq, seq, *weights),
        out_specs=(rows, rows, *weights),
        check_vma=False,
    )
```

```python
import functools
import math

import jax
import jax.numpy as jnp
from jax import lax
from jax.experimental import pallas as pl
from jax.experimental.pallas import tpu as pltpu
from jax.sharding import PartitionSpec as P

H = 15
KVH = 5
HD = 64
LEN = 1024
PIECE = 256
GRAIN = 128
MAXDOC = 512
GROUP = H // KVH
KW = KVH * HD
QW = H * HD
SPAN = MAXDOC + 2 * GRAIN

EPS = 1e-05
NEG = -1e30
F32 = jnp.float32
BF16 = jnp.bfloat16
VMEM_LIMIT = 20 * 1024 * 1024
SCALE = 10.0
FLOPS_PER_US = 1.15e9


def dot(left, right, dims):
    return lax.dot_general(left, right, (dims, ((), ())), preferred_element_type=F32)


def nn(left, right):
    return dot(left, right, ((1,), (0,)))


def nt(left, right):
    return dot(left, right, ((1,), (1,)))


def tn(left, right):
    return dot(left, right, ((0,), (0,)))


def wide(width):
    return -(-width // 128) * 128


class Order:
    last = None
    awaited = ()


def arrive(*values):
    Order.awaited += values


def after(value, *deps):
    return lax.optimization_barrier((value, deps))[0] if deps else value


def in_turn(value):
    return value if Order.last is None else after(value, *Order.last)


def struct(shape, dtype):
    return jax.ShapeDtypeStruct(shape, dtype)


def rows_at(array, index, count):
    return array, pl.BlockSpec((count, array.shape[1]), lambda *_: (index, 0))


def rows_each(array, count):
    return array, pl.BlockSpec((count, array.shape[1]), lambda i: (i, 0))


def call(kernel, outs, args, *, us, grid=(1,), scratch=(), limit=VMEM_LIMIT):
    def split(operands):
        arrays, specs = [], []
        for operand in operands:
            if isinstance(operand, tuple):
                array, spec = operand
            elif operand.dtype == jnp.int32:
                array, spec = operand, pl.BlockSpec(memory_space=pltpu.SMEM)
            else:
                array = operand
                spec = pl.BlockSpec(array.shape, lambda *_, n=len(array.shape): (0,) * n)
            arrays.append(array)
            specs.append(spec)
        return arrays, specs

    arrays, in_specs = split(args)
    shapes, out_specs = split(outs)
    first = next(i for i, a in enumerate(arrays) if a.dtype != jnp.int32)
    arrays[first] = after(arrays[first], *(Order.last or ()), *Order.awaited)
    Order.awaited = ()
    result = pl.pallas_call(
        kernel,
        out_shape=shapes,
        grid=grid,
        in_specs=in_specs,
        out_specs=out_specs,
        scratch_shapes=list(scratch),
        compiler_params=pltpu.CompilerParams(vmem_limit_bytes=limit),
        cost_estimate=pl.CostEstimate(
            flops=int(us * SCALE * FLOPS_PER_US), bytes_accessed=0, transcendentals=0
        ),
    )(*arrays)
    Order.last = (result[0],)
    return result


class Chain:
    def __init__(self, steps):
        self.steps, self.result = steps, None
        self.step()

    def step(self):
        if self.result is None:
            try:
                self.got = next(self.steps)
            except StopIteration as stop:
                self.result = stop.value

    def finish(self):
        while self.result is None:
            self.step()
        return self.result


def rotary_tables(offset, length):
    half = HD // 2
    place = (offset + jnp.arange(length, dtype=jnp.int32)).astype(F32)
    freq = jnp.exp(jnp.arange(half).astype(F32) * (-2.0 * math.log(10000.0) / HD))
    angle = place[:, None] * freq[None, :]
    cosine, sine = jnp.cos(angle), jnp.sin(angle)
    return (
        jnp.concatenate([cosine] * 4, axis=1),
        jnp.concatenate([-sine, sine, -sine, sine], axis=1),
    )


def rotate(tile, cosine, sine):
    lane = lax.broadcasted_iota(jnp.int32, tile.shape, 1)
    partner = jnp.where(lane % HD < HD // 2, pltpu.roll(tile, 96, 1), pltpu.roll(tile, 32, 1))
    return tile * cosine + partner * sine


def rotate_into(out_ref, value_ref, width, cosine, sine, factor):
    for start in range(0, width, 128):
        stop = min(start + 128, width)
        turned = rotate(value_ref[:, start : start + 128], cosine, sine) * factor
        out_ref[:, start:stop] = turned[:, : stop - start].astype(out_ref.dtype)


def inverse_mean(value):
    return lax.rsqrt(jnp.mean(value * value, axis=-1, keepdims=True) + EPS)


def prepare_kernel(*refs):
    count = len(refs) // 2
    for source, out in zip(refs[:count], refs[count:]):
        seqs, _, rows = source.shape
        for s in range(seqs):
            out[s * rows : (s + 1) * rows, : source.shape[1]] = source[s].T


def prepare(*arrays):
    outs = [struct((a.shape[0] * a.shape[2], wide(a.shape[1])), a.dtype) for a in arrays]
    return call(prepare_kernel, outs, arrays, us=0.8)


def weight_kernel(kernel, ins, outs, pieces, place_ref, *refs):
    args, parts, rest = refs[:ins], refs[ins : ins + len(pieces)], refs[ins + len(pieces) :]
    if len(pieces) == 1:
        kernel(*args, parts[0], *rest)
        return
    w_ref = rest[outs]

    @pl.when(pl.program_id(0) == 0)
    def _():
        for i, ((start, count), part) in enumerate(zip(pieces, parts)):
            rows = pl.ds(pl.multiple_of(place_ref[i], 16), count)
            w_ref[rows, :] = part[start : start + count, :]

    kernel(*args, w_ref, *rest[:outs], *rest[outs + 1 :])


def with_weight(kernel, outs, args, pieces, places, **kw):
    counts = [(start, count) for _, start, count in pieces]
    arrays = [a for a, _, _ in pieces]
    made = list(outs)
    if len(pieces) > 1:
        made.append(struct((2 * pieces[0][2], arrays[0].shape[1]), arrays[0].dtype))
    body = functools.partial(weight_kernel, kernel, len(args), len(outs), counts)
    result = call(body, made, (places, *args, *arrays), **kw)
    weight = result[-1] if len(pieces) > 1 else arrays[0]
    return result[: len(outs)], [(weight, 0, weight.shape[0])]


def kv_kernel(tok_ref, gain_ref, cos_ref, sin_ref, w_ref, normed_ref, kv_ref, first_ref, ks):
    source = tok_ref[:, : normed_ref.shape[1]].astype(F32)
    normed = (source * inverse_mean(source) * gain_ref[...]).astype(BF16)
    normed_ref[...] = normed
    raw = nn(normed, w_ref[...])
    ks[:, :KW] = raw[:, :KW]
    kv_ref[:, KW:] = raw[:, KW:].astype(BF16)
    rotate_into(kv_ref, ks, KW, cos_ref[...], sin_ref[...], 1.0)
    first_ref[...] = kv_ref[:GRAIN, :]


def project_kv(tokens, seqs, gain, cosine, sine, pieces, places):
    total, width = tokens.shape[0], gain.shape[1]
    rows = total // seqs
    outs = [
        rows_each(struct((total, width), BF16), rows),
        rows_each(struct((total, 2 * KW), BF16), rows),
        rows_each(struct((seqs * GRAIN, 2 * KW), BF16), GRAIN),
    ]
    return with_weight(
        kv_kernel,
        outs,
        (rows_each(tokens, rows), gain, cosine, sine),
        pieces,
        places,
        grid=(seqs,),
        scratch=[pltpu.VMEM((rows, wide(KW)), F32)],
        us=2.2,
    )


def q_kernel(normed_ref, cos_ref, sin_ref, w_ref, q_ref, qs):
    qs[:, :QW] = nn(normed_ref[...], w_ref[...])
    rotate_into(q_ref, qs, QW, cos_ref[...], sin_ref[...], HD**-0.5)


def project_q(normed, seqs, cosine, sine, pieces, places):
    total = normed.shape[0]
    rows = total // seqs
    return with_weight(
        q_kernel,
        [rows_each(struct((total, QW), BF16), rows)],
        (rows_each(normed, rows), cosine, sine),
        pieces,
        places,
        grid=(seqs,),
        scratch=[pltpu.VMEM((rows, wide(QW)), F32)],
        us=2.2,
    )


def residual_kernel(tok_ref, mixed_ref, gain_ref, w_ref, hidden_ref, normed_ref):
    hidden = tok_ref[:, : hidden_ref.shape[1]].astype(F32) + nn(mixed_ref[...], w_ref[...])
    hidden_ref[...] = hidden
    normed_ref[...] = (hidden * inverse_mean(hidden) * gain_ref[...]).astype(BF16)


def residual(tokens, seq, mixed, gain, pieces, places):
    rows, width = mixed.shape[0], gain.shape[1]
    return with_weight(
        residual_kernel,
        [struct((rows, width), F32), struct((rows, width), BF16)],
        (rows_at(tokens, seq, rows), mixed, gain),
        pieces,
        places,
        us=1.8,
    )


def marks(scal_ref, pos, valid):
    segment = jnp.zeros(pos.shape, jnp.int32)
    for d in range(2):
        segment += (pos >= scal_ref[0, d]).astype(jnp.int32)
    number = jnp.zeros(pos.shape, jnp.int32)
    for j in range(2):
        start = scal_ref[0, 2 + j]
        number += jnp.where((pos >= start) & (pos < start + PIECE), j + 1, 0)
    return jnp.where(valid, segment, -1), number


def bias_of(scal_ref, start, across):
    q_shape, k_shape, q_dim, k_dim = (
        ((GRAIN, 1), (1, SPAN), 0, 1) if across else ((1, GRAIN), (SPAN, 1), 1, 0)
    )
    q_pos = start + lax.broadcasted_iota(jnp.int32, q_shape, q_dim)
    k_pos = start - MAXDOC + lax.broadcasted_iota(jnp.int32, k_shape, k_dim)
    q_seg, q_num = marks(scal_ref, q_pos, q_pos >= 0)
    k_seg, k_num = marks(scal_ref, k_pos, (k_pos >= 0) & (k_pos < LEN))
    q_num = jnp.where(q_num > 0, q_num, -1)
    permit = (q_seg == k_seg) & ((k_pos <= q_pos) | (q_num == k_num))
    return jnp.where(permit, 0.0, NEG).astype(F32)


def load_window(window, parts):
    row = 0
    for part in parts:
        window[row : row + part.shape[0], :] = part[...]
        row += part.shape[0]


def head_columns(j):
    return [slice(h * HD, (h + 1) * HD) for h in range(j * GROUP, (j + 1) * GROUP)]


def attend_kernel(scal_ref, q_ref, far_ref, near_ref, own_ref, next_ref, mixed_ref, lse_ref, window):
    sub = pl.program_id(0)

    @pl.when(sub == 0)
    def _():
        load_window(window, (far_ref, near_ref, own_ref, next_ref))

    bias = bias_of(scal_ref, scal_ref[0, 4] + sub * GRAIN, True)
    bias = jnp.concatenate([bias] * GROUP, axis=0)
    rows = pl.ds(pl.multiple_of(sub * GRAIN, GRAIN), SPAN)
    lse = jnp.zeros((GRAIN, 128), F32)
    lane = lax.broadcasted_iota(jnp.int32, (GRAIN, 128), 1)
    for j in range(KVH):
        key = window[rows, j * HD : (j + 1) * HD]
        value = window[rows, KW + j * HD : KW + (j + 1) * HD]
        query = jnp.concatenate([q_ref[:, c] for c in head_columns(j)], axis=0)
        scores = nt(query, key) + bias
        top = jnp.max(scores, axis=-1, keepdims=True)
        raised = jnp.exp(scores - top)
        total = jnp.sum(raised, axis=-1, keepdims=True)
        out = nn(raised.astype(BF16), value) / total
        logsum = top + jnp.log(total)
        for g, c in enumerate(head_columns(j)):
            at = slice(g * GRAIN, (g + 1) * GRAIN)
            mixed_ref[:, c] = out[at].astype(BF16)
            lse = jnp.where(lane == j * GROUP + g, logsum[at], lse)
    lse_ref[...] = lse


def window_parts(windows, seq, rows):
    far, near, own, ahead = windows
    parts = [rows_at(a, seq, rows) for a in (far, near, own)]
    return (*parts, rows_at(ahead, seq, GRAIN))


def sub_rows(array, seq, rows):
    first = seq * (rows // GRAIN)
    return array, pl.BlockSpec((GRAIN, array.shape[1]), lambda i: (first + i, 0))


def attend(scal, q, seq, rows, windows):
    return call(
        attend_kernel,
        [rows_each(struct((rows, w), t), GRAIN) for w, t in ((QW, BF16), (128, F32))],
        (scal, sub_rows(q, seq, rows), *window_parts(windows, seq, rows)),
        grid=(rows // GRAIN,),
        scratch=[pltpu.VMEM((MAXDOC + rows + GRAIN, 2 * KW), BF16)],
        us=6.8,
    )


def attend_back_kernel(
    earlier,
    scal_ref,
    q_ref,
    far_ref,
    near_ref,
    own_ref,
    next_ref,
    mixed_ref,
    lse_ref,
    grad_ref,
    cos_ref,
    sin_ref,
    *refs,
):
    dq_ref, dfar_ref, dnear_ref, down_ref, dnext_ref, window, sums, qs = refs[earlier:]
    sub = pl.program_id(0)

    @pl.when(sub == 0)
    def _():
        load_window(window, (far_ref, near_ref, own_ref, next_ref))
        sums[...] = jnp.zeros_like(sums)

    bias = bias_of(scal_ref, scal_ref[0, 4] + sub * GRAIN, False)
    bias = jnp.concatenate([bias] * GROUP, axis=1)
    rows = pl.ds(pl.multiple_of(sub * GRAIN, GRAIN), SPAN)
    lane = lax.broadcasted_iota(jnp.int32, (GRAIN, 128), 1)
    product = mixed_ref[...].astype(F32) * grad_ref[...].astype(F32)
    delta = jnp.zeros((GRAIN, 128), F32)
    for h in range(H):
        share = jnp.sum(product[:, h * HD : (h + 1) * HD], axis=-1, keepdims=True)
        delta = jnp.where(lane == h, share, delta)
    delta = delta.T
    lse = lse_ref[...].T

    def heads(array, j):
        return jnp.concatenate([array[h : h + 1] for h in range(j * GROUP, (j + 1) * GROUP)], axis=1)

    for j in range(KVH):
        k_cols = slice(j * HD, (j + 1) * HD)
        v_cols = slice(KW + j * HD, KW + (j + 1) * HD)
        key, value = window[rows, k_cols], window[rows, v_cols]
        query = jnp.concatenate([q_ref[:, c] for c in head_columns(j)], axis=0)
        grad = jnp.concatenate([grad_ref[:, c] for c in head_columns(j)], axis=0)
        probs = jnp.exp(nt(key, query) + bias - heads(lse, j))
        grad_scores = (probs * (nt(value, grad) - heads(delta, j))).astype(BF16)
        sums[rows, v_cols] += nn(probs.astype(BF16), grad)
        sums[rows, k_cols] += nn(grad_scores, query)
        dq = tn(key, grad_scores).T
        for g, c in enumerate(head_columns(j)):
            qs[:, c] = dq[g * GRAIN : (g + 1) * GRAIN, :]
    rotate_into(dq_ref, qs, QW, cos_ref[...], -sin_ref[...], HD**-0.5)

    @pl.when(sub == pl.num_programs(0) - 1)
    def _():
        row = 0
        for part in (dfar_ref, dnear_ref, down_ref):
            part[...] = sums[row : row + part.shape[0], :].astype(part.dtype)
            row += part.shape[0]
        done = dnext_ref.shape[0] - GRAIN
        if earlier:
            dnext_ref[:done, :] = refs[0][...]
        dnext_ref[done:, :] = sums[row:, :].astype(BF16)


def attend_back(scal, q, seq, rows, windows, mixed, lse, grad, cosine, sine, earlier):
    window = MAXDOC + rows + GRAIN
    each = lambda a: rows_each(a, GRAIN)
    shapes = ((rows, BF16), (rows, BF16), (rows, F32), ((seq + 1) * GRAIN, BF16))
    return call(
        functools.partial(attend_back_kernel, len(earlier)),
        [each(struct((rows, QW), BF16)), *(struct((r, 2 * KW), t) for r, t in shapes)],
        (
            scal,
            sub_rows(q, seq, rows),
            *window_parts(windows, seq, rows),
            *map(each, (mixed, lse, grad, cosine, sine)),
            *earlier,
        ),
        grid=(rows // GRAIN,),
        scratch=[
            pltpu.VMEM((window, 2 * KW), BF16),
            pltpu.VMEM((window, 2 * KW), F32),
            pltpu.VMEM((GRAIN, wide(QW)), F32),
        ],
        us=0.05 if earlier else 11.7,
    )


def ff_kernel(nrm_a, nrm_b, cot_a, cot_b, w_ref, inner_ref, gg_ref, gu_ref, sum_a, sum_b):
    first = pl.program_id(0) == 0
    (rows, units), width = inner_ref.shape, w_ref.shape[0]
    wg, wu, wd = (w_ref[:, k * units : (k + 1) * units] for k in range(3))
    normed = jnp.where(first, nrm_a[...], nrm_b[...])
    gate = nn(normed, wg)
    up = nn(normed, wu)
    grad = nn(jnp.where(first, cot_a[:, :width], cot_b[:, :width]), wd)
    sigma = jax.nn.sigmoid(gate)
    raised = gate * sigma
    inner = (raised * up).astype(BF16)
    grad_gate = (grad * up * (sigma + raised * (1.0 - sigma))).astype(BF16)
    grad_up = (grad * raised).astype(BF16)
    inner_ref[...] = inner
    gg_ref[...] = grad_gate
    gu_ref[...] = grad_up
    grad_normed = (nt(grad_gate, wg) + nt(grad_up, wu)).astype(BF16)
    out = nt(inner, wd).astype(BF16)

    @pl.when(first)
    def _():
        sum_a[:rows, :width] = grad_normed
        sum_a[rows:, :width] = out

    @pl.when(jnp.logical_not(first))
    def _():
        sum_b[:rows, :width] = grad_normed
        sum_b[rows:, :width] = out


def ff(normed_pair, cot_pair, weights, seq):
    rows, width = normed_pair[0].shape
    units = weights.shape[1] // 3
    unit = lambda: rows_each(struct((2 * rows, units), BF16), rows)
    result = call(
        ff_kernel,
        [unit(), unit(), unit()] + [struct((2 * rows, wide(width)), BF16)] * 2,
        (*normed_pair, *(rows_at(c, seq, rows) for c in cot_pair), weights),
        grid=(2,),
        us=7.2,
    )
    return result[:3], result[3:]


def outer_kernel(counts, split, place_ref, *refs):
    acc = refs[-1]
    column = 0
    for lefts, rights, gains in counts:
        left_refs, refs = refs[:lefts], refs[lefts:]
        right_refs, refs = refs[:rights], refs[rights:]
        gain_refs, refs = refs[:gains], refs[gains:]
        width = right_refs[0].shape[-1]
        at = slice(column, column + width)
        join = lambda some, w: jnp.concatenate([r[:, :w] for r in some], axis=0)
        if lefts % rights:
            groups = [(left_refs, right_refs)]
        else:
            per = lefts // rights
            groups = [(left_refs[i * per : (i + 1) * per], [r]) for i, r in enumerate(right_refs)]
        for i, (some_left, some_right) in enumerate(groups):
            product = tn(join(some_left, acc.shape[0]), join(some_right, width))
            if i == 0:
                acc[:, at] = product
            else:
                acc[:, at] += product
        column += width
        if gains:
            total = functools.reduce(jnp.add, [g[...] for g in gain_refs])
            across = jnp.broadcast_to(total, (128, total.shape[1])).T
            stop = wide(column)
            acc[:, column:stop] = across[:, : stop - column]
            column = stop
    outs = refs[:-1]
    if split is None:
        outs[0][...] = acc[...]
        return
    keep_ref, send_ref = outs
    half = keep_ref.shape[0] if split == "shard" else keep_ref.shape[0] // 2
    for s in range(acc.shape[0] // (2 * half)):
        rows = slice(s * half, (s + 1) * half)
        keep_ref[rows, :] = acc[pl.ds(pl.multiple_of(2 * s * half + place_ref[0], 16), half), :]
        other = pl.ds(pl.multiple_of((2 * s + 1) * half - place_ref[0], 16), half)
        send_ref[rows, :] = acc[other, :].astype(BF16)


def outer(products, width, place, split, us, limit=VMEM_LIMIT):
    array = lambda operand: operand[0] if isinstance(operand, tuple) else operand
    full = 0
    for _, rights, gains in products:
        full += array(rights[0]).shape[1]
        full = wide(full) if gains else full
    if split is None:
        outs = [struct((width, full), F32)]
    else:
        outs = [struct((width // 2, full), F32), struct((width // 2, full), BF16)]
    args = [a for product in products for group in product for a in group]
    return call(
        functools.partial(outer_kernel, [tuple(map(len, p)) for p in products], split),
        outs,
        (place, *args),
        scratch=[pltpu.VMEM((width, full), F32)],
        us=us,
        limit=limit,
    )


def output_kernel(hidden_ref, *refs):
    total = hidden_ref[...]
    for term in refs[:-1]:
        total += term[:, : total.shape[1]].astype(F32)
    refs[-1][...] = total.T.astype(BF16)


def output_of(hidden, terms):
    rows, width = hidden.shape
    return call(output_kernel, [struct((width, rows), BF16)], (hidden, *terms), us=1.4)[0]


def ff_back_kernel(
    hidden_ref, cot_ref, a_ref, b_ref, c_ref, gain_ref, wo_ref, gh_ref, gb_ref, gm_ref, gg_ref
):
    hidden, gain = hidden_ref[...], gain_ref[...]
    factor = inverse_mean(hidden)
    width = hidden.shape[1]
    grad = sum(ref[:, :width].astype(F32) for ref in (a_ref, b_ref, c_ref))
    weighted = grad * gain
    back = factor * weighted - hidden * factor**3 * jnp.mean(
        hidden * weighted, axis=-1, keepdims=True
    )
    grad_hidden = cot_ref[:, :width].astype(F32) + back
    branch = grad_hidden.astype(BF16)
    gh_ref[...] = grad_hidden
    gb_ref[...] = branch
    gm_ref[...] = nt(branch, wo_ref[...]).astype(BF16)
    gg_ref[...] = jnp.sum(grad * hidden * factor, axis=0, keepdims=True)


def ff_back(hidden, cotangent, seq, terms, gain, wo):
    rows, width = hidden.shape
    outs = [
        struct((rows, width), F32),
        struct((rows, width), BF16),
        struct((rows, QW), BF16),
        struct((1, width), F32),
    ]
    return call(
        ff_back_kernel,
        outs,
        (hidden, rows_at(cotangent, seq, rows), *terms, gain, wo),
        us=0.05,
    )


def input_kernel(
    tok_ref,
    gh_ref,
    gq_ref,
    own_ref,
    left_ref,
    right_ref,
    gain_ref,
    wq_ref,
    wkv_ref,
    cos_ref,
    sin_ref,
    ig_ref,
    gkv_ref,
    ks,
):
    ks[...] = own_ref[...] + right_ref[...].astype(F32)
    ks[:GRAIN, :] += left_ref[...].astype(F32)
    gkv_ref[:, KW:] = ks[:, KW:].astype(BF16)
    rotate_into(gkv_ref, ks, KW, cos_ref[...], -sin_ref[...], 1.0)
    grad = nt(gq_ref[...], wq_ref[...]) + nt(gkv_ref[...], wkv_ref[...])
    source, gain = tok_ref[:, : gh_ref.shape[1]].astype(F32), gain_ref[...]
    factor = inverse_mean(source)
    weighted = grad * gain
    back = factor * weighted - source * factor**3 * jnp.mean(
        source * weighted, axis=-1, keepdims=True
    )
    ig_ref[...] = (gh_ref[...] + back).T


def input_back(tokens, seq, args):
    rows, width = args[0].shape
    return call(
        input_kernel,
        [struct((width, rows), F32), struct((rows, 2 * KW), BF16)],
        (rows_at(tokens, seq, rows), *args),
        scratch=[pltpu.VMEM((rows, 2 * KW), F32)],
        us=0.05,
    )


def add_kernel(*refs):
    total = refs[0][...].astype(F32)
    for ref in refs[1:-1]:
        total += ref[...].astype(F32)
    refs[-1][...] = total.astype(refs[-1].dtype)


def add_up(terms, shape, dtype, us=0.7):
    return call(add_kernel, [struct(shape, dtype)], terms, us=us)[0]


def side_kernel(*refs):
    width = refs[0].shape[1]
    for i, ref in enumerate(refs[:-1]):
        refs[-1][:, i * width : (i + 1) * width] = ref[...]


def side_by_side(*arrays):
    rows, width = arrays[0].shape
    return call(side_kernel, [struct((rows, len(arrays) * width), BF16)], arrays, us=0.8)[0]


def widen_kernel(all_ref, *outs):
    units = outs[0].shape[1]
    for i, out in enumerate(outs):
        out[...] = all_ref[:, i * units : (i + 1) * units].astype(F32)


def widen(value):
    rows, columns = value.shape
    return call(widen_kernel, [struct((rows, columns // 3), F32)] * 3, (value,), us=2.0)


def beside_kernel(left_ref, keep_ref, got_ref, out_ref):
    columns = left_ref.shape[1]
    out_ref[:, :columns] = left_ref[...]
    out_ref[:, columns:] = (keep_ref[...] + got_ref[...].astype(F32)).astype(BF16)


def set_beside(left, keep, got):
    shape = (left.shape[0], left.shape[1] + keep.shape[1])
    return call(beside_kernel, [struct(shape, BF16)], (left, keep, got), us=1.5)[0]


def pair_kernel(*refs):
    out = refs[-1]
    rows = refs[0].shape[0]
    for s in range(len(refs) // 2):
        total = refs[2 * s][...].astype(F32) + refs[2 * s + 1][...].astype(F32)
        out[s * rows : (s + 1) * rows, :] = total.astype(BF16)


def split_kernel(at_ref, keep_ref, got_ref, kept_ref, sent_ref, total):
    total[...] = keep_ref[...].astype(F32) + got_ref[...].astype(F32)
    half = kept_ref.shape[0]
    kept_ref[...] = total[pl.ds(pl.multiple_of(at_ref[0] * half, 8), half), :]
    sent_ref[...] = total[pl.ds(pl.multiple_of((1 - at_ref[0]) * half, 8), half), :].astype(BF16)


def split_sum(at, keep, got):
    shape = (keep.shape[0] // 2, keep.shape[1])
    return call(
        split_kernel,
        [struct(shape, F32), struct(shape, BF16)],
        (at, keep, got),
        scratch=[pltpu.VMEM(keep.shape, F32)],
        us=0.05,
    )


def put_halves(both, at_ref, own_ref, got_ref):
    half = own_ref.shape[0]
    if half == both.shape[0]:
        both[...] = own_ref[...].astype(F32)
        return
    for place, ref in ((at_ref[0], own_ref), (1 - at_ref[0], got_ref)):
        both[pl.ds(pl.multiple_of(place * half, 8), half), :] = ref[...].astype(F32)


def join_kernel(at_ref, own_ref, got_ref, out_ref, both):
    put_halves(both, at_ref, own_ref, got_ref)
    out_ref[...] = both[...].astype(out_ref.dtype)


def join_rows(at, own, got):
    shape = (2 * own.shape[0], own.shape[1])
    return call(
        join_kernel,
        [struct(shape, BF16)],
        (at, own, got),
        scratch=[pltpu.VMEM(shape, F32)],
        us=0.9,
    )[0]


def as_row(column):
    return jnp.broadcast_to(column, (column.shape[0], 128)).T[:1]


def finish_pair_kernel(at_ref, own_ref, got_ref, w_ref, out_ref, gain_ref, query_ref, sum_ref, both):
    put_halves(both, at_ref, own_ref, got_ref)
    width = out_ref.shape[1]
    out_ref[...] = both[:, :width]
    gain_ref[...] = as_row(both[:, width : width + 1])
    query = both[:, both.shape[1] - QW :]
    query_ref[...] = query
    sum_ref[...] = as_row(jnp.sum(query * w_ref[...].astype(F32), axis=-1, keepdims=True))


def finish_pair(at, own, got, weight, width):
    rows = weight.shape[0]
    return call(
        finish_pair_kernel,
        [struct(s, F32) for s in ((rows, width), (1, rows), (rows, QW), (1, rows))],
        (at, own, got, weight),
        scratch=[pltpu.VMEM((rows, own.shape[1]), F32)],
        us=1.5,
    )


def finish_kv_kernel(at_ref, own_ref, got_ref, w_ref, sum_ref, gain_ref, k_ref, v_ref, grad_ref, both):
    put_halves(both, at_ref, own_ref, got_ref)
    k_ref[...] = both[:, :KW].T
    v_ref[...] = both[:, KW:].T
    rest = as_row(jnp.sum(both[...] * w_ref[...].astype(F32), axis=-1, keepdims=True))
    grad_ref[...] = (sum_ref[...] + rest) / gain_ref[...]


def finish_kv(at, own, got, weight, sums, gain):
    rows = weight.shape[0]
    return call(
        finish_kv_kernel,
        [struct(s, F32) for s in ((KW, rows), (KW, rows), (1, rows))],
        (at, own, got, weight, sums, gain),
        scratch=[pltpu.VMEM((rows, own.shape[1]), F32)],
        us=1.5,
    )


def program(mesh):
    shards, ctxs = mesh.shape["shard"], mesh.shape["ctx"]

    def swap(value, axis, bit):
        count = mesh.shape[axis]
        return lax.ppermute(value, axis, [(i, i ^ bit) for i in range(count)])

    def shift(value, by):
        pairs = [(i, i + by) for i in range(ctxs) if 0 <= i + by < ctxs]
        return lax.ppermute(value, "ctx", pairs)

    def place_of(index):
        return index.astype(jnp.int32)[None]

    def over_shard(terms):
        return lax.psum_scatter(terms[0], "shard", scatter_dimension=0, tiled=True)

    def reduce_units(terms, finish):
        if shards != 2:
            return finish(over_shard(terms), None)
        keep, send = terms
        got = swap(send, "shard", 1)
        yield got
        return finish(keep, got)

    def all_over_ctx(value):
        part = lax.psum_scatter(value, "ctx", scatter_dimension=0, tiled=True)
        return lax.all_gather(part, "ctx", axis=0, tiled=True)

    def reduce_attention(terms, finish):
        zero = jnp.zeros((1,), jnp.int32)
        if shards != 2:
            total = lax.psum(over_shard(terms), ("ctx", "tp"))
            return finish(zero, total, total)
        tp = lax.axis_index("tp")
        mine, core, row = map(place_of, (lax.axis_index("shard"), tp % 2, tp // 2))
        held, low = terms
        got = swap(low, "tp", 1)
        yield got
        held, low = split_sum(mine, held, got)
        got = swap(low, "shard", 1)
        yield got
        held, low = split_sum(row, held, got)
        got = swap(low, "tp", 2)
        yield got
        low = add_up((held, got), held.shape, BF16)
        bit = 1
        while bit < ctxs:
            got = swap(low, "ctx", bit)
            yield got
            low = add_up((low, got), low.shape, BF16)
            bit *= 2
        got = swap(low, "tp", 2)
        yield got
        low = join_rows(row, low, got)
        got = swap(low, "tp", 1)
        yield got
        return finish(core, low, got)

    def per_device(
        tokens,
        cotangent,
        piece_starts,
        doc_lengths,
        attn_gain,
        w_query,
        w_key,
        w_value,
        w_out,
        ff_gain,
        w_gate,
        w_up,
        w_down,
    ):
        Order.last, Order.awaited = None, ()
        seqs, rows, width = tokens.shape
        offset = (lax.axis_index("ctx") * rows).astype(jnp.int32)
        mine, tp = lax.axis_index("shard"), lax.axis_index("tp")
        core, row = tp % 2, tp // 2
        every = range(seqs)
        last = seqs - 1

        (tokens,) = prepare(tokens.transpose(0, 2, 1))
        cosine, sine = rotary_tables(offset, rows)
        ends = jnp.cumsum(doc_lengths, axis=1)[:, :-1]
        scal = jnp.concatenate(
            [ends, piece_starts, jnp.broadcast_to(offset, (seqs, 1))], axis=1
        ).astype(jnp.int32)
        scals = [scal[s : s + 1] for s in every]

        w_kv = jnp.concatenate([w_key, w_value], axis=1)
        gains = jnp.stack([attn_gain, ff_gain])
        if shards == 2:
            full = w_query.shape[0]
            half = full // 2
            span = -(-half // 32) * 16
            other = (1 - mine) * full
            near_rows, far_rows = other + core * half, other + (1 - core) * half
            step, back = row * (half - span), (1 - row) * (half - span)
            kv_places = jnp.stack([mine * full, near_rows, far_rows]).astype(jnp.int32)
            places = [near_rows + step, near_rows + back, far_rows + step, far_rows + back]
            places = jnp.stack([mine * full, *places]).astype(jnp.int32)
            quarter = lambda w: lax.dynamic_slice_in_dim(w, core * half + step, span)

            got = swap(gains, "shard", 1)
            all_gains = jnp.where(
                mine == 0,
                jnp.concatenate([gains, got], axis=1),
                jnp.concatenate([got, gains], axis=1),
            )
            kv_part = swap(lax.dynamic_slice_in_dim(w_kv, core * half, half), "shard", 1)
            kv_beside = swap(in_turn(kv_part), "tp", 1)
            kv_pieces = [(w_kv, 0, full), (kv_part, 0, half), (kv_beside, 0, half)]
            two = jnp.concatenate([quarter(w_query), quarter(w_out)], axis=0)
            two_x = swap(after(two, kv_part), "shard", 1)
        else:
            gather = lambda w: lax.all_gather(w, "shard", axis=0, tiled=True)
            kv_places = places = jnp.zeros((1,), jnp.int32)
            all_gains = lax.all_gather(gains, "shard", axis=1, tiled=True)
            kv_pieces = [(gather(w_kv), 0, width)]
        gain_one, gain_two = all_gains[:1].astype(F32), all_gains[1:].astype(F32)

        (normed_one, kv, first), kv_pieces = project_kv(
            tokens, seqs, gain_one, cosine, sine, kv_pieces, kv_places
        )
        wkv = kv_pieces[0][0]
        near, ahead = shift(kv, 1), shift(first, -1)
        if shards == 2:
            arrive(two_x)
        ff_weights = lax.all_gather(side_by_side(w_gate, w_up, w_down), "shard", axis=0, tiled=True)
        if shards == 2:
            two_y, two_beside = swap(two_x, "tp", 2), swap(two_x, "tp", 1)
            arrive(two_beside)
        arrive(near, ahead)
        (cotangent,) = prepare(cotangent.transpose(0, 2, 1))
        windows = (shift(in_turn(near), 1), near, kv, ahead)
        if shards == 2:
            two_y = in_turn(two_y)
            parts = (two_x, two_y, two_beside, swap(two_y, "tp", 1))
            q_pieces = [(w_query, 0, full), *((p, 0, span) for p in parts)]
            out_pieces = [(w_out, 0, full), *((p, span, span) for p in parts)]
        else:
            q_pieces, out_pieces = ([(gather(w), 0, width)] for w in (w_query, w_out))
            two_y = w_query
        cot_y = swap(after(cotangent, two_y), "tp", 2)
        (query,), q_pieces = project_q(normed_one, seqs, cosine, sine, q_pieces, places)
        wq = q_pieces[0][0]
        cot_core = swap(in_turn(cotangent), "tp", 1)

        mixed, lse, hidden, normed_rows = [], [], [], []
        for s in every:
            if s == 1:
                cot_y = in_turn(cot_y)
                cot_diagonal = swap(cot_y, "tp", 1)
            m, l = attend(scals[s], query, s, rows, windows)
            if s == 0:
                arrive(cot_core)
            else:
                arrive(normed_rows[-1][1])
            if s == 1:
                arrive(cot_diagonal)
            (h, own), out_pieces = residual(tokens, s, m, gain_two, out_pieces, places)
            normed_rows.append((own, swap(own, "tp", 1), swap(own, "tp", 2)))
            mixed.append(m)
            lse.append(l)
            hidden.append(h)
        wo = out_pieces[0][0]
        if seqs == 1:
            cot_diagonal = swap(cot_y, "tp", 1)
        cots = (cotangent, cot_core, cot_y, cot_diagonal)

        row_blocks, units, near_sums, far_sums = [], [], [], []
        grad_at = lambda a: rows_at(a, 0, rows)
        out_at = lambda a: rows_at(a, 1, rows)

        def cross_grad(s):
            partial = add_up([grad_at(a) for a in far_sums[s]], (rows, wide(width)), BF16)
            return (*map(grad_at, near_sums[s]), swap(partial, "tp", 2))

        grad_terms = []
        for s in every:
            own, beside, facing = normed_rows[s]
            diagonal = swap(in_turn(facing), "tp", 1)
            if s > 0:
                arrive(near_sums[s - 1][1])
            unit, (a, b) = ff((own, beside), cots[:2], ff_weights, s)
            near_sums.append((a, swap(b, "tp", 1)))
            units.append(unit)
            if s > 0:
                grad_terms.append(cross_grad(s - 1))
            arrive(*(n[1] for n in normed_rows[s + 1 : s + 2]))
            unit, (a, b) = ff((facing, diagonal), cots[2:], ff_weights, s)
            far_sums.append((a, swap(b, "tp", 1)))
            units.append(unit)
            row_blocks += [own, beside, facing, diagonal]

        by_shard, by_core = ("shard", "core") if shards == 2 else (None, None)
        shard_place, core_place = place_of(mine * (width // 2)), place_of(core * (width // 4))
        cot_lefts = [rows_at(c, s, rows) for s in every for c in cots]

        def unit_product(lefts, k):
            return lefts, [u[k] for u in units], ()

        arrive(near_sums[last][1])
        def down_sum(keep, got):
            if got is None:
                return keep.astype(BF16)
            return add_up((keep, got), keep.shape, BF16, 0.05)

        def units_sum(keep, got):
            left = down.finish()
            if got is None:
                return jnp.concatenate([left, keep.astype(BF16)], axis=1)
            return set_beside(left, keep, got)

        down_grad = outer([unit_product(cot_lefts, 0)], width, shard_place, by_shard, 5.0)
        down = Chain(reduce_units(down_grad, down_sum))
        grad_terms.append(cross_grad(last))
        both = [unit_product(row_blocks, 1), unit_product(row_blocks, 2)]
        arrive(*(t[2] for t in grad_terms[:-1]))
        gate_up_grad = outer(both, width, shard_place, by_shard, 10.0, 2 * VMEM_LIMIT)
        gate_up = Chain(reduce_units(gate_up_grad, units_sum))
        out_terms = [out_at(a) for s in every for a in far_sums[s]]
        out_partial = call(
            pair_kernel, [struct((seqs * rows, wide(width)), BF16)], out_terms, us=0.05
        )[0]
        outs_got = swap(after(out_partial, grad_terms[last][2]), "tp", 2)

        branch, gain_two_grad, grad_hidden = [], [], []
        backs, input_grads, gkv = [], [], []
        ahead_grads = ()

        def mixed_back(s, ahead_grads):
            gh, gb, gm, gg = ff_back(hidden[s], cotangent, s, grad_terms[s], gain_two, wo)
            grad_hidden.append(gh)
            branch.append(gb)
            gain_two_grad.append(gg)
            if s == 0:
                down.step()
            dq, dfar, dnear, own, dnext = attend_back(
                scals[s], query, s, rows, windows, mixed[s], lse[s], gm, cosine, sine, ahead_grads
            )
            backs.append((dq, dnear, own, shift(dfar, -1)))
            return (dnext,)

        def pass_on(s):
            dq, dnear, own, passed = backs[s]
            backs[s] = dq, own, shift(add_up((dnear, passed), dnear.shape, BF16, 0.05), -1)

        def rows_back(s):
            dq, own, right = backs[s]
            args = (grad_hidden[s], dq, own, rows_at(left, s, GRAIN), right)
            args += (gain_one, wq, wkv, cosine, sine)
            input_grad, g = input_back(tokens, s, args)
            input_grads.append(input_grad)
            gkv.append(g)

        for s in every:
            ahead_grads = mixed_back(s, ahead_grads)
        left = shift(ahead_grads[0], 1)
        for s in every[:-1]:
            pass_on(s)
        arrive(outs_got)
        gate_up.step()
        unit_sums = all_over_ctx(gate_up.finish())
        pass_on(last)
        grads = [b[0] for b in backs]
        pair = Chain(
            reduce_attention(
                outer(
                    [(mixed, branch, gain_two_grad), ([normed_one], grads, ())],
                    width,
                    core_place,
                    by_core,
                    2.7,
                    2 * VMEM_LIMIT,
                ),
                lambda at, own, got: finish_pair(at, own, got, w_query, width),
            )
        )
        outputs = []
        for s in every:
            near_terms = [out_at(a) for a in near_sums[s]]
            outputs.append(output_of(hidden[s], (*near_terms, rows_at(outs_got, s, rows))))
        pair.step()
        for s in every:
            rows_back(s)
        finish_last = lambda at, own, got: (at, own, got)
        keys = Chain(
            reduce_attention(
                outer([([normed_one], gkv, ())], width, core_place, by_core, 0.05), finish_last
            )
        )
        for chain in (keys, pair, keys, pair, keys, pair, keys, pair, keys):
            chain.step()
        sum_down, sum_gate, sum_up = widen(unit_sums)
        for chain in (pair, keys):
            chain.step()
        sum_out, sum_gain_two, sum_query, products = pair.finish()
        keys_done = keys.finish()
        sum_key, sum_value, sum_gain_one = finish_kv(
            *keys_done, w_kv, products, gains[:1].astype(F32)
        )
        join = lambda blocks: jnp.stack(blocks).transpose(0, 2, 1)
        return (
            join(outputs),
            join(input_grads),
            sum_gain_one[0],
            sum_query,
            sum_key.T,
            sum_value.T,
            sum_out,
            sum_gain_two[0],
            sum_gate,
            sum_up,
            sum_down,
        )

    return per_device


def solution(mesh):
    rows = P(("shard", "tp"), "ctx", None)
    seq = P(("shard", "tp"), None)
    gain, weight, ff_weight = P("shard"), P("shard", None), P("shard", "tp")
    weights = (gain, weight, weight, weight, weight, gain, ff_weight, ff_weight, ff_weight)
    return jax.shard_map(
        program(mesh),
        mesh=mesh,
        in_specs=(rows, rows, seq, seq, *weights),
        out_specs=(rows, rows, *weights),
        check_vma=False,
    )
```

```python
import functools
import math

import jax
import jax.numpy as jnp
from jax import lax
from jax.experimental import pallas as pl
from jax.experimental.pallas import tpu as pltpu
from jax.sharding import PartitionSpec as P

H = 15
KVH = 5
HD = 64
LEN = 1024
PIECE = 256
GRAIN = 128
MAXDOC = 512
GROUP = H // KVH
KW = KVH * HD
QW = H * HD
SPAN = MAXDOC + 2 * GRAIN

EPS = 1e-05
NEG = -1e30
F32 = jnp.float32
BF16 = jnp.bfloat16
VMEM_LIMIT = 20 * 1024 * 1024
SCALE = 10.0
FLOPS_PER_US = 1.15e9


def dot(left, right, dims):
    return lax.dot_general(left, right, (dims, ((), ())), preferred_element_type=F32)


def nn(left, right):
    return dot(left, right, ((1,), (0,)))


def nt(left, right):
    return dot(left, right, ((1,), (1,)))


def tn(left, right):
    return dot(left, right, ((0,), (0,)))


def wide(width):
    return -(-width // 128) * 128


class Order:
    last = None
    awaited = ()


def arrive(*values):
    Order.awaited += values


def after(value, *deps):
    return lax.optimization_barrier((value, deps))[0] if deps else value


def in_turn(value):
    return value if Order.last is None else after(value, *Order.last)


def struct(shape, dtype):
    return jax.ShapeDtypeStruct(shape, dtype)


def rows_at(array, index, count):
    return array, pl.BlockSpec((count, array.shape[1]), lambda *_: (index, 0))


def rows_each(array, count):
    return array, pl.BlockSpec((count, array.shape[1]), lambda i: (i, 0))


def call(kernel, outs, args, *, us, grid=(1,), scratch=(), limit=VMEM_LIMIT):
    def split(operands):
        arrays, specs = [], []
        for operand in operands:
            if isinstance(operand, tuple):
                array, spec = operand
            elif operand.dtype == jnp.int32:
                array, spec = operand, pl.BlockSpec(memory_space=pltpu.SMEM)
            else:
                array = operand
                spec = pl.BlockSpec(array.shape, lambda *_, n=len(array.shape): (0,) * n)
            arrays.append(array)
            specs.append(spec)
        return arrays, specs

    arrays, in_specs = split(args)
    shapes, out_specs = split(outs)
    first = next(i for i, a in enumerate(arrays) if a.dtype != jnp.int32)
    arrays[first] = after(arrays[first], *(Order.last or ()), *Order.awaited)
    Order.awaited = ()
    result = pl.pallas_call(
        kernel,
        out_shape=shapes,
        grid=grid,
        in_specs=in_specs,
        out_specs=out_specs,
        scratch_shapes=list(scratch),
        compiler_params=pltpu.CompilerParams(vmem_limit_bytes=limit),
        cost_estimate=pl.CostEstimate(
            flops=int(us * SCALE * FLOPS_PER_US), bytes_accessed=0, transcendentals=0
        ),
    )(*arrays)
    Order.last = (result[0],)
    return result


class Chain:
    def __init__(self, steps):
        self.steps, self.result = steps, None
        self.step()

    def step(self):
        if self.result is None:
            try:
                self.got = next(self.steps)
            except StopIteration as stop:
                self.result = stop.value

    def finish(self):
        while self.result is None:
            self.step()
        return self.result


def rotary_tables(offset, length):
    half = HD // 2
    place = (offset + jnp.arange(length, dtype=jnp.int32)).astype(F32)
    freq = jnp.exp(jnp.arange(half).astype(F32) * (-2.0 * math.log(10000.0) / HD))
    angle = place[:, None] * freq[None, :]
    cosine, sine = jnp.cos(angle), jnp.sin(angle)
    return (
        jnp.concatenate([cosine] * 4, axis=1),
        jnp.concatenate([-sine, sine, -sine, sine], axis=1),
    )


def rotate(tile, cosine, sine):
    lane = lax.broadcasted_iota(jnp.int32, tile.shape, 1)
    partner = jnp.where(lane % HD < HD // 2, pltpu.roll(tile, 96, 1), pltpu.roll(tile, 32, 1))
    return tile * cosine + partner * sine


def rotate_into(out_ref, value_ref, width, cosine, sine, factor):
    for start in range(0, width, 128):
        stop = min(start + 128, width)
        turned = rotate(value_ref[:, start : start + 128], cosine, sine) * factor
        out_ref[:, start:stop] = turned[:, : stop - start].astype(out_ref.dtype)


def inverse_mean(value):
    return lax.rsqrt(jnp.mean(value * value, axis=-1, keepdims=True) + EPS)


def prepare_kernel(*refs):
    count = len(refs) // 2
    for source, out in zip(refs[:count], refs[count:]):
        seqs, _, rows = source.shape
        for s in range(seqs):
            out[s * rows : (s + 1) * rows, : source.shape[1]] = source[s].T


def prepare(*arrays):
    outs = [struct((a.shape[0] * a.shape[2], wide(a.shape[1])), a.dtype) for a in arrays]
    return call(prepare_kernel, outs, arrays, us=0.8)


def weight_kernel(kernel, ins, outs, pieces, place_ref, *refs):
    args, parts, rest = refs[:ins], refs[ins : ins + len(pieces)], refs[ins + len(pieces) :]
    if len(pieces) == 1:
        kernel(*args, parts[0], *rest)
        return
    w_ref = rest[outs]

    @pl.when(pl.program_id(0) == 0)
    def _():
        for i, ((start, count), part) in enumerate(zip(pieces, parts)):
            rows = pl.ds(pl.multiple_of(place_ref[i], 16), count)
            w_ref[rows, :] = part[start : start + count, :]

    kernel(*args, w_ref, *rest[:outs], *rest[outs + 1 :])


def with_weight(kernel, outs, args, pieces, places, **kw):
    counts = [(start, count) for _, start, count in pieces]
    arrays = [a for a, _, _ in pieces]
    made = list(outs)
    if len(pieces) > 1:
        made.append(struct((2 * pieces[0][2], arrays[0].shape[1]), arrays[0].dtype))
    body = functools.partial(weight_kernel, kernel, len(args), len(outs), counts)
    result = call(body, made, (places, *args, *arrays), **kw)
    weight = result[-1] if len(pieces) > 1 else arrays[0]
    return result[: len(outs)], [(weight, 0, weight.shape[0])]


def kv_kernel(tok_ref, gain_ref, cos_ref, sin_ref, w_ref, normed_ref, kv_ref, first_ref, ks):
    source = tok_ref[:, : normed_ref.shape[1]].astype(F32)
    normed = (source * inverse_mean(source) * gain_ref[...]).astype(BF16)
    normed_ref[...] = normed
    raw = nn(normed, w_ref[...])
    ks[:, :KW] = raw[:, :KW]
    kv_ref[:, KW:] = raw[:, KW:].astype(BF16)
    rotate_into(kv_ref, ks, KW, cos_ref[...], sin_ref[...], 1.0)
    first_ref[...] = kv_ref[:GRAIN, :]


def project_kv(tokens, seqs, gain, cosine, sine, pieces, places):
    total, width = tokens.shape[0], gain.shape[1]
    rows = total // seqs
    outs = [
        rows_each(struct((total, width), BF16), rows),
        rows_each(struct((total, 2 * KW), BF16), rows),
        rows_each(struct((seqs * GRAIN, 2 * KW), BF16), GRAIN),
    ]
    return with_weight(
        kv_kernel,
        outs,
        (rows_each(tokens, rows), gain, cosine, sine),
        pieces,
        places,
        grid=(seqs,),
        scratch=[pltpu.VMEM((rows, wide(KW)), F32)],
        us=2.2,
    )


def q_kernel(normed_ref, cos_ref, sin_ref, w_ref, q_ref, qs):
    qs[:, :QW] = nn(normed_ref[...], w_ref[...])
    rotate_into(q_ref, qs, QW, cos_ref[...], sin_ref[...], HD**-0.5)


def project_q(normed, seqs, cosine, sine, pieces, places):
    total = normed.shape[0]
    rows = total // seqs
    return with_weight(
        q_kernel,
        [rows_each(struct((total, QW), BF16), rows)],
        (rows_each(normed, rows), cosine, sine),
        pieces,
        places,
        grid=(seqs,),
        scratch=[pltpu.VMEM((rows, wide(QW)), F32)],
        us=2.2,
    )


def residual_kernel(tok_ref, mixed_ref, gain_ref, w_ref, hidden_ref, normed_ref):
    hidden = tok_ref[:, : hidden_ref.shape[1]].astype(F32) + nn(mixed_ref[...], w_ref[...])
    hidden_ref[...] = hidden
    normed_ref[...] = (hidden * inverse_mean(hidden) * gain_ref[...]).astype(BF16)


def residual(tokens, seq, mixed, gain, pieces, places):
    rows, width = mixed.shape[0], gain.shape[1]
    return with_weight(
        residual_kernel,
        [struct((rows, width), F32), struct((rows, width), BF16)],
        (rows_at(tokens, seq, rows), mixed, gain),
        pieces,
        places,
        us=1.8,
    )


def marks(scal_ref, pos, valid):
    segment = jnp.zeros(pos.shape, jnp.int32)
    for d in range(2):
        segment += (pos >= scal_ref[0, d]).astype(jnp.int32)
    number = jnp.zeros(pos.shape, jnp.int32)
    for j in range(2):
        start = scal_ref[0, 2 + j]
        number += jnp.where((pos >= start) & (pos < start + PIECE), j + 1, 0)
    return jnp.where(valid, segment, -1), number


def bias_of(scal_ref, start, across):
    q_shape, k_shape, q_dim, k_dim = (
        ((GRAIN, 1), (1, SPAN), 0, 1) if across else ((1, GRAIN), (SPAN, 1), 1, 0)
    )
    q_pos = start + lax.broadcasted_iota(jnp.int32, q_shape, q_dim)
    k_pos = start - MAXDOC + lax.broadcasted_iota(jnp.int32, k_shape, k_dim)
    q_seg, q_num = marks(scal_ref, q_pos, q_pos >= 0)
    k_seg, k_num = marks(scal_ref, k_pos, (k_pos >= 0) & (k_pos < LEN))
    q_num = jnp.where(q_num > 0, q_num, -1)
    permit = (q_seg == k_seg) & ((k_pos <= q_pos) | (q_num == k_num))
    return jnp.where(permit, 0.0, NEG).astype(F32)


def load_window(window, parts):
    row = 0
    for part in parts:
        window[row : row + part.shape[0], :] = part[...]
        row += part.shape[0]


def head_columns(j):
    return [slice(h * HD, (h + 1) * HD) for h in range(j * GROUP, (j + 1) * GROUP)]


def attend_kernel(scal_ref, q_ref, far_ref, near_ref, own_ref, next_ref, mixed_ref, lse_ref, window):
    sub = pl.program_id(0)

    @pl.when(sub == 0)
    def _():
        load_window(window, (far_ref, near_ref, own_ref, next_ref))

    bias = bias_of(scal_ref, scal_ref[0, 4] + sub * GRAIN, True)
    bias = jnp.concatenate([bias] * GROUP, axis=0)
    rows = pl.ds(pl.multiple_of(sub * GRAIN, GRAIN), SPAN)
    lse = jnp.zeros((GRAIN, 128), F32)
    lane = lax.broadcasted_iota(jnp.int32, (GRAIN, 128), 1)
    for j in range(KVH):
        key = window[rows, j * HD : (j + 1) * HD]
        value = window[rows, KW + j * HD : KW + (j + 1) * HD]
        query = jnp.concatenate([q_ref[:, c] for c in head_columns(j)], axis=0)
        scores = nt(query, key) + bias
        top = jnp.max(scores, axis=-1, keepdims=True)
        raised = jnp.exp(scores - top)
        total = jnp.sum(raised, axis=-1, keepdims=True)
        out = nn(raised.astype(BF16), value) / total
        logsum = top + jnp.log(total)
        for g, c in enumerate(head_columns(j)):
            at = slice(g * GRAIN, (g + 1) * GRAIN)
            mixed_ref[:, c] = out[at].astype(BF16)
            lse = jnp.where(lane == j * GROUP + g, logsum[at], lse)
    lse_ref[...] = lse


def window_parts(windows, seq, rows):
    far, near, own, ahead = windows
    parts = [rows_at(a, seq, rows) for a in (far, near, own)]
    return (*parts, rows_at(ahead, seq, GRAIN))


def sub_rows(array, seq, rows):
    first = seq * (rows // GRAIN)
    return array, pl.BlockSpec((GRAIN, array.shape[1]), lambda i: (first + i, 0))


def attend(scal, q, seq, rows, windows):
    return call(
        attend_kernel,
        [rows_each(struct((rows, w), t), GRAIN) for w, t in ((QW, BF16), (128, F32))],
        (scal, sub_rows(q, seq, rows), *window_parts(windows, seq, rows)),
        grid=(rows // GRAIN,),
        scratch=[pltpu.VMEM((MAXDOC + rows + GRAIN, 2 * KW), BF16)],
        us=6.8,
    )


def attend_back_kernel(
    earlier,
    scal_ref,
    q_ref,
    far_ref,
    near_ref,
    own_ref,
    next_ref,
    mixed_ref,
    lse_ref,
    grad_ref,
    cos_ref,
    sin_ref,
    *refs,
):
    dq_ref, dfar_ref, dnear_ref, down_ref, dnext_ref, window, sums, qs = refs[earlier:]
    sub = pl.program_id(0)

    @pl.when(sub == 0)
    def _():
        load_window(window, (far_ref, near_ref, own_ref, next_ref))
        sums[...] = jnp.zeros_like(sums)

    bias = bias_of(scal_ref, scal_ref[0, 4] + sub * GRAIN, False)
    bias = jnp.concatenate([bias] * GROUP, axis=1)
    rows = pl.ds(pl.multiple_of(sub * GRAIN, GRAIN), SPAN)
    lane = lax.broadcasted_iota(jnp.int32, (GRAIN, 128), 1)
    product = mixed_ref[...].astype(F32) * grad_ref[...].astype(F32)
    delta = jnp.zeros((GRAIN, 128), F32)
    for h in range(H):
        share = jnp.sum(product[:, h * HD : (h + 1) * HD], axis=-1, keepdims=True)
        delta = jnp.where(lane == h, share, delta)
    delta = delta.T
    lse = lse_ref[...].T

    def heads(array, j):
        return jnp.concatenate([array[h : h + 1] for h in range(j * GROUP, (j + 1) * GROUP)], axis=1)

    for j in range(KVH):
        k_cols = slice(j * HD, (j + 1) * HD)
        v_cols = slice(KW + j * HD, KW + (j + 1) * HD)
        key, value = window[rows, k_cols], window[rows, v_cols]
        query = jnp.concatenate([q_ref[:, c] for c in head_columns(j)], axis=0)
        grad = jnp.concatenate([grad_ref[:, c] for c in head_columns(j)], axis=0)
        probs = jnp.exp(nt(key, query) + bias - heads(lse, j))
        grad_scores = (probs * (nt(value, grad) - heads(delta, j))).astype(BF16)
        sums[rows, v_cols] += nn(probs.astype(BF16), grad)
        sums[rows, k_cols] += nn(grad_scores, query)
        dq = tn(key, grad_scores).T
        for g, c in enumerate(head_columns(j)):
            qs[:, c] = dq[g * GRAIN : (g + 1) * GRAIN, :]
    rotate_into(dq_ref, qs, QW, cos_ref[...], -sin_ref[...], HD**-0.5)

    @pl.when(sub == pl.num_programs(0) - 1)
    def _():
        row = 0
        for part in (dfar_ref, dnear_ref, down_ref):
            part[...] = sums[row : row + part.shape[0], :].astype(part.dtype)
            row += part.shape[0]
        done = dnext_ref.shape[0] - GRAIN
        if earlier:
            dnext_ref[:done, :] = refs[0][...]
        dnext_ref[done:, :] = sums[row:, :].astype(BF16)


def attend_back(scal, q, seq, rows, windows, mixed, lse, grad, cosine, sine, earlier):
    window = MAXDOC + rows + GRAIN
    each = lambda a: rows_each(a, GRAIN)
    shapes = ((rows, BF16), (rows, BF16), (rows, F32), ((seq + 1) * GRAIN, BF16))
    return call(
        functools.partial(attend_back_kernel, len(earlier)),
        [each(struct((rows, QW), BF16)), *(struct((r, 2 * KW), t) for r, t in shapes)],
        (
            scal,
            sub_rows(q, seq, rows),
            *window_parts(windows, seq, rows),
            *map(each, (mixed, lse, grad, cosine, sine)),
            *earlier,
        ),
        grid=(rows // GRAIN,),
        scratch=[
            pltpu.VMEM((window, 2 * KW), BF16),
            pltpu.VMEM((window, 2 * KW), F32),
            pltpu.VMEM((GRAIN, wide(QW)), F32),
        ],
        us=0.05 if earlier else 11.7,
    )


def ff_kernel(nrm_a, nrm_b, cot_a, cot_b, w_ref, inner_ref, gg_ref, gu_ref, sum_a, sum_b):
    first = pl.program_id(0) == 0
    (rows, units), width = inner_ref.shape, w_ref.shape[0]
    wg, wu, wd = (w_ref[:, k * units : (k + 1) * units] for k in range(3))
    normed = jnp.where(first, nrm_a[...], nrm_b[...])
    gate = nn(normed, wg)
    up = nn(normed, wu)
    grad = nn(jnp.where(first, cot_a[:, :width], cot_b[:, :width]), wd)
    sigma = jax.nn.sigmoid(gate)
    raised = gate * sigma
    inner = (raised * up).astype(BF16)
    grad_gate = (grad * up * (sigma + raised * (1.0 - sigma))).astype(BF16)
    grad_up = (grad * raised).astype(BF16)
    inner_ref[...] = inner
    gg_ref[...] = grad_gate
    gu_ref[...] = grad_up
    grad_normed = (nt(grad_gate, wg) + nt(grad_up, wu)).astype(BF16)
    out = nt(inner, wd).astype(BF16)

    @pl.when(first)
    def _():
        sum_a[:rows, :width] = grad_normed
        sum_a[rows:, :width] = out

    @pl.when(jnp.logical_not(first))
    def _():
        sum_b[:rows, :width] = grad_normed
        sum_b[rows:, :width] = out


def ff(normed_pair, cot_pair, weights, seq):
    rows, width = normed_pair[0].shape
    units = weights.shape[1] // 3
    unit = lambda: rows_each(struct((2 * rows, units), BF16), rows)
    result = call(
        ff_kernel,
        [unit(), unit(), unit()] + [struct((2 * rows, wide(width)), BF16)] * 2,
        (*normed_pair, *(rows_at(c, seq, rows) for c in cot_pair), weights),
        grid=(2,),
        us=7.2,
    )
    return result[:3], result[3:]


def outer_kernel(counts, split, place_ref, *refs):
    acc = refs[-1]
    column = 0
    for lefts, rights, gains in counts:
        left_refs, refs = refs[:lefts], refs[lefts:]
        right_refs, refs = refs[:rights], refs[rights:]
        gain_refs, refs = refs[:gains], refs[gains:]
        width = right_refs[0].shape[-1]
        at = slice(column, column + width)
        join = lambda some, w: jnp.concatenate([r[:, :w] for r in some], axis=0)
        if lefts % rights:
            groups = [(left_refs, right_refs)]
        else:
            per = lefts // rights
            groups = [(left_refs[i * per : (i + 1) * per], [r]) for i, r in enumerate(right_refs)]
        for i, (some_left, some_right) in enumerate(groups):
            product = tn(join(some_left, acc.shape[0]), join(some_right, width))
            if i == 0:
                acc[:, at] = product
            else:
                acc[:, at] += product
        column += width
        if gains:
            total = functools.reduce(jnp.add, [g[...] for g in gain_refs])
            across = jnp.broadcast_to(total, (128, total.shape[1])).T
            stop = wide(column)
            acc[:, column:stop] = across[:, : stop - column]
            column = stop
    outs = refs[:-1]
    if split is None:
        outs[0][...] = acc[...]
        return
    keep_ref, send_ref = outs
    half = keep_ref.shape[0] if split == "shard" else keep_ref.shape[0] // 2
    for s in range(acc.shape[0] // (2 * half)):
        rows = slice(s * half, (s + 1) * half)
        keep_ref[rows, :] = acc[pl.ds(pl.multiple_of(2 * s * half + place_ref[0], 16), half), :]
        other = pl.ds(pl.multiple_of((2 * s + 1) * half - place_ref[0], 16), half)
        send_ref[rows, :] = acc[other, :].astype(BF16)


def outer(products, width, place, split, us, limit=VMEM_LIMIT):
    array = lambda operand: operand[0] if isinstance(operand, tuple) else operand
    full = 0
    for _, rights, gains in products:
        full += array(rights[0]).shape[1]
        full = wide(full) if gains else full
    if split is None:
        outs = [struct((width, full), F32)]
    else:
        outs = [struct((width // 2, full), F32), struct((width // 2, full), BF16)]
    args = [a for product in products for group in product for a in group]
    return call(
        functools.partial(outer_kernel, [tuple(map(len, p)) for p in products], split),
        outs,
        (place, *args),
        scratch=[pltpu.VMEM((width, full), F32)],
        us=us,
        limit=limit,
    )


def output_kernel(hidden_ref, *refs):
    total = hidden_ref[...]
    for term in refs[:-1]:
        total += term[:, : total.shape[1]].astype(F32)
    refs[-1][...] = total.T.astype(BF16)


def output_of(hidden, terms):
    rows, width = hidden.shape
    return call(output_kernel, [struct((width, rows), BF16)], (hidden, *terms), us=1.4)[0]


def ff_back_kernel(
    hidden_ref, cot_ref, a_ref, b_ref, c_ref, gain_ref, wo_ref, gh_ref, gb_ref, gm_ref, gg_ref
):
    hidden, gain = hidden_ref[...], gain_ref[...]
    factor = inverse_mean(hidden)
    width = hidden.shape[1]
    grad = sum(ref[:, :width].astype(F32) for ref in (a_ref, b_ref, c_ref))
    weighted = grad * gain
    back = factor * weighted - hidden * factor**3 * jnp.mean(
        hidden * weighted, axis=-1, keepdims=True
    )
    grad_hidden = cot_ref[:, :width].astype(F32) + back
    branch = grad_hidden.astype(BF16)
    gh_ref[...] = grad_hidden
    gb_ref[...] = branch
    gm_ref[...] = nt(branch, wo_ref[...]).astype(BF16)
    gg_ref[...] = jnp.sum(grad * hidden * factor, axis=0, keepdims=True)


def ff_back(hidden, cotangent, seq, terms, gain, wo):
    rows, width = hidden.shape
    outs = [
        struct((rows, width), F32),
        struct((rows, width), BF16),
        struct((rows, QW), BF16),
        struct((1, width), F32),
    ]
    return call(
        ff_back_kernel,
        outs,
        (hidden, rows_at(cotangent, seq, rows), *terms, gain, wo),
        us=0.05,
    )


def input_kernel(
    tok_ref,
    gh_ref,
    gq_ref,
    own_ref,
    left_ref,
    right_ref,
    gain_ref,
    wq_ref,
    wkv_ref,
    cos_ref,
    sin_ref,
    ig_ref,
    gkv_ref,
    ks,
):
    ks[...] = own_ref[...] + right_ref[...].astype(F32)
    ks[:GRAIN, :] += left_ref[...].astype(F32)
    gkv_ref[:, KW:] = ks[:, KW:].astype(BF16)
    rotate_into(gkv_ref, ks, KW, cos_ref[...], -sin_ref[...], 1.0)
    grad = nt(gq_ref[...], wq_ref[...]) + nt(gkv_ref[...], wkv_ref[...])
    source, gain = tok_ref[:, : gh_ref.shape[1]].astype(F32), gain_ref[...]
    factor = inverse_mean(source)
    weighted = grad * gain
    back = factor * weighted - source * factor**3 * jnp.mean(
        source * weighted, axis=-1, keepdims=True
    )
    ig_ref[...] = (gh_ref[...] + back).T


def input_back(tokens, seq, args):
    rows, width = args[0].shape
    return call(
        input_kernel,
        [struct((width, rows), F32), struct((rows, 2 * KW), BF16)],
        (rows_at(tokens, seq, rows), *args),
        scratch=[pltpu.VMEM((rows, 2 * KW), F32)],
        us=0.05,
    )


def add_kernel(*refs):
    total = refs[0][...].astype(F32)
    for ref in refs[1:-1]:
        total += ref[...].astype(F32)
    refs[-1][...] = total.astype(refs[-1].dtype)


def add_up(terms, shape, dtype, us=0.7):
    return call(add_kernel, [struct(shape, dtype)], terms, us=us)[0]


def side_kernel(*refs):
    width = refs[0].shape[1]
    for i, ref in enumerate(refs[:-1]):
        refs[-1][:, i * width : (i + 1) * width] = ref[...]


def side_by_side(*arrays):
    rows, width = arrays[0].shape
    return call(side_kernel, [struct((rows, len(arrays) * width), BF16)], arrays, us=0.8)[0]


def widen_kernel(all_ref, *outs):
    units = outs[0].shape[1]
    for i, out in enumerate(outs):
        out[...] = all_ref[:, i * units : (i + 1) * units].astype(F32)


def widen(value):
    rows, columns = value.shape
    return call(widen_kernel, [struct((rows, columns // 3), F32)] * 3, (value,), us=2.0)


def beside_kernel(left_ref, keep_ref, got_ref, out_ref):
    columns = left_ref.shape[1]
    out_ref[:, :columns] = left_ref[...]
    out_ref[:, columns:] = (keep_ref[...] + got_ref[...].astype(F32)).astype(BF16)


def set_beside(left, keep, got):
    shape = (left.shape[0], left.shape[1] + keep.shape[1])
    return call(beside_kernel, [struct(shape, BF16)], (left, keep, got), us=1.5)[0]


def pair_kernel(*refs):
    out = refs[-1]
    rows = refs[0].shape[0]
    for s in range(len(refs) // 2):
        total = refs[2 * s][...].astype(F32) + refs[2 * s + 1][...].astype(F32)
        out[s * rows : (s + 1) * rows, :] = total.astype(BF16)


def split_kernel(at_ref, keep_ref, got_ref, kept_ref, sent_ref, total):
    total[...] = keep_ref[...].astype(F32) + got_ref[...].astype(F32)
    half = kept_ref.shape[0]
    kept_ref[...] = total[pl.ds(pl.multiple_of(at_ref[0] * half, 8), half), :]
    sent_ref[...] = total[pl.ds(pl.multiple_of((1 - at_ref[0]) * half, 8), half), :].astype(BF16)


def split_sum(at, keep, got):
    shape = (keep.shape[0] // 2, keep.shape[1])
    return call(
        split_kernel,
        [struct(shape, F32), struct(shape, BF16)],
        (at, keep, got),
        scratch=[pltpu.VMEM(keep.shape, F32)],
        us=0.05,
    )


def put_halves(both, at_ref, own_ref, got_ref):
    half = own_ref.shape[0]
    if half == both.shape[0]:
        both[...] = own_ref[...].astype(F32)
        return
    for place, ref in ((at_ref[0], own_ref), (1 - at_ref[0], got_ref)):
        both[pl.ds(pl.multiple_of(place * half, 8), half), :] = ref[...].astype(F32)


def join_kernel(at_ref, own_ref, got_ref, out_ref, both):
    put_halves(both, at_ref, own_ref, got_ref)
    out_ref[...] = both[...].astype(out_ref.dtype)


def join_rows(at, own, got):
    shape = (2 * own.shape[0], own.shape[1])
    return call(
        join_kernel,
        [struct(shape, BF16)],
        (at, own, got),
        scratch=[pltpu.VMEM(shape, F32)],
        us=0.9,
    )[0]


def as_row(column):
    return jnp.broadcast_to(column, (column.shape[0], 128)).T[:1]


def finish_pair_kernel(at_ref, own_ref, got_ref, w_ref, out_ref, gain_ref, query_ref, sum_ref, both):
    put_halves(both, at_ref, own_ref, got_ref)
    width = out_ref.shape[1]
    out_ref[...] = both[:, :width]
    gain_ref[...] = as_row(both[:, width : width + 1])
    query = both[:, both.shape[1] - QW :]
    query_ref[...] = query
    sum_ref[...] = as_row(jnp.sum(query * w_ref[...].astype(F32), axis=-1, keepdims=True))


def finish_pair(at, own, got, weight, width):
    rows = weight.shape[0]
    return call(
        finish_pair_kernel,
        [struct(s, F32) for s in ((rows, width), (1, rows), (rows, QW), (1, rows))],
        (at, own, got, weight),
        scratch=[pltpu.VMEM((rows, own.shape[1]), F32)],
        us=1.5,
    )


def finish_kv_kernel(at_ref, own_ref, got_ref, w_ref, sum_ref, gain_ref, k_ref, v_ref, grad_ref, both):
    put_halves(both, at_ref, own_ref, got_ref)
    k_ref[...] = both[:, :KW].T
    v_ref[...] = both[:, KW:].T
    rest = as_row(jnp.sum(both[...] * w_ref[...].astype(F32), axis=-1, keepdims=True))
    grad_ref[...] = (sum_ref[...] + rest) / gain_ref[...]


def finish_kv(at, own, got, weight, sums, gain):
    rows = weight.shape[0]
    return call(
        finish_kv_kernel,
        [struct(s, F32) for s in ((KW, rows), (KW, rows), (1, rows))],
        (at, own, got, weight, sums, gain),
        scratch=[pltpu.VMEM((rows, own.shape[1]), F32)],
        us=1.5,
    )


def program(mesh):
    shards, ctxs = mesh.shape["shard"], mesh.shape["ctx"]

    def swap(value, axis, bit):
        count = mesh.shape[axis]
        return lax.ppermute(value, axis, [(i, i ^ bit) for i in range(count)])

    def shift(value, by):
        pairs = [(i, i + by) for i in range(ctxs) if 0 <= i + by < ctxs]
        return lax.ppermute(value, "ctx", pairs)

    def place_of(index):
        return index.astype(jnp.int32)[None]

    def over_shard(terms):
        return lax.psum_scatter(terms[0], "shard", scatter_dimension=0, tiled=True)

    def reduce_units(terms, finish):
        if shards != 2:
            return finish(over_shard(terms), None)
        keep, send = terms
        got = swap(send, "shard", 1)
        yield got
        return finish(keep, got)

    def all_over_ctx(value):
        part = lax.psum_scatter(value, "ctx", scatter_dimension=0, tiled=True)
        return lax.all_gather(part, "ctx", axis=0, tiled=True)

    def reduce_attention(terms, finish):
        zero = jnp.zeros((1,), jnp.int32)
        if shards != 2:
            total = lax.psum(over_shard(terms), ("ctx", "tp"))
            return finish(zero, total, total)
        tp = lax.axis_index("tp")
        mine, core, row = map(place_of, (lax.axis_index("shard"), tp % 2, tp // 2))
        held, low = terms
        got = swap(low, "tp", 1)
        yield got
        held, low = split_sum(mine, held, got)
        got = swap(low, "shard", 1)
        yield got
        held, low = split_sum(row, held, got)
        got = swap(low, "tp", 2)
        yield got
        low = add_up((held, got), held.shape, BF16)
        bit = 1
        while bit < ctxs:
            got = swap(low, "ctx", bit)
            yield got
            low = add_up((low, got), low.shape, BF16)
            bit *= 2
        got = swap(low, "tp", 2)
        yield got
        low = join_rows(row, low, got)
        got = swap(low, "tp", 1)
        yield got
        return finish(core, low, got)

    def per_device(
        tokens,
        cotangent,
        piece_starts,
        doc_lengths,
        attn_gain,
        w_query,
        w_key,
        w_value,
        w_out,
        ff_gain,
        w_gate,
        w_up,
        w_down,
    ):
        Order.last, Order.awaited = None, ()
        seqs, rows, width = tokens.shape
        offset = (lax.axis_index("ctx") * rows).astype(jnp.int32)
        mine, tp = lax.axis_index("shard"), lax.axis_index("tp")
        core, row = tp % 2, tp // 2
        every = range(seqs)
        last = seqs - 1

        tokens, cotangent = prepare(tokens.transpose(0, 2, 1), cotangent.transpose(0, 2, 1))
        cosine, sine = rotary_tables(offset, rows)
        ends = jnp.cumsum(doc_lengths, axis=1)[:, :-1]
        scal = jnp.concatenate(
            [ends, piece_starts, jnp.broadcast_to(offset, (seqs, 1))], axis=1
        ).astype(jnp.int32)
        scals = [scal[s : s + 1] for s in every]

        w_kv = jnp.concatenate([w_key, w_value], axis=1)
        gains = jnp.stack([attn_gain, ff_gain])
        if shards == 2:
            full = w_query.shape[0]
            half = full // 2
            span = -(-half // 32) * 16
            other = (1 - mine) * full
            near_rows, far_rows = other + core * half, other + (1 - core) * half
            step, back = row * (half - span), (1 - row) * (half - span)
            kv_places = jnp.stack([mine * full, near_rows, far_rows]).astype(jnp.int32)
            places = [near_rows + step, near_rows + back, far_rows + step, far_rows + back]
            places = jnp.stack([mine * full, *places]).astype(jnp.int32)
            quarter = lambda w: lax.dynamic_slice_in_dim(w, core * half + step, span)

            got = swap(gains, "shard", 1)
            all_gains = jnp.where(
                mine == 0,
                jnp.concatenate([gains, got], axis=1),
                jnp.concatenate([got, gains], axis=1),
            )
            kv_part = swap(lax.dynamic_slice_in_dim(w_kv, core * half, half), "shard", 1)
            kv_beside = swap(in_turn(kv_part), "tp", 1)
            kv_pieces = [(w_kv, 0, full), (kv_part, 0, half), (kv_beside, 0, half)]
            two = jnp.concatenate([quarter(w_query), quarter(w_out)], axis=0)
            two_x = swap(after(two, kv_part), "shard", 1)
        else:
            gather = lambda w: lax.all_gather(w, "shard", axis=0, tiled=True)
            kv_places = places = jnp.zeros((1,), jnp.int32)
            all_gains = lax.all_gather(gains, "shard", axis=1, tiled=True)
            kv_pieces = [(gather(w_kv), 0, width)]
        gain_one, gain_two = all_gains[:1].astype(F32), all_gains[1:].astype(F32)

        (normed_one, kv, first), kv_pieces = project_kv(
            tokens, seqs, gain_one, cosine, sine, kv_pieces, kv_places
        )
        wkv = kv_pieces[0][0]
        near, ahead = shift(kv, 1), shift(first, -1)
        if shards == 2:
            arrive(two_x)
        ff_weights = lax.all_gather(side_by_side(w_gate, w_up, w_down), "shard", axis=0, tiled=True)
        if shards == 2:
            two_y, two_beside = swap(two_x, "tp", 2), swap(two_x, "tp", 1)
            arrive(two_beside)
        arrive(ahead)
        windows = (shift(in_turn(near), 1), near, kv, ahead)
        if shards == 2:
            two_y = in_turn(two_y)
            parts = (two_x, two_y, two_beside, swap(two_y, "tp", 1))
            q_pieces = [(w_query, 0, full), *((p, 0, span) for p in parts)]
            out_pieces = [(w_out, 0, full), *((p, span, span) for p in parts)]
        else:
            q_pieces, out_pieces = ([(gather(w), 0, width)] for w in (w_query, w_out))
            two_y = w_query
        cot_y = swap(after(cotangent, two_y), "tp", 2)
        (query,), q_pieces = project_q(normed_one, seqs, cosine, sine, q_pieces, places)
        wq = q_pieces[0][0]
        cot_core = swap(in_turn(cotangent), "tp", 1)

        mixed, lse, hidden, normed_rows = [], [], [], []
        for s in every:
            if s == 1:
                cot_y = in_turn(cot_y)
                cot_diagonal = swap(cot_y, "tp", 1)
            m, l = attend(scals[s], query, s, rows, windows)
            if s == 0:
                arrive(cot_core)
            else:
                arrive(normed_rows[-1][1])
            if s == 1:
                arrive(cot_diagonal)
            (h, own), out_pieces = residual(tokens, s, m, gain_two, out_pieces, places)
            normed_rows.append((own, swap(own, "tp", 1), swap(own, "tp", 2)))
            mixed.append(m)
            lse.append(l)
            hidden.append(h)
        wo = out_pieces[0][0]
        if seqs == 1:
            cot_diagonal = swap(cot_y, "tp", 1)
        cots = (cotangent, cot_core, cot_y, cot_diagonal)

        row_blocks, units, near_sums, far_sums = [], [], [], []
        grad_at = lambda a: rows_at(a, 0, rows)
        out_at = lambda a: rows_at(a, 1, rows)

        def cross_grad(s):
            partial = add_up([grad_at(a) for a in far_sums[s]], (rows, wide(width)), BF16)
            return (*map(grad_at, near_sums[s]), swap(partial, "tp", 2))

        grad_terms = []
        for s in every:
            own, beside, facing = normed_rows[s]
            diagonal = swap(in_turn(facing), "tp", 1)
            if s > 0:
                arrive(near_sums[s - 1][1])
            unit, (a, b) = ff((own, beside), cots[:2], ff_weights, s)
            near_sums.append((a, swap(b, "tp", 1)))
            units.append(unit)
            if s > 0:
                grad_terms.append(cross_grad(s - 1))
            arrive(*(n[1] for n in normed_rows[s + 1 : s + 2]))
            unit, (a, b) = ff((facing, diagonal), cots[2:], ff_weights, s)
            far_sums.append((a, swap(b, "tp", 1)))
            units.append(unit)
            row_blocks += [own, beside, facing, diagonal]

        by_shard, by_core = ("shard", "core") if shards == 2 else (None, None)
        shard_place, core_place = place_of(mine * (width // 2)), place_of(core * (width // 4))
        cot_lefts = [rows_at(c, s, rows) for s in every for c in cots]

        def unit_product(lefts, k):
            return lefts, [u[k] for u in units], ()

        arrive(near_sums[last][1])
        def down_sum(keep, got):
            if got is None:
                return keep.astype(BF16)
            return add_up((keep, got), keep.shape, BF16, 0.05)

        def units_sum(keep, got):
            left = down.finish()
            if got is None:
                return jnp.concatenate([left, keep.astype(BF16)], axis=1)
            return set_beside(left, keep, got)

        down_grad = outer([unit_product(cot_lefts, 0)], width, shard_place, by_shard, 5.0)
        down = Chain(reduce_units(down_grad, down_sum))
        grad_terms.append(cross_grad(last))
        both = [unit_product(row_blocks, 1), unit_product(row_blocks, 2)]
        arrive(*(t[2] for t in grad_terms[:-1]))
        gate_up_grad = outer(both, width, shard_place, by_shard, 10.0, 2 * VMEM_LIMIT)
        gate_up = Chain(reduce_units(gate_up_grad, units_sum))
        out_terms = [out_at(a) for s in every for a in far_sums[s]]
        out_partial = call(
            pair_kernel, [struct((seqs * rows, wide(width)), BF16)], out_terms, us=0.05
        )[0]
        outs_got = swap(after(out_partial, grad_terms[last][2]), "tp", 2)

        branch, gain_two_grad, grad_hidden = [], [], []
        backs, input_grads, gkv = [], [], []
        ahead_grads = ()

        def mixed_back(s, ahead_grads):
            gh, gb, gm, gg = ff_back(hidden[s], cotangent, s, grad_terms[s], gain_two, wo)
            grad_hidden.append(gh)
            branch.append(gb)
            gain_two_grad.append(gg)
            if s == 0:
                down.step()
            dq, dfar, dnear, own, dnext = attend_back(
                scals[s], query, s, rows, windows, mixed[s], lse[s], gm, cosine, sine, ahead_grads
            )
            backs.append((dq, dnear, own, shift(dfar, -1)))
            return (dnext,)

        def pass_on(s):
            dq, dnear, own, passed = backs[s]
            backs[s] = dq, own, shift(add_up((dnear, passed), dnear.shape, BF16, 0.05), -1)

        def rows_back(s):
            dq, own, right = backs[s]
            args = (grad_hidden[s], dq, own, rows_at(left, s, GRAIN), right)
            args += (gain_one, wq, wkv, cosine, sine)
            input_grad, g = input_back(tokens, s, args)
            input_grads.append(input_grad)
            gkv.append(g)

        for s in every:
            ahead_grads = mixed_back(s, ahead_grads)
        left = shift(ahead_grads[0], 1)
        for s in every[:-1]:
            pass_on(s)
        arrive(outs_got)
        gate_up.step()
        unit_sums = all_over_ctx(gate_up.finish())
        pass_on(last)
        grads = [b[0] for b in backs]
        pair = Chain(
            reduce_attention(
                outer(
                    [(mixed, branch, gain_two_grad), ([normed_one], grads, ())],
                    width,
                    core_place,
                    by_core,
                    2.7,
                    2 * VMEM_LIMIT,
                ),
                lambda at, own, got: finish_pair(at, own, got, w_query, width),
            )
        )
        outputs = []
        for s in every:
            near_terms = [out_at(a) for a in near_sums[s]]
            outputs.append(output_of(hidden[s], (*near_terms, rows_at(outs_got, s, rows))))
        pair.step()
        for s in every:
            rows_back(s)
        finish_last = lambda at, own, got: (at, own, got)
        keys = Chain(
            reduce_attention(
                outer([([normed_one], gkv, ())], width, core_place, by_core, 0.05), finish_last
            )
        )
        for chain in (keys, pair, keys, pair, keys, pair, keys, pair, keys):
            chain.step()
        sum_down, sum_gate, sum_up = widen(unit_sums)
        for chain in (pair, keys):
            chain.step()
        sum_out, sum_gain_two, sum_query, products = pair.finish()
        keys_done = keys.finish()
        sum_key, sum_value, sum_gain_one = finish_kv(
            *keys_done, w_kv, products, gains[:1].astype(F32)
        )
        join = lambda blocks: jnp.stack(blocks).transpose(0, 2, 1)
        return (
            join(outputs),
            join(input_grads),
            sum_gain_one[0],
            sum_query,
            sum_key.T,
            sum_value.T,
            sum_out,
            sum_gain_two[0],
            sum_gate,
            sum_up,
            sum_down,
        )

    return per_device


def solution(mesh):
    rows = P(("shard", "tp"), "ctx", None)
    seq = P(("shard", "tp"), None)
    gain, weight, ff_weight = P("shard"), P("shard", None), P("shard", "tp")
    weights = (gain, weight, weight, weight, weight, gain, ff_weight, ff_weight, ff_weight)
    return jax.shard_map(
        program(mesh),
        mesh=mesh,
        in_specs=(rows, rows, seq, seq, *weights),
        out_specs=(rows, rows, *weights),
        check_vma=False,
    )
```
